32 devices in a mesh: seq: 8 (over z, y), fsdp: 4 (over x, core).
Axes of the slice: x: 2, y: 2, z: 4, core: 2. Of those that a mesh axis runs over, the one named last changes fastest.
Arguments:
- layer_in: bfloat16 [4, 1024, 1536], P('fsdp', 'seq'), may hold values from -6 to 6
- cotangent: bfloat16 [4, 1024, 1536], P('fsdp', 'seq'), may hold values from -6 to 6
- doc_starts: int32 [4, 4], P('fsdp'), may hold values from 0 to 1023, as said below
- routes: int32 [4, 1024, 8], P('fsdp', 'seq'), may hold values from 0 to 23, all different within a row; in each aligned block of 128 rows (0 to 127, 128 to 255, ..., all dimensions but the last counted through in order) at most 57 rows name the same one
- attn_gain: bfloat16 [2, 1536], P(None, ('seq', 'fsdp')), may hold values from 0.5 to 1.5
- ffn_gain: bfloat16 [2, 1536], P(None, ('seq', 'fsdp')), may hold values from 0.5 to 1.5
- query_weight: bfloat16 [2, 1536, 1536], P(None, ('seq', 'fsdp')), may hold values from -0.15625 to 0.15625
- key_matrix: bfloat16 [2, 1536, 512], P(None, ('seq', 'fsdp')), may hold values from -0.15625 to 0.15625
- value_matrix: bfloat16 [2, 1536, 512], P(None, ('seq', 'fsdp')), may hold values from -0.15625 to 0.15625
- out_weight: bfloat16 [2, 1536, 1536], P(None, ('seq', 'fsdp')), may hold values from -0.875 to 0.875
- router_weight: bfloat16 [2, 1536, 24], P(None, ('seq', 'fsdp')), may hold values from -0.078125 to 0.078125
- gate_weight: bfloat16 [2, 24, 1536, 512], P(None, 'seq', 'fsdp'), may hold values from -0.15625 to 0.15625
- up_weight: bfloat16 [2, 24, 1536, 512], P(None, 'seq', 'fsdp'), may hold values from -0.15625 to 0.15625
- down_weight: bfloat16 [2, 24, 512, 1536], P(None, 'seq', None, 'fsdp'), may hold values from -1 to 1
Outputs:
- layer_out: bfloat16 [4, 1024, 1536], P('fsdp', 'seq')
- input_grad: float32 [4, 1024, 1536], P('fsdp', 'seq')
- attn_gain_grad: float32 [2, 1536], P(None, ('seq', 'fsdp'))
- ffn_gain_grad: float32 [2, 1536], P(None, ('seq', 'fsdp'))
- query_grad: float32 [2, 1536, 1536], P(None, ('seq', 'fsdp'))
- key_grad: float32 [2, 1536, 512], P(None, ('seq', 'fsdp'))
- value_grad: float32 [2, 1536, 512], P(None, ('seq', 'fsdp'))
- out_grad: float32 [2, 1536, 1536], P(None, ('seq', 'fsdp'))
- router_grad: float32 [2, 1536, 24], P(None, ('seq', 'fsdp'))
- gate_grad: float32 [2, 24, 1536, 512], P(None, 'seq', 'fsdp')
- up_grad: float32 [2, 24, 1536, 512], P(None, 'seq', 'fsdp')
- down_grad: float32 [2, 24, 512, 1536], P(None, 'seq', None, 'fsdp')
The draws below stay inside these ranges and needn't reach their ends.
Inputs may be any that keep to these rules, and one draw needn't show every extreme that they name: `doc_starts`: in each stream the 4 starts rise strictly and the first is 0; a document runs from its start to the next start, the last one to the end of the stream, and may be a single position. `routes`: the 8 experts of a position are distinct; among the 128 positions of a stream that one device holds (aligned blocks) no expert is named more than 57 times.
All inputs are finite; a program needn't handle non-finite values.
Results may differ from the reference program's by a relative error of at most 0.025.
Values may be sent and summed in bfloat16 or wider, within the bound.
A program may use at most 384 MiB of HBM per device.

```python
import math
import jax
import jax.numpy as jnp
import numpy as np
from jax import lax

MODEL_WIDTH = 1536
QUERY_HEADS = 24
KEY_VALUE_HEADS = 8
HEAD_SIZE = 64
FF = 512
TOP = 8
LAYER_TOTAL = 2
DOCS = 4
STREAM_LENGTH = 1024
TOK_DEV = 128
STREAMS = 4
E = 24
CAP = 57
N_SEQ = 8


def draw_doc_starts(key, part):
    stream_keys = jax.random.split(key, STREAMS)

    def one_stream(stream_key, stream_id):
        cut_points = jax.random.permutation(stream_key, STREAM_LENGTH - 2)[:DOCS - 1] + 1
        cut_points = jnp.sort(cut_points).astype(jnp.int32)
        last_value = jnp.where(stream_id == 0, jnp.int32(STREAM_LENGTH - 1), cut_points[DOCS - 2])
        cut_points = cut_points.at[DOCS - 2].set(last_value)
        return jnp.concatenate([jnp.zeros((1,), jnp.int32), cut_points])
    return jax.vmap(one_stream)(stream_keys, jnp.arange(STREAMS, dtype=jnp.int32))


def block_levels(key, dims, shards, low, top_value):
    loudness, own = 1.0, jax.random.fold_in(key, 6)
    for dim, parts in shards:
        steps = jnp.exp(jax.random.uniform(jax.random.fold_in(own, dim), (parts,), jnp.float32, low / len(shards), top_value / len(shards)))
        loudness = loudness * jnp.repeat(steps, dims[dim] // parts).reshape([-1 if axis == dim else 1 for axis in range(len(dims))])
    return loudness


def routed_block(key, own, number, rows, amount, top, most, lean):
    ranking = jax.random.permutation(key, amount)
    crowded, common = load_shares(amount, rows * top, most, lean, True), load_shares(amount, rows * top, most, lean, False)
    places = jnp.arange(amount)

    def named(lengths, turn):
        used = int((lengths > 0).sum())
        fixed = max(1, used // 4)
        shifted = fixed + (places - fixed + turn * (used - fixed)) % max(1, amount - fixed)
        return jnp.zeros((amount,), jnp.int32).at[ranking[jnp.where(places < fixed, places, shifted)]].set(jnp.asarray(lengths, jnp.int32))

    lengths = jnp.where(number % 4 == 0, named(crowded, number // 4), named(common, number - number // 4 - 1))
    mixed = jax.random.permutation(jax.random.fold_in(own, 3), amount)
    giver, sink = mixed[0:amount // 2 * 2:2], mixed[1:amount // 2 * 2:2]
    slack = jnp.minimum(lengths[giver] - 1, most - lengths[sink]) // 2
    slack = jnp.where((giver == ranking[0]) | (sink == ranking[0]) | (lengths[sink] == 0), 0, jnp.maximum(slack, 0))
    shifted = jax.random.randint(jax.random.fold_in(own, 4), (amount // 2,), 0, 1 << 20) % (slack + 1)
    lengths = lengths.at[giver].add(-shifted).at[sink].add(shifted)
    items = jnp.searchsorted(jnp.cumsum(lengths), jnp.arange(rows * top), side="right").astype(jnp.int32)
    table = items.reshape(top, rows).T
    table = table[jax.random.permutation(jax.random.fold_in(own, 1), rows)]
    turn = jax.random.randint(jax.random.fold_in(own, 2), (rows, 1), 0, top)
    return jnp.take_along_axis(table, (jnp.arange(top)[None, :] + turn) % top, axis=1)


def load_shares(amount, total, reach, slope, full):
    portions = [(1 << 20) // math.isqrt(grade ** slope) + 1 for grade in range(1, amount + 1)]
    largest = reach if full else min(reach, max(-(-total // amount), total * portions[0] // sum(portions)))
    least = 1 if total - largest >= amount - 1 else 0
    holding, rest = [largest] + [least] * (amount - 1), total - largest - least * (amount - 1)
    while rest > 0:
        free = [i for i in range(1, amount) if holding[i] < largest] or [i for i in range(1, amount) if holding[i] < reach]
        pool, remaining = sum([portions[i] for i in free]), rest
        for i in free:
            addition = min(reach - holding[i], max(1, remaining * portions[i] // pool), rest)
            holding[i] = holding[i] + addition
            rest = rest - addition
    return np.array(holding)


def normal_values(rng, extent, deviation, limit, pieces=(), kind=jnp.bfloat16):
    values = deviation * jax.random.normal(rng, extent, jnp.float32)
    if pieces:
        values = values * block_levels(rng, extent, pieces, -0.22, 0.18)
    return jnp.clip(values, -limit, limit).astype(kind)


def setup_inputs(seed: int = 0) -> dict:
    key_list = jax.random.split(jax.random.key(seed), 15)
    layer_in = normal_values(key_list[0], (STREAMS, STREAM_LENGTH, MODEL_WIDTH), 1.0, 6.0, ((0, 4), (1, 8)))
    cotangent = normal_values(key_list[1], (STREAMS, STREAM_LENGTH, MODEL_WIDTH), 1.0, 6.0, ((0, 4), (1, 8)))
    doc_starts = draw_doc_starts(jax.random.fold_in(key_list[14], 71), 0)
    routes_keys = jax.random.split(jax.random.fold_in(key_list[3], 1), STREAMS * STREAM_LENGTH // TOK_DEV)
    routes_turns = jax.random.permutation(jax.random.fold_in(key_list[3], 3), STREAMS * STREAM_LENGTH // TOK_DEV)
    routes = jax.vmap(lambda own, number: routed_block(jax.random.fold_in(key_list[3], 2), own, number, TOK_DEV, E, TOP, CAP, 1))(routes_keys, routes_turns).reshape((STREAMS, STREAM_LENGTH, TOP))
    attn_gain = jnp.clip(1.0 + 0.1 * jax.random.normal(key_list[4], (LAYER_TOTAL, MODEL_WIDTH), jnp.float32), 0.5, 1.5).astype(jnp.bfloat16)
    ffn_gain = jnp.clip(1.0 + 0.1 * jax.random.normal(key_list[5], (LAYER_TOTAL, MODEL_WIDTH), jnp.float32), 0.5, 1.5).astype(jnp.bfloat16)
    query_weight = normal_values(key_list[6], (LAYER_TOTAL, MODEL_WIDTH, QUERY_HEADS * HEAD_SIZE), MODEL_WIDTH ** -0.5, 0.15625, ((1, 32),))
    key_matrix = normal_values(key_list[7], (LAYER_TOTAL, MODEL_WIDTH, KEY_VALUE_HEADS * HEAD_SIZE), MODEL_WIDTH ** -0.5, 0.15625, ((1, 32),))
    value_matrix = normal_values(key_list[8], (LAYER_TOTAL, MODEL_WIDTH, KEY_VALUE_HEADS * HEAD_SIZE), MODEL_WIDTH ** -0.5, 0.15625, ((1, 32),))
    out_weight = normal_values(key_list[9], (LAYER_TOTAL, QUERY_HEADS * HEAD_SIZE, MODEL_WIDTH), (QUERY_HEADS * HEAD_SIZE // 32) ** -0.5, 0.875, ((1, 32),))
    router_weight = normal_values(key_list[10], (LAYER_TOTAL, MODEL_WIDTH, E), (4 * MODEL_WIDTH) ** -0.5, 0.078125, ((1, 32),))
    gate_weight = normal_values(key_list[11], (LAYER_TOTAL, E, MODEL_WIDTH, FF), MODEL_WIDTH ** -0.5, 0.15625, ((1, 8), (2, 4)))
    up_weight = normal_values(key_list[12], (LAYER_TOTAL, E, MODEL_WIDTH, FF), MODEL_WIDTH ** -0.5, 0.15625, ((1, 8), (2, 4)))
    down_weight = normal_values(key_list[13], (LAYER_TOTAL, E, FF, MODEL_WIDTH), (FF // 16) ** -0.5, 1.0, ((1, 8), (3, 4)))
    return {"layer_in": layer_in, "cotangent": cotangent, "doc_starts": doc_starts, "routes": routes, "attn_gain": attn_gain, "ffn_gain": ffn_gain, "query_weight": query_weight, "key_matrix": key_matrix, "value_matrix": value_matrix, "out_weight": out_weight, "router_weight": router_weight, "gate_weight": gate_weight, "up_weight": up_weight, "down_weight": down_weight}


@jax.custom_vjp
def low(v):
    return lax.optimization_barrier(v.astype(jnp.bfloat16)).astype(jnp.float32)

@jax.custom_vjp
def low_back(v):
    return v

def low_keep(v):
    return (low(v), None)

def low_pass(kept, grad):
    return (grad,)

def back_keep(v):
    return (v, None)

def back_low(kept, grad):
    return (low(grad),)
low.defvjp(low_keep, low_pass)
low_back.defvjp(back_keep, back_low)
EPSILON = 1e-05
HIGHEST = lax.Precision.HIGHEST

def rms_normed(stream, gain_row):
    factor = lax.rsqrt(lax.optimization_barrier(jnp.mean(stream * stream, axis=-1, keepdims=True)) + EPSILON)
    return stream * factor * gain_row

def rotation_apply(source, token_positions, head_count, head_size):
    half_size = head_size // 2
    inverse = 10000.0 ** (-2.0 * jnp.arange(half_size, dtype=jnp.float32) / head_size)
    angle_table = token_positions.astype(jnp.float32)[:, None] * inverse[None, :]
    cosine = jnp.cos(angle_table)[:, None, :]
    sine_part = jnp.sin(angle_table)[:, None, :]
    shaped = source.reshape(source.shape[:-1] + (head_count, head_size))
    first_half = shaped[..., :half_size]
    second = shaped[..., half_size:]
    turned = jnp.concatenate([first_half * cosine - second * sine_part, second * cosine + first_half * sine_part], axis=-1)
    return turned.reshape(source.shape)

def attend_stream(operands):
    query_rows, key_token_rows, value_token_rows, starts = operands
    all_positions = jnp.arange(STREAM_LENGTH, dtype=jnp.int32)
    doc_ids = lax.optimization_barrier(jnp.sum((starts[None, :] <= all_positions[:, None]).astype(jnp.int32), axis=1))
    allowed = (doc_ids[:, None] == doc_ids[None, :]) & (all_positions[None, :] <= all_positions[:, None])
    query_group_width = QUERY_HEADS // KEY_VALUE_HEADS
    query_grouped = query_rows.reshape(STREAM_LENGTH, KEY_VALUE_HEADS, query_group_width, HEAD_SIZE)
    key_head_rows = key_token_rows.reshape(STREAM_LENGTH, KEY_VALUE_HEADS, HEAD_SIZE)
    value_head_rows = value_token_rows.reshape(STREAM_LENGTH, KEY_VALUE_HEADS, HEAD_SIZE)
    scores = jnp.einsum('qhgd,khd->hgqk', query_grouped, key_head_rows, precision=HIGHEST) * (1.0 / math.sqrt(HEAD_SIZE))
    scores = low_back(scores)
    scores = jnp.where(allowed[None, None], scores, -1e+30)
    highest = lax.optimization_barrier(jnp.max(scores, axis=-1, keepdims=True))
    weights = jnp.exp(scores - highest)
    probs = low(weights / lax.optimization_barrier(jnp.sum(weights, axis=-1, keepdims=True)))
    mixed_rows = jnp.einsum('hgqk,khd->qhgd', probs, value_head_rows, precision=HIGHEST)
    return mixed_rows.reshape(STREAM_LENGTH, QUERY_HEADS * HEAD_SIZE)

def expert_block(operands, gate_weight, up_weight, down_weight):
    row_values, chosen, gate_probs = operands
    flat_routes = chosen.reshape(-1)
    onehot = (flat_routes[:, None] == jnp.arange(E, dtype=jnp.int32)[None, :]).astype(jnp.int32)
    slot_ids = lax.optimization_barrier(jnp.sum((jnp.cumsum(onehot, axis=0) - onehot) * onehot, axis=1))
    places = flat_routes * CAP + slot_ids
    owners = jnp.arange(TOK_DEV * TOP, dtype=jnp.int32) // TOP
    sources = jnp.full((E * CAP,), TOK_DEV, jnp.int32).at[places].set(owners)
    padded = jnp.concatenate([row_values, jnp.zeros((1, MODEL_WIDTH), row_values.dtype)], axis=0)
    buffer = low_back(padded[sources]).reshape(E, CAP, MODEL_WIDTH)
    gate_part = low_back(jnp.einsum('ecd,edf->ecf', buffer, gate_weight, precision=HIGHEST))
    up_part = low_back(jnp.einsum('ecd,edf->ecf', buffer, up_weight, precision=HIGHEST))
    hidden = low(gate_part * jax.nn.sigmoid(gate_part) * up_part)
    produced = low_back(low(jnp.einsum('ecf,efd->ecd', hidden, down_weight, precision=HIGHEST)))
    picked = produced.reshape(E * CAP, MODEL_WIDTH)[places].reshape(TOK_DEV, TOP, MODEL_WIDTH)
    return jnp.einsum('tk,tkd->td', gate_probs, picked, precision=HIGHEST)

def layer_forward(stream, layer_id, params, doc_starts, routes):
    attn_gain, ffn_gain, query_weight, key_matrix, value_matrix, out_weight, router_weight, gate_weight, up_weight, down_weight = params
    normed = low(rms_normed(stream, attn_gain[layer_id]))
    token_positions = jnp.arange(STREAM_LENGTH, dtype=jnp.int32)
    query_raw = low_back(jnp.matmul(normed, query_weight[layer_id], precision=HIGHEST))
    key_unrotated = low_back(jnp.matmul(normed, key_matrix[layer_id], precision=HIGHEST))
    query_rows = low_back(low(rotation_apply(query_raw, token_positions, QUERY_HEADS, HEAD_SIZE)))
    key_token_rows = low_back(low(rotation_apply(key_unrotated, token_positions, KEY_VALUE_HEADS, HEAD_SIZE)))
    value_token_rows = low_back(low(jnp.matmul(normed, value_matrix[layer_id], precision=HIGHEST)))
    mixed_rows = lax.map(jax.checkpoint(attend_stream), (query_rows, key_token_rows, value_token_rows, doc_starts))
    mixed_rows = low_back(low(mixed_rows))
    branch = low_back(jnp.matmul(mixed_rows, out_weight[layer_id], precision=HIGHEST))
    middle = stream + branch
    normed_two = low(rms_normed(middle, ffn_gain[layer_id]))
    logits = jnp.matmul(normed_two, router_weight[layer_id], precision=HIGHEST)
    selected = jnp.take_along_axis(logits, routes, axis=-1)
    highest = lax.optimization_barrier(jnp.max(selected, axis=-1, keepdims=True))
    weights = jnp.exp(selected - highest)
    gate_probs = weights / lax.optimization_barrier(jnp.sum(weights, axis=-1, keepdims=True))
    block_count = STREAMS * N_SEQ
    gate_layer = gate_weight[layer_id]
    up_layer = up_weight[layer_id]
    down_layer = down_weight[layer_id]

    def run_block(operands):
        return expert_block(operands, gate_layer, up_layer, down_layer)
    expert_sum = lax.map(jax.checkpoint(run_block), (normed_two.reshape(block_count, TOK_DEV, MODEL_WIDTH), routes.reshape(block_count, TOK_DEV, TOP), gate_probs.reshape(block_count, TOK_DEV, TOP)))
    return middle + expert_sum.reshape(STREAMS, STREAM_LENGTH, MODEL_WIDTH)

def reference(layer_in, cotangent, doc_starts, routes, attn_gain, ffn_gain, query_weight, key_matrix, value_matrix, out_weight, router_weight, gate_weight, up_weight, down_weight):
    weights = tuple((array.astype(jnp.float32) for array in (attn_gain, ffn_gain, query_weight, key_matrix, value_matrix, out_weight, router_weight, gate_weight, up_weight, down_weight)))

    def forward(stream, *params):
        for layer_id in range(LAYER_TOTAL):
            stream = layer_forward(stream, layer_id, params, doc_starts, routes)
        return stream
    result, pullback = jax.vjp(forward, layer_in.astype(jnp.float32), *weights)
    gradients = pullback(cotangent.astype(jnp.float32))
    return (result.astype(jnp.bfloat16), gradients[0], gradients[1], gradients[2], gradients[3], gradients[4], gradients[5], gradients[6], gradients[7], gradients[8], gradients[9], gradients[10])
```

```python
import functools, math
import jax, jax.numpy as jnp
from jax import lax
from jax.experimental import pallas as pl
from jax.experimental.pallas import tpu as pltpu
from jax.sharding import Mesh, PartitionSpec as P
MESH = pl.DeviceIdType.MESH
AX=("za","yb","grp","xh","co")

class Ring8:
    def __init__(self, na):
        self.n=2*na; self.na=na
        za=lax.axis_index("za"); yb=lax.axis_index("yb")
        self.rho = za + yb*(2*na-1-2*za)
    def pos(self, r):
        r = lax.rem(r+2*self.n, self.n)
        yb = r//self.na
        za = r + yb*(2*self.na-1-2*r)
        return za, yb
    def dev(self, r):
        za,yb=self.pos(r); return {"za":za,"yb":yb}
    def slot(self, r):
        za,yb=self.pos(r); return za*2+yb

class Ring4:
    def __init__(self):
        self.n=4
        x=lax.axis_index("xh"); b=lax.axis_index("yb"); self.c=lax.axis_index("co")
        self.rho = 2*x + (x+b-2*x*b)
    def pos(self, r):
        r = lax.rem(r+2*self.n, self.n)
        x = r//2; m=lax.rem(r,2)
        return x, m+x-2*x*m
    def dev(self, r):
        x,b=self.pos(r); return {"xh":x,"yb":b}
    def slot(self, r, sib=False):
        x,b=self.pos(r); c = (1-self.c) if sib else self.c
        return (x*2+c)*2+b
    def sib_dev(self):
        return {"co":1-self.c}

def barrier(devs):
    sem = pltpu.get_barrier_semaphore()
    for d in devs:
        pl.semaphore_signal(sem, inc=1, device_id=d, device_id_type=MESH)
    pl.semaphore_wait(sem, len(devs))

def rcopy(src, dst, ss, rs, dev):
    return pltpu.make_async_remote_copy(src_ref=src, dst_ref=dst, send_sem=ss, recv_sem=rs, device_id=dev, device_id_type=MESH)

def ag_ring(ring, K, own, out, send, recv, sib=None):
    n=ring.n; S=n//2; T=own.shape[0]; rows=T//K; rho=ring.rho
    def chunks(d,s): return range(K) if s<S else (range(K//2) if d==0 else range(K//2,K))
    def mk(d,s,c):
        sg=1-2*d
        slot=ring.slot(rho-(s-1)*sg)
        sl=pl.ds(c*rows,rows)
        src = own.at[sl] if s==1 else out.at[slot,sl]
        return rcopy(src, out.at[slot,sl], send.at[d,s-1,c], recv.at[d,s-1,c], ring.dev(rho+sg))
    def rd(d,s,c):
        sg=1-2*d
        slot=ring.slot(rho-s*sg); sl=pl.ds(c*rows,rows)
        return rcopy(out.at[slot,sl], out.at[slot,sl], send.at[d,s-1,c], recv.at[d,s-1,c], ring.dev(rho-sg))
    started=[]
    def sibcopy(slot, slot_src, c, idx, src):
        ss,rs=sib
        cp=rcopy(src, out.at[slot,pl.ds(c*rows,rows)], ss.at[idx,c], rs.at[idx,c], ring.sib_dev())
        cp.start(); started.append(cp)
    def arrived(d,s,c):
        rd(d,s,c).wait_recv()
        if sib is not None:
            sg=1-2*d
            slot=ring.slot(rho-s*sg)
            idx = s*sg % n
            sibcopy(slot, None, c, idx, out.at[slot,pl.ds(c*rows,rows)])
    sends=[]
    for s in range(1,S+1):
        for c in range(K):
            for d in (0,1):
                if c in chunks(d,s):
                    if s>1: arrived(d,s-1,c)
                    cp=mk(d,s,c); cp.start(); sends.append(cp)
        if s==1 and sib is not None:
            for c in range(K): sibcopy(ring.slot(rho), None, c, 0, own.at[pl.ds(c*rows,rows)])
    for s in (S-1,S):
        for c in range(K):
            for d in (0,1):
                if s==S and c in chunks(d,S): arrived(d,S,c)
                if s==S-1 and S>1 and c not in chunks(d,S): arrived(d,S-1,c)
    if sib is not None:
        ss,rs=sib
        for idx in range(n):
            for c in range(K):
                slot=ring.slot(rho-idx, True); sl=pl.ds(c*rows,rows)
                rcopy(out.at[slot,sl],out.at[slot,sl],ss.at[idx,c],rs.at[idx,c],ring.sib_dev()).wait_recv()
    for cp in sends+started: cp.wait_send()

def rs_ring(ring, K, part, buf, send, recv, slotf):
    n=ring.n; S=n//2; T=buf.shape[2]; rows=T//K; rho=ring.rho
    def chunks(d,s): return range(K) if s>1 else (range(K//2) if d==0 else range(K//2,K))
    sends=[]
    def rd(d,s,c):
        sl=pl.ds(c*rows,rows)
        return rcopy(buf.at[d,s-1,sl],buf.at[d,s-1,sl],send.at[d,s-1,c],recv.at[d,s-1,c],ring.dev(rho-(1-2*d)))
    for s in range(1,S+1):
        order=list(range(K))
        if s==2:
            pass
        for c in order:
            for d in (0,1):
                if c not in chunks(d,s): continue
                sg=1-2*d
                dest=rho+sg*(S+1-s)
                sl=pl.ds(c*rows,rows)
                if s>1 and c in chunks(d,s-1):
                    rd(d,s-1,c).wait_recv()
                    buf[d,s-2,sl,:] = (buf[d,s-2,sl,:].astype(jnp.float32)+part[slotf(dest),sl,:].astype(jnp.float32)).astype(buf.dtype)
                    src=buf.at[d,s-2,sl]
                else:
                    src=part.at[slotf(dest),sl]
                cp=rcopy(src,buf.at[d,s-1,sl],send.at[d,s-1,c],recv.at[d,s-1,c],ring.dev(rho+sg))
                cp.start(); sends.append(cp)
    for c in range(K):
        for d in (0,1):
            rd(d,S,c).wait_recv()
    for cp in sends: cp.wait_send()

HEAD_SIZE = 64
EPSILON = 1e-05
HIGHEST = lax.Precision.HIGHEST
F32 = jnp.float32
BF16 = jnp.bfloat16
ANY_SPEC = pl.BlockSpec(memory_space=pl.ANY)
VMEM_SPEC = pl.BlockSpec(memory_space=pltpu.VMEM)
CHUNKS = 4
DMA = pltpu.SemaphoreType.DMA


def comm_params(number):
    return pltpu.CompilerParams(
        collective_id=number, has_side_effects=True, vmem_limit_bytes=40 << 20
    )


def gather_group(rows, planes):
    count, width = rows.shape

    def kernel(x_ref, o_ref, send, recv, own):
        ring = Ring8(planes)
        barrier([ring.dev(ring.rho + 1), ring.dev(ring.rho - 1)])
        local = pltpu.make_async_copy(x_ref, o_ref.at[ring.slot(ring.rho)], own)
        local.start()
        ag_ring(ring, CHUNKS, x_ref, o_ref, send, recv)
        local.wait()

    return pl.pallas_call(
        kernel,
        out_shape=jax.ShapeDtypeStruct((2 * planes, count, width), BF16),
        in_specs=[VMEM_SPEC],
        out_specs=ANY_SPEC,
        scratch_shapes=[DMA((2, planes, CHUNKS)), DMA((2, planes, CHUNKS)), DMA],
        compiler_params=comm_params(0),
        name="gather_group",
    )(rows)


def scatter_group(parts, planes, number):
    _, count, width = parts.shape

    def kernel(p_ref, o_ref, buf, send, recv):
        ring = Ring8(planes)
        barrier([ring.dev(ring.rho + 1), ring.dev(ring.rho - 1)])
        rs_ring(ring, CHUNKS, p_ref, buf, send, recv, ring.slot)
        last = planes - 1
        o_ref[...] = (
            buf[0, last].astype(F32) + buf[1, last].astype(F32)
        ) + p_ref[ring.slot(ring.rho)].astype(F32)

    return pl.pallas_call(
        kernel,
        out_shape=jax.ShapeDtypeStruct((count, width), F32),
        in_specs=[VMEM_SPEC],
        out_specs=VMEM_SPEC,
        scratch_shapes=[
            pltpu.VMEM((2, planes, count, width), BF16),
            DMA((2, planes, CHUNKS)),
            DMA((2, planes, CHUNKS)),
        ],
        compiler_params=comm_params(number),
        name="scatter_group",
    )(parts)


def gather_plane(rows):
    count, width = rows.shape

    def kernel(x_ref, o_ref, send, recv, sib_send, sib_recv, own):
        ring = Ring4()
        barrier([ring.dev(ring.rho + 1), ring.dev(ring.rho - 1), ring.sib_dev()])
        local = pltpu.make_async_copy(x_ref, o_ref.at[ring.slot(ring.rho)], own)
        local.start()
        ag_ring(ring, CHUNKS, x_ref, o_ref, send, recv, (sib_send, sib_recv))
        local.wait()

    return pl.pallas_call(
        kernel,
        out_shape=jax.ShapeDtypeStruct((8, count, width), BF16),
        in_specs=[VMEM_SPEC],
        out_specs=ANY_SPEC,
        scratch_shapes=[
            DMA((2, 2, CHUNKS)),
            DMA((2, 2, CHUNKS)),
            DMA((4, CHUNKS)),
            DMA((4, CHUNKS)),
            DMA,
        ],
        compiler_params=comm_params(3),
        name="gather_plane",
    )(rows)


def scatter_plane(parts):
    _, count, width = parts.shape

    def kernel(p_ref, o_ref, pair, buf, send, recv, sib_send, sib_recv):
        ring = Ring4()
        barrier([ring.dev(ring.rho + 1), ring.dev(ring.rho - 1), ring.sib_dev()])

        def chip(r):
            x, b = ring.pos(r)
            return x * 2 + b

        copies = []
        for i in (2, 1, 3, 0):
            copy = rcopy(
                p_ref.at[ring.slot(ring.rho + i, True)],
                pair.at[chip(ring.rho + i)],
                sib_send.at[i],
                sib_recv.at[i],
                ring.sib_dev(),
            )
            copy.start()
            copies.append(copy)
        for i, copy in zip((2, 1, 3, 0), copies):
            place = chip(ring.rho + i)
            copy.wait_recv()
            pair[place] = (
                pair[place].astype(F32) + p_ref[ring.slot(ring.rho + i)].astype(F32)
            ).astype(BF16)
        rs_ring(ring, CHUNKS, pair, buf, send, recv, chip)
        o_ref[...] = (
            buf[0, 1].astype(F32) + buf[1, 1].astype(F32)
        ) + pair[chip(ring.rho)].astype(F32)
        for copy in copies:
            copy.wait_send()

    return pl.pallas_call(
        kernel,
        out_shape=jax.ShapeDtypeStruct((count, width), F32),
        in_specs=[VMEM_SPEC],
        out_specs=VMEM_SPEC,
        scratch_shapes=[
            pltpu.VMEM((4, count, width), BF16),
            pltpu.VMEM((2, 2, count, width), BF16),
            DMA((2, 2, CHUNKS)),
            DMA((2, 2, CHUNKS)),
            DMA((4,)),
            DMA((4,)),
        ],
        compiler_params=comm_params(4),
        name="scatter_plane",
    )(parts)


def norm_factor(stream):
    return lax.rsqrt(jnp.mean(stream * stream, axis=-1, keepdims=True) + EPSILON)


def norm_back(stream, factor, gain_row, upstream):
    scaled = gain_row * upstream
    inner_mean = jnp.mean(stream * scaled, axis=-1, keepdims=True)
    return factor * scaled - stream * (factor * factor * factor) * inner_mean


def rotate(source, cosine, sine):
    half = HEAD_SIZE // 2
    shaped = source.reshape(source.shape[0], -1, HEAD_SIZE)
    first, second = shaped[..., :half], shaped[..., half:]
    c, s = cosine[:, None, :], sine[:, None, :]
    turned = jnp.concatenate([first * c - second * s, second * c + first * s], axis=-1)
    return turned.reshape(source.shape)


def attend_blocks(length):
    rows = min(512, length)
    return [(i * rows, (i + 1) * rows) for i in range(length // rows)]


def masked(scores, documents, start, stop):
    ids = jnp.arange(stop, dtype=jnp.int32)
    allowed = (documents[start:stop, None] == documents[None, :stop]) & (
        ids[None, :] <= ids[start:stop, None]
    )
    return jnp.where(allowed[None], scores * (1.0 / math.sqrt(HEAD_SIZE)), -1e30)


def attend(queries, keys, values, documents):
    mixed, logs = [], []
    for start, stop in attend_blocks(queries.shape[0]):
        scores = masked(
            jnp.einsum(
                "qhd,kd->hqk", queries[start:stop], keys[:stop], preferred_element_type=F32
            ),
            documents,
            start,
            stop,
        )
        highest = jnp.max(scores, axis=-1, keepdims=True)
        weights = jnp.exp(scores - highest)
        totals = jnp.sum(weights, axis=-1, keepdims=True)
        probs = (weights / totals).astype(BF16)
        mixed.append(
            jnp.einsum("hqk,kd->qhd", probs, values[:stop], preferred_element_type=F32).astype(BF16)
        )
        logs.append(highest + jnp.log(totals))
    return jnp.concatenate(mixed, axis=0), logs


def attend_back(queries, keys, values, documents, logs, mixed_grad):
    scale = 1.0 / math.sqrt(HEAD_SIZE)
    key_sum = jnp.zeros(keys.shape, F32)
    value_sum = jnp.zeros(values.shape, F32)
    query_list = []
    for (start, stop), log in zip(attend_blocks(queries.shape[0]), logs):
        query_rows, upstream = queries[start:stop], mixed_grad[start:stop]
        scores = masked(
            jnp.einsum("qhd,kd->hqk", query_rows, keys[:stop], preferred_element_type=F32),
            documents,
            start,
            stop,
        )
        probs = jnp.exp(scores - log)
        prob_grad = jnp.einsum("qhd,kd->hqk", upstream, values[:stop], preferred_element_type=F32)
        centre = jnp.sum(probs * prob_grad, axis=-1, keepdims=True)
        score_grad = (probs * (prob_grad - centre)).astype(BF16)
        query_list.append(
            jnp.einsum("hqk,kd->qhd", score_grad, keys[:stop], preferred_element_type=F32) * scale
        )
        key_sum = key_sum.at[:stop].add(
            jnp.einsum("hqk,qhd->kd", score_grad, query_rows, preferred_element_type=F32) * scale
        )
        value_sum = value_sum.at[:stop].add(
            jnp.einsum("hqk,qhd->kd", probs.astype(BF16), upstream, preferred_element_type=F32)
        )
    return jnp.concatenate(query_list, axis=0).astype(BF16), key_sum.astype(BF16), value_sum.astype(BF16)


def per_device(
    layer_in,
    cotangent,
    doc_starts,
    routes,
    attn_gain,
    ffn_gain,
    query_weight,
    key_matrix,
    value_matrix,
    out_weight,
    router_weight,
    gate_weight,
    up_weight,
    down_weight,
):
    planes, groups = lax.axis_size("za"), lax.axis_size("grp")
    seq_count = 2 * planes
    place = lax.axis_index("za") * 2 + lax.axis_index("yb")
    count, width = layer_in.shape[1:]
    length = count * seq_count
    layers = attn_gain.shape[0]
    experts_all = router_weight.shape[2]
    local = gate_weight.shape[1]
    top = routes.shape[2]
    slots = -(-(count * top * 4 // (3 * experts_all) + 1) // 16) * 16
    heads = query_weight.shape[2] // HEAD_SIZE // 8
    columns = heads * HEAD_SIZE
    kv = key_matrix.shape[2] // 8
    bands = query_weight.shape[1]

    swap = [(a * 4 + f, f * 4 + a) for a in range(planes) for f in range(4)]

    def exchange(array):
        return lax.ppermute(array, ("za", "xh", "co"), swap)

    stream = exchange(layer_in[0]).astype(F32)
    upstream_low = exchange(cotangent[0])
    starts = exchange(doc_starts)[0]
    chosen = exchange(routes[0])

    small = jnp.stack([attn_gain, ffn_gain], axis=-1)
    pieces = jnp.concatenate(
        [
            jnp.moveaxis(query_weight.reshape(layers, bands, 8, columns), 2, 0),
            jnp.moveaxis(key_matrix.reshape(layers, bands, 8, kv), 2, 0),
            jnp.moveaxis(value_matrix.reshape(layers, bands, 8, kv), 2, 0),
            jnp.broadcast_to(
                jnp.concatenate([router_weight, small], axis=-1)[None],
                (8, layers, bands, experts_all + 2),
            ),
        ],
        axis=-1,
    )
    used = pieces.shape[-1]
    slab = lax.all_to_all(pieces, ("xh", "co", "yb"), 0, 0)
    slab = lax.all_gather(slab, ("za", "grp"))
    slab = slab.reshape(planes, groups, 4, 2, layers, bands, used)
    slab = jnp.transpose(slab, (4, 0, 3, 1, 2, 5, 6)).reshape(layers, width, used)
    qkv_weight = slab[:, :, : columns + 2 * kv]
    router_full = slab[:, :, columns + 2 * kv : columns + 2 * kv + experts_all]
    gains = slab[:, :, columns + 2 * kv + experts_all :].astype(F32)
    out_rows = lax.all_gather(out_weight, ("za", "grp"))
    out_rows = lax.all_to_all(
        out_rows.reshape(planes, groups, layers, bands, width), ("xh", "co"), 0, 0
    )
    out_rows = jnp.transpose(out_rows, (2, 1, 0, 3, 4)).reshape(layers, columns, width)

    def fetch_experts(layer):
        return (
            lax.all_gather(gate_weight[layer], ("grp", "xh", "co"), axis=1, tiled=True),
            lax.all_gather(up_weight[layer], ("grp", "xh", "co"), axis=1, tiled=True),
            lax.all_gather(down_weight[layer], ("grp", "xh", "co"), axis=2, tiled=True),
        )

    named = jnp.sum(
        (chosen[:, :, None] == jnp.arange(experts_all, dtype=jnp.int32)).astype(F32), axis=1
    )
    ids = jnp.arange(count, dtype=jnp.int32)
    before = (ids[None, :] < ids[:, None]).astype(BF16)
    rank = jnp.dot(before, named.astype(BF16), preferred_element_type=F32)
    codes = lax.all_gather(jnp.where(named > 0, rank, -1.0).astype(BF16), ("za", "yb"))
    routed = (codes >= 0).reshape(length, experts_all)
    mine = lax.dynamic_slice_in_dim(codes, place * local, local, axis=2).astype(F32)
    slot_ids = jnp.arange(slots, dtype=jnp.int32).astype(F32)
    spread = mine[:, :, :, None] == slot_ids
    back_ones = spread.reshape(seq_count, count, local * slots).astype(BF16)
    row_ones = jnp.transpose(spread, (0, 2, 3, 1)).reshape(seq_count, local * slots, count)
    row_ones = row_ones.astype(BF16)

    def to_experts(rows):
        shaped = rows.reshape(seq_count, local, slots, -1)
        return jnp.moveaxis(shaped, 1, 0).reshape(local, seq_count * slots, -1)

    def from_experts(rows):
        shaped = rows.reshape(local, seq_count, slots, -1)
        return jnp.moveaxis(shaped, 0, 1).reshape(seq_count, local * slots, -1)

    positions = jnp.arange(length, dtype=jnp.int32)
    documents = jnp.sum((starts[None, :] <= positions[:, None]).astype(jnp.int32), axis=1) - 1
    inverse = 10000.0 ** (
        -2.0 * jnp.arange(HEAD_SIZE // 2, dtype=F32) / HEAD_SIZE
    )
    angles = positions.astype(F32)[:, None] * inverse[None, :]
    cosine, sine = jnp.cos(angles), jnp.sin(angles)

    states = []
    for layer in range(layers):
        gate_w, up_w, down_w = fetch_experts(layer)
        attn_row, ffn_row = gains[layer, :, 0], gains[layer, :, 1]
        factor_one = norm_factor(stream)
        normed_one = gather_plane((stream * factor_one * attn_row).astype(BF16))
        normed_one = normed_one.reshape(length, width)
        qkv = jnp.dot(normed_one, qkv_weight[layer], preferred_element_type=F32)
        queries = rotate(qkv[:, :columns], cosine, sine).astype(BF16)
        keys = rotate(qkv[:, columns : columns + kv], cosine, sine).astype(BF16)
        values = qkv[:, columns + kv :].astype(BF16)
        queries = queries.reshape(length, heads, HEAD_SIZE)
        mixed, logs = attend(queries, keys, values, documents)
        mixed = mixed.reshape(length, columns)
        branch = jnp.dot(mixed, out_rows[layer], preferred_element_type=F32).astype(BF16)
        middle = stream + scatter_plane(branch.reshape(8, count, width))
        factor_two = norm_factor(middle)
        own_two = (middle * factor_two * ffn_row).astype(BF16)
        normed_two = gather_group(own_two, planes)
        logits = jnp.dot(
            normed_two.reshape(length, width), router_full[layer], preferred_element_type=F32
        )
        highest = jnp.max(jnp.where(routed, logits, -1e30), axis=-1, keepdims=True)
        raised = jnp.where(routed, jnp.exp(jnp.where(routed, logits - highest, 0.0)), 0.0)
        gate_probs = raised / jnp.sum(raised, axis=-1, keepdims=True)
        gate_probs = gate_probs.reshape(seq_count, count, experts_all)
        own_probs = lax.dynamic_index_in_dim(gate_probs, place, 0, keepdims=False)
        my_probs = lax.dynamic_slice_in_dim(gate_probs, place * local, local, axis=2)
        back_probs = jnp.where(spread, my_probs[..., None], 0.0)
        row_probs = jnp.transpose(back_probs, (0, 2, 3, 1)).reshape(
            seq_count, local * slots, count
        )
        back_probs = back_probs.reshape(seq_count, count, local * slots).astype(BF16)
        rows = to_experts(
            jnp.einsum("brt,btd->brd", row_ones, normed_two, preferred_element_type=BF16)
        )
        gate_part = jnp.einsum("erd,edf->erf", rows, gate_w, preferred_element_type=F32)
        up_part = jnp.einsum("erd,edf->erf", rows, up_w, preferred_element_type=F32)
        hidden = (gate_part * jax.nn.sigmoid(gate_part) * up_part).astype(BF16)
        produced = jnp.einsum("erf,efd->erd", hidden, down_w, preferred_element_type=F32)
        total = jnp.einsum(
            "btr,brd->btd",
            back_probs,
            from_experts(produced.astype(BF16)),
            preferred_element_type=F32,
        ).astype(BF16)
        states.append(
            (
                stream, factor_one, normed_one, queries, keys, values, logs, mixed, middle,
                factor_two, own_two, own_probs, row_probs, rows, gate_part, up_part, hidden,
                gate_w, up_w, down_w,
            )
        )
        stream = middle + scatter_group(total, planes, 1)

    result = exchange(stream.astype(BF16))[None]

    upstream = upstream_low.astype(F32)
    dense_out, expert_out, small_out = [None] * layers, [None] * layers, [None] * layers
    for layer in reversed(range(layers)):
        (
            stream, factor_one, normed_one, queries, keys, values, logs, mixed, middle,
            factor_two, own_two, own_probs, row_probs, rows, gate_part, up_part, hidden,
            gate_w, up_w, down_w,
        ) = states[layer]
        attn_row, ffn_row = gains[layer, :, 0], gains[layer, :, 1]
        arrived = gather_group(upstream.astype(BF16), planes)
        out_rows_grad = to_experts(
            jnp.einsum(
                "brt,btd->brd", row_probs.astype(BF16), arrived, preferred_element_type=F32
            ).astype(BF16)
        )
        hidden_grad = jnp.einsum("erd,efd->erf", out_rows_grad, down_w, preferred_element_type=F32)
        down_term = jnp.einsum("erf,erd->efd", hidden, out_rows_grad, preferred_element_type=F32)
        weighted = jnp.sum(hidden.astype(F32) * hidden_grad, axis=-1)
        logistic = jax.nn.sigmoid(gate_part)
        gate_low = (
            hidden_grad * up_part * logistic * (1.0 + gate_part * (1.0 - logistic))
        ).astype(BF16)
        up_low = (hidden_grad * gate_part * logistic).astype(BF16)
        gate_term = jnp.einsum("erd,erf->edf", rows, gate_low, preferred_element_type=F32)
        up_term = jnp.einsum("erd,erf->edf", rows, up_low, preferred_element_type=F32)
        rows_grad = jnp.einsum("erf,edf->erd", gate_low, gate_w, preferred_element_type=F32)
        rows_grad = (
            rows_grad + jnp.einsum("erf,edf->erd", up_low, up_w, preferred_element_type=F32)
        ).astype(BF16)
        row_sums = jnp.einsum(
            "btr,brd->btd", back_ones, from_experts(rows_grad), preferred_element_type=F32
        ).astype(BF16)
        by_row = jnp.moveaxis(weighted.reshape(local, seq_count, slots), 1, 0)
        by_token = jnp.sum(jnp.where(spread, by_row[:, None], 0.0), axis=-1)
        extra = jnp.zeros((seq_count, count, 64), F32)
        extra = lax.dynamic_update_slice_in_dim(extra, by_token, place * local, axis=2)
        high = extra.astype(BF16)
        rest = (extra - high.astype(F32)).astype(BF16)
        summed = scatter_group(
            jnp.concatenate([row_sums, high, rest], axis=2), planes, 2
        )
        weighted = summed[:, width : width + experts_all]
        weighted = weighted + summed[:, width + 64 : width + 64 + experts_all]
        logit_grad = weighted - own_probs * jnp.sum(weighted, axis=-1, keepdims=True)
        router_term = jnp.einsum("td,te->ed", own_two.astype(F32), logit_grad, precision=HIGHEST)
        normed_two_grad = summed[:, :width] + jnp.einsum(
            "te,de->td", logit_grad, router_full[layer].astype(F32), precision=HIGHEST
        )
        ffn_gain_term = jnp.sum(normed_two_grad * middle * factor_two, axis=0)
        middle_grad = upstream + norm_back(middle, factor_two, ffn_row, normed_two_grad)
        branch_low = gather_plane(middle_grad.astype(BF16)).reshape(length, width)
        out_term = jnp.einsum("tc,td->cd", mixed, branch_low, preferred_element_type=F32)
        mixed_grad = jnp.einsum(
            "td,cd->tc", branch_low, out_rows[layer], preferred_element_type=F32
        ).astype(BF16)
        query_grad, key_grad, value_grad = attend_back(
            queries, keys, values, documents, logs, mixed_grad.reshape(length, heads, HEAD_SIZE)
        )
        query_grad = query_grad.reshape(length, columns)
        low = jnp.concatenate(
            [
                rotate(query_grad.astype(F32), cosine, -sine).astype(BF16),
                rotate(key_grad.astype(F32), cosine, -sine).astype(BF16),
                value_grad,
            ],
            axis=1,
        )
        qkv_term = jnp.einsum("td,tc->dc", normed_one, low, preferred_element_type=F32)
        partial = jnp.einsum(
            "tc,dc->td", low, qkv_weight[layer], preferred_element_type=F32
        ).astype(BF16)
        normed_one_grad = scatter_plane(partial.reshape(8, count, width))
        attn_gain_term = jnp.sum(normed_one_grad * stream * factor_one, axis=0)
        upstream = middle_grad + norm_back(stream, factor_one, attn_row, normed_one_grad)

        expert_out[layer] = (
            lax.psum_scatter(
                gate_term.astype(BF16), ("grp", "xh", "co"), scatter_dimension=1, tiled=True
            ).astype(F32),
            lax.psum_scatter(
                up_term.astype(BF16), ("grp", "xh", "co"), scatter_dimension=1, tiled=True
            ).astype(F32),
            lax.psum_scatter(
                down_term.astype(BF16), ("grp", "xh", "co"), scatter_dimension=2, tiled=True
            ).astype(F32),
        )
        wide = qkv_term.astype(BF16).reshape(planes, 2, groups, 4, bands, columns + 2 * kv)
        wide = jnp.transpose(wide, (0, 2, 3, 1, 4, 5)).reshape(
            planes * groups, 8, bands, columns + 2 * kv
        )
        wide = lax.psum_scatter(wide, ("za", "grp"), scatter_dimension=0)
        wide = lax.all_to_all(wide, ("xh", "co", "yb"), 0, 0)
        tall = out_term.astype(BF16).reshape(groups, 4, bands, width)
        tall = lax.all_to_all(jnp.moveaxis(tall, 1, 0), ("xh", "co"), 0, 0)
        tall = lax.psum_scatter(
            tall.reshape(planes * groups, bands, width), ("za", "grp"), scatter_dimension=0
        )
        dense_out[layer] = (
            jnp.moveaxis(wide[..., :columns], 0, 1).reshape(bands, -1).astype(F32),
            jnp.moveaxis(wide[..., columns : columns + kv], 0, 1).reshape(bands, -1).astype(F32),
            jnp.moveaxis(wide[..., columns + kv :], 0, 1).reshape(bands, -1).astype(F32),
            tall.astype(F32),
        )
        small_out[layer] = jnp.concatenate(
            [router_term, attn_gain_term[None], ffn_gain_term[None]], axis=0
        )

    rest = jnp.stack(small_out)
    kinds = rest.shape[1]
    rest = jnp.moveaxis(rest.reshape(layers, kinds, width // bands, bands), 2, 0)
    rest = lax.psum_scatter(
        rest.reshape(width // bands, layers * kinds, bands),
        ("za", "yb", "grp", "xh", "co"),
        scatter_dimension=0,
    ).reshape(layers, kinds, bands)

    def stacked(lists, i):
        return jnp.stack([lists[layer][i] for layer in range(layers)])

    return (
        result,
        exchange(upstream)[None],
        rest[:, experts_all],
        rest[:, experts_all + 1],
        stacked(dense_out, 0),
        stacked(dense_out, 1),
        stacked(dense_out, 2),
        stacked(dense_out, 3),
        jnp.moveaxis(rest[:, :experts_all], 1, 2),
        stacked(expert_out, 0),
        stacked(expert_out, 1),
        stacked(expert_out, 2),
    )


def solution(mesh):
    seq, fsdp = mesh.shape["seq"], mesh.shape["fsdp"]
    split = Mesh(mesh.devices.reshape(seq // 2, 2, fsdp // 4, 2, 2), AX)
    s, f = ("za", "yb"), ("grp", "xh", "co")
    token = P(f, s, None)
    dense = P(None, s + f, None)
    gain = P(None, s + f)
    wide, tall = P(None, s, f, None), P(None, s, None, f)
    return jax.shard_map(
        per_device,
        mesh=split,
        in_specs=(token, token, P(f, None), token, gain, gain, dense, dense, dense, dense, dense, wide, wide, tall),
        out_specs=(token, token, gain, gain, dense, dense, dense, dense, dense, wide, wide, tall),
        check_vma=False,
    )
```

```python
import functools, math
import jax, jax.numpy as jnp
from jax import lax
from jax.experimental import pallas as pl
from jax.experimental.pallas import tpu as pltpu
from jax.sharding import Mesh, PartitionSpec as P
MESH = pl.DeviceIdType.MESH
AX=("za","yb","grp","xh","co")

class Ring8:
    def __init__(self, na):
        self.n=2*na; self.na=na
        za=lax.axis_index("za"); yb=lax.axis_index("yb")
        self.rho = za + yb*(2*na-1-2*za)
    def pos(self, r):
        r = lax.rem(r+2*self.n, self.n)
        yb = r//self.na
        za = r + yb*(2*self.na-1-2*r)
        return za, yb
    def dev(self, r):
        za,yb=self.pos(r); return {"za":za,"yb":yb}
    def slot(self, r):
        za,yb=self.pos(r); return za*2+yb

class Ring4:
    def __init__(self):
        self.n=4
        x=lax.axis_index("xh"); b=lax.axis_index("yb"); self.c=lax.axis_index("co")
        self.rho = 2*x + (x+b-2*x*b)
    def pos(self, r):
        r = lax.rem(r+2*self.n, self.n)
        x = r//2; m=lax.rem(r,2)
        return x, m+x-2*x*m
    def dev(self, r):
        x,b=self.pos(r); return {"xh":x,"yb":b}
    def slot(self, r, sib=False):
        x,b=self.pos(r); c = (1-self.c) if sib else self.c
        return (x*2+c)*2+b
    def sib_dev(self):
        return {"co":1-self.c}

def barrier(devs):
    sem = pltpu.get_barrier_semaphore()
    for d in devs:
        pl.semaphore_signal(sem, inc=1, device_id=d, device_id_type=MESH)
    pl.semaphore_wait(sem, len(devs))

def rcopy(src, dst, ss, rs, dev):
    return pltpu.make_async_remote_copy(src_ref=src, dst_ref=dst, send_sem=ss, recv_sem=rs, device_id=dev, device_id_type=MESH)

def ag_ring(ring, K, own, out, send, recv, sib=None, beside=None):
    n=ring.n; S=n//2; T=own.shape[0]; rows=T//K; rho=ring.rho
    def chunks(d,s): return range(K) if s<S else (range(K//2) if d==0 else range(K//2,K))
    def mk(d,s,c):
        sg=1-2*d
        slot=ring.slot(rho-(s-1)*sg)
        sl=pl.ds(c*rows,rows)
        src = own.at[sl] if s==1 else out.at[slot,sl]
        return rcopy(src, out.at[slot,sl], send.at[d,s-1,c], recv.at[d,s-1,c], ring.dev(rho+sg))
    def rd(d,s,c):
        sg=1-2*d
        slot=ring.slot(rho-s*sg); sl=pl.ds(c*rows,rows)
        return rcopy(out.at[slot,sl], out.at[slot,sl], send.at[d,s-1,c], recv.at[d,s-1,c], ring.dev(rho-sg))
    started=[]
    def sibcopy(slot, slot_src, c, idx, src):
        ss,rs=sib
        cp=rcopy(src, out.at[slot,pl.ds(c*rows,rows)], ss.at[idx,c], rs.at[idx,c], ring.sib_dev())
        cp.start(); started.append(cp)
    def arrived(d,s,c):
        rd(d,s,c).wait_recv()
        if sib is not None:
            sg=1-2*d
            slot=ring.slot(rho-s*sg)
            idx = s*sg % n
            sibcopy(slot, None, c, idx, out.at[slot,pl.ds(c*rows,rows)])
    sends=[]
    for s in range(1,S+1):
        for c in range(K):
            for d in (0,1):
                if c in chunks(d,s):
                    if s>1: arrived(d,s-1,c)
                    cp=mk(d,s,c); cp.start(); sends.append(cp)
        if beside is not None: beside(s)
        if s==1 and sib is not None:
            for c in range(K): sibcopy(ring.slot(rho), None, c, 0, own.at[pl.ds(c*rows,rows)])
    for s in (S-1,S):
        for c in range(K):
            for d in (0,1):
                if s==S and c in chunks(d,S): arrived(d,S,c)
                if s==S-1 and S>1 and c not in chunks(d,S): arrived(d,S-1,c)
    if sib is not None:
        ss,rs=sib
        for idx in range(n):
            for c in range(K):
                slot=ring.slot(rho-idx, True); sl=pl.ds(c*rows,rows)
                rcopy(out.at[slot,sl],out.at[slot,sl],ss.at[idx,c],rs.at[idx,c],ring.sib_dev()).wait_recv()
    for cp in sends+started: cp.wait_send()

def rs_ring(ring, K, part, buf, send, recv, slotf):
    n=ring.n; S=n//2; T=buf.shape[2]; rows=T//K; rho=ring.rho
    def chunks(d,s): return range(K) if s>1 else (range(K//2) if d==0 else range(K//2,K))
    sends=[]
    def rd(d,s,c):
        sl=pl.ds(c*rows,rows)
        return rcopy(buf.at[d,s-1,sl],buf.at[d,s-1,sl],send.at[d,s-1,c],recv.at[d,s-1,c],ring.dev(rho-(1-2*d)))
    for s in range(1,S+1):
        order=list(range(K))
        if s==2:
            pass
        for c in order:
            for d in (0,1):
                if c not in chunks(d,s): continue
                sg=1-2*d
                dest=rho+sg*(S+1-s)
                sl=pl.ds(c*rows,rows)
                if s>1 and c in chunks(d,s-1):
                    rd(d,s-1,c).wait_recv()
                    buf[d,s-2,sl,:] = (buf[d,s-2,sl,:].astype(jnp.float32)+part[slotf(dest),sl,:].astype(jnp.float32)).astype(buf.dtype)
                    src=buf.at[d,s-2,sl]
                else:
                    src=part.at[slotf(dest),sl]
                cp=rcopy(src,buf.at[d,s-1,sl],send.at[d,s-1,c],recv.at[d,s-1,c],ring.dev(rho+sg))
                cp.start(); sends.append(cp)
    for c in range(K):
        for d in (0,1):
            rd(d,S,c).wait_recv()
    for cp in sends: cp.wait_send()

HEAD_SIZE = 64
EPSILON = 1e-05
HIGHEST = lax.Precision.HIGHEST
F32 = jnp.float32
BF16 = jnp.bfloat16
ANY_SPEC = pl.BlockSpec(memory_space=pl.ANY)
VMEM_SPEC = pl.BlockSpec(memory_space=pltpu.VMEM)
CHUNKS = 4
DMA = pltpu.SemaphoreType.DMA


def comm_params(number):
    return pltpu.CompilerParams(
        collective_id=number, has_side_effects=True, vmem_limit_bytes=40 << 20
    )


def busy(microseconds):
    return pl.CostEstimate(flops=0, bytes_accessed=microseconds * 3_690_000, transcendentals=0)


def gather_group(rows, planes, number=0):
    count, width = rows.shape

    def kernel(x_ref, o_ref, send, recv, own):
        ring = Ring8(planes)
        barrier([ring.dev(ring.rho + 1), ring.dev(ring.rho - 1)])
        local = pltpu.make_async_copy(x_ref, o_ref.at[ring.slot(ring.rho)], own)
        local.start()
        ag_ring(ring, CHUNKS, x_ref, o_ref, send, recv)
        local.wait()

    return pl.pallas_call(
        kernel,
        out_shape=jax.ShapeDtypeStruct((2 * planes, count, width), BF16),
        in_specs=[VMEM_SPEC],
        out_specs=ANY_SPEC,
        scratch_shapes=[DMA((2, planes, CHUNKS)), DMA((2, planes, CHUNKS)), DMA],
        compiler_params=comm_params(number),
        cost_estimate=busy(33),
        name="gather_group",
    )(rows)


def scatter_group(parts, planes, number):
    _, count, width = parts.shape

    def kernel(p_ref, o_ref, buf, send, recv):
        ring = Ring8(planes)
        barrier([ring.dev(ring.rho + 1), ring.dev(ring.rho - 1)])
        rs_ring(ring, CHUNKS, p_ref, buf, send, recv, ring.slot)
        last = planes - 1
        o_ref[...] = (
            buf[0, last].astype(F32) + buf[1, last].astype(F32)
        ) + p_ref[ring.slot(ring.rho)].astype(F32)

    return pl.pallas_call(
        kernel,
        out_shape=jax.ShapeDtypeStruct((count, width), F32),
        in_specs=[VMEM_SPEC],
        out_specs=VMEM_SPEC,
        scratch_shapes=[
            pltpu.VMEM((2, planes, count, width), BF16),
            DMA((2, planes, CHUNKS)),
            DMA((2, planes, CHUNKS)),
        ],
        compiler_params=comm_params(number),
        cost_estimate=busy(32),
        name="scatter_group",
    )(parts)


def gather_plane(rows):
    count, width = rows.shape

    def kernel(x_ref, o_ref, send, recv, sib_send, sib_recv, own):
        ring = Ring4()
        barrier([ring.dev(ring.rho + 1), ring.dev(ring.rho - 1), ring.sib_dev()])
        local = pltpu.make_async_copy(x_ref, o_ref.at[ring.slot(ring.rho)], own)
        local.start()
        ag_ring(ring, CHUNKS, x_ref, o_ref, send, recv, (sib_send, sib_recv))
        local.wait()

    return pl.pallas_call(
        kernel,
        out_shape=jax.ShapeDtypeStruct((8, count, width), BF16),
        in_specs=[VMEM_SPEC],
        out_specs=ANY_SPEC,
        scratch_shapes=[
            DMA((2, 2, CHUNKS)),
            DMA((2, 2, CHUNKS)),
            DMA((4, CHUNKS)),
            DMA((4, CHUNKS)),
            DMA,
        ],
        compiler_params=comm_params(3),
        cost_estimate=busy(20),
        name="gather_plane",
    )(rows)


def scatter_plane(parts):
    _, count, width = parts.shape

    def kernel(p_ref, o_ref, pair, buf, send, recv, sib_send, sib_recv):
        ring = Ring4()
        barrier([ring.dev(ring.rho + 1), ring.dev(ring.rho - 1), ring.sib_dev()])

        def chip(r):
            x, b = ring.pos(r)
            return x * 2 + b

        copies = []
        for i in (2, 1, 3, 0):
            copy = rcopy(
                p_ref.at[ring.slot(ring.rho + i, True)],
                pair.at[chip(ring.rho + i)],
                sib_send.at[i],
                sib_recv.at[i],
                ring.sib_dev(),
            )
            copy.start()
            copies.append(copy)
        for i, copy in zip((2, 1, 3, 0), copies):
            place = chip(ring.rho + i)
            copy.wait_recv()
            pair[place] = (
                pair[place].astype(F32) + p_ref[ring.slot(ring.rho + i)].astype(F32)
            ).astype(BF16)
        rs_ring(ring, CHUNKS, pair, buf, send, recv, chip)
        o_ref[...] = (
            buf[0, 1].astype(F32) + buf[1, 1].astype(F32)
        ) + pair[chip(ring.rho)].astype(F32)
        for copy in copies:
            copy.wait_send()

    return pl.pallas_call(
        kernel,
        out_shape=jax.ShapeDtypeStruct((count, width), F32),
        in_specs=[VMEM_SPEC],
        out_specs=VMEM_SPEC,
        scratch_shapes=[
            pltpu.VMEM((4, count, width), BF16),
            pltpu.VMEM((2, 2, count, width), BF16),
            DMA((2, 2, CHUNKS)),
            DMA((2, 2, CHUNKS)),
            DMA((4,)),
            DMA((4,)),
        ],
        compiler_params=comm_params(4),
        cost_estimate=busy(20),
        name="scatter_plane",
    )(parts)


def plane_peers():
    x, c, b = lax.axis_index("xh"), lax.axis_index("co"), lax.axis_index("yb")
    peers = []
    for k in range(1, 8):
        px = x + (k // 4) * (1 - 2 * x)
        pc = c + (k // 2 % 2) * (1 - 2 * c)
        pb = b + (k % 2) * (1 - 2 * b)
        peers.append(
            ({"xh": px, "co": pc, "yb": pb}, (px * 2 + pc) * 2 + pb, pb * 4 + px * 2 + pc)
        )
    return peers


def own_places():
    x, c, b = lax.axis_index("xh"), lax.axis_index("co"), lax.axis_index("yb")
    return (x * 2 + c) * 2 + b, b * 4 + x * 2 + c


def line_barrier(planes, devices):
    za = lax.axis_index("za")
    sem = pltpu.get_barrier_semaphore()
    for device in devices:
        pl.semaphore_signal(sem, inc=1, device_id=device, device_id_type=MESH)

    @pl.when(za > 0)
    def _():
        pl.semaphore_signal(sem, inc=1, device_id={"za": za - 1}, device_id_type=MESH)

    @pl.when(za < planes - 1)
    def _():
        pl.semaphore_signal(sem, inc=1, device_id={"za": za + 1}, device_id_type=MESH)

    below, above = (za + planes - 1) // planes, (2 * planes - 2 - za) // planes
    pl.semaphore_wait(sem, len(devices) + below + above)


class LineGather:
    def __init__(self, planes, stores, send, recv):
        self.planes, self.stores, self.send, self.recv = planes, stores, send, recv
        self.za = lax.axis_index("za")

    def copy(self, i, d, s):
        sign = 1 - 2 * d
        block = self.za - (s - 1) * sign
        return rcopy(
            self.stores[i].at[block],
            self.stores[i].at[block],
            self.send.at[i, d, s - 1],
            self.recv.at[i, d, s - 1],
            {"za": self.za + sign},
        )

    def sends(self, d, s):
        za, last = self.za, self.planes - 1
        if d == 0:
            return (za < last) & (za >= s - 1)
        return (za > 0) & (za <= last - (s - 1))

    def step(self, s):
        for i in range(len(self.stores)):
            for d in (0, 1):
                if s > 1:
                    self.wait_arrival(i, d, s - 1)

                @pl.when(self.sends(d, s))
                def _():
                    self.copy(i, d, s).start()

    def wait_arrival(self, i, d, s):
        za, last, sign = self.za, self.planes - 1, 1 - 2 * d
        has = (za >= s) if d == 0 else (za <= last - s)

        @pl.when(has)
        def _():
            block = za - s * sign
            ref = self.stores[i].at[block]
            rcopy(
                ref, ref, self.send.at[i, d, s - 1], self.recv.at[i, d, s - 1],
                {"za": za - sign},
            ).wait_recv()

    def finish(self):
        for i in range(len(self.stores)):
            for d in (0, 1):
                self.wait_arrival(i, d, self.planes - 1)
        self.finish_sends()

    def finish_sends(self):
        for i in range(len(self.stores)):
            for d in (0, 1):
                for s in range(1, self.planes):

                    @pl.when(self.sends(d, s))
                    def _():
                        self.copy(i, d, s).wait_send()


def spread_first(pieces, planes):
    _, layers, count, width = pieces.shape

    def kernel(p_ref, a_ref, *refs):
        later, (send, recv, own, z_send, z_recv) = refs[: layers - 1], refs[layers - 1 :]
        za = lax.axis_index("za")
        peers = plane_peers()
        line_barrier(planes, [peer[0] for peer in peers])
        group, place = own_places()
        copies = []

        def target(layer, at):
            return a_ref.at[za, at] if layer == 0 else later[layer - 1].at[at]

        for layer in range(layers):
            for k, (device, their_group, _) in enumerate(peers):
                copy = rcopy(
                    p_ref.at[their_group, layer], target(layer, place),
                    send.at[layer, k], recv.at[layer, k], device,
                )
                copy.start()
                copies.append(copy)
        locals_ = [
            pltpu.make_async_copy(p_ref.at[group, layer], target(layer, place), own.at[layer])
            for layer in range(layers)
        ]
        for copy in locals_:
            copy.start()

        def arrivals(layer):
            for k, (device, _, their_place) in enumerate(peers):
                ref = target(layer, their_place)
                rcopy(ref, ref, send.at[layer, k], recv.at[layer, k], device).wait_recv()
            locals_[layer].wait()

        arrivals(0)
        line = LineGather(planes, [a_ref], z_send, z_recv)
        for s in range(1, planes):
            line.step(s)
            if s == 1:
                for layer in range(1, layers):
                    arrivals(layer)
        line.finish()
        for copy in copies:
            copy.wait_send()

    return pl.pallas_call(
        kernel,
        out_shape=[jax.ShapeDtypeStruct((planes, 8, count, width), BF16)]
        + [jax.ShapeDtypeStruct((8, count, width), BF16)] * (layers - 1),
        in_specs=[VMEM_SPEC],
        out_specs=[VMEM_SPEC] * layers,
        scratch_shapes=[
            DMA((layers, 7)),
            DMA((layers, 7)),
            DMA((layers,)),
            DMA((1, 2, planes - 1)),
            DMA((1, 2, planes - 1)),
        ],
        compiler_params=comm_params(5),
        cost_estimate=busy(20),
        name="spread_first",
    )(pieces)


def gather_plane_first(rows, later, out_weight, planes):
    count, width = rows.shape
    extra = len(later)

    def kernel(x_ref, w_ref, *refs):
        l_refs, refs = refs[:extra], refs[extra:]
        o_ref, t_ref, refs = refs[0], refs[1], refs[2:]
        s_refs, refs = refs[:extra], refs[extra:]
        stage, send, recv, sib_send, sib_recv, own, put, z_send, z_recv, f_send, f_recv = refs
        za = lax.axis_index("za")
        x, c = lax.axis_index("xh"), lax.axis_index("co")
        mine = x * 2 + c
        ring = Ring4()
        peers = plane_peers()
        line_barrier(planes, [peer[0] for peer in peers])
        puts = [
            pltpu.make_async_copy(src, dst.at[za], put.at[i])
            for i, (src, dst) in enumerate(
                [(w_ref, stage)] + [(l_refs[i], s_refs[i]) for i in range(extra)]
            )
        ]
        for copy in puts:
            copy.start()
        local = pltpu.make_async_copy(x_ref, o_ref.at[ring.slot(ring.rho)], own)
        local.start()
        line = LineGather(planes, [stage] + list(s_refs), z_send, z_recv)

        def beside(turn):
            if turn == 1:
                for copy in puts:
                    copy.wait()
            line.step(turn)

        ag_ring(ring, CHUNKS, x_ref, o_ref, send, recv, (sib_send, sib_recv), beside)
        for turn in range(3, planes):
            beside(turn)
        local.wait()
        for d in (0, 1):
            line.wait_arrival(0, d, planes - 1)
        copies = []
        for k in (1, 2, 3):
            px = x + (k // 2) * (1 - 2 * x)
            pc = c + (k % 2) * (1 - 2 * c)
            copies.append(
                rcopy(
                    stage.at[px * 2 + pc], t_ref.at[mine], f_send.at[k - 1], f_recv.at[k - 1],
                    {"xh": px, "co": pc},
                )
            )
            copies[-1].start()
        keep = pltpu.make_async_copy(stage.at[mine], t_ref.at[mine], own)
        keep.start()
        keep.wait()
        for k in (1, 2, 3):
            px = x + (k // 2) * (1 - 2 * x)
            pc = c + (k % 2) * (1 - 2 * c)
            ref = t_ref.at[px * 2 + pc]
            rcopy(ref, ref, f_send.at[k - 1], f_recv.at[k - 1], {"xh": px, "co": pc}).wait_recv()
        for copy in copies:
            copy.wait_send()
        for i in range(1 + extra):
            for d in (0, 1):
                if i > 0:
                    line.wait_arrival(i, d, planes - 1)
        line.finish_sends()

    return pl.pallas_call(
        kernel,
        out_shape=[
            jax.ShapeDtypeStruct((8, count, width), BF16),
            jax.ShapeDtypeStruct((4,) + out_weight.shape, BF16),
        ]
        + [jax.ShapeDtypeStruct((planes,) + array.shape, BF16) for array in later],
        in_specs=[VMEM_SPEC] * (2 + extra),
        out_specs=[ANY_SPEC] + [VMEM_SPEC] * (1 + extra),
        scratch_shapes=[
            pltpu.VMEM((planes,) + out_weight.shape, BF16),
            DMA((2, 2, CHUNKS)),
            DMA((2, 2, CHUNKS)),
            DMA((4, CHUNKS)),
            DMA((4, CHUNKS)),
            DMA,
            DMA((1 + extra,)),
            DMA((1 + extra, 2, planes - 1)),
            DMA((1 + extra, 2, planes - 1)),
            DMA((3,)),
            DMA((3,)),
        ],
        compiler_params=comm_params(6),
        cost_estimate=busy(30),
        name="gather_plane_first",
    )(rows, out_weight, *later)


def collect(wide, tall, planes):
    layers = len(wide)
    count, width = wide[0].shape[2:]
    depth = tall[0].shape[2]

    def kernel(*refs):
        w_in, refs = refs[:layers], refs[layers:]
        t_in, refs = refs[:layers], refs[layers:]
        w_out, refs = refs[:layers], refs[layers:]
        t_out, refs = refs[:layers], refs[layers:]
        w_up, t_own, t_up, summed, own, f_send, f_recv, z_send, z_recv, p_send, p_recv = refs
        za = lax.axis_index("za")
        x, c = lax.axis_index("xh"), lax.axis_index("co")
        mine = x * 2 + c
        peers = plane_peers()
        line_barrier(planes, [peer[0] for peer in peers])
        group, place = own_places()
        firsts, keeps = [], []
        for l in range(layers):
            for k in (1, 2, 3):
                px = x + (k // 2) * (1 - 2 * x)
                pc = c + (k % 2) * (1 - 2 * c)
                copy = rcopy(
                    t_in[l].at[px * 2 + pc], t_own.at[l, mine], f_send.at[l, k - 1],
                    f_recv.at[l, k - 1], {"xh": px, "co": pc},
                )
                copy.start()
                firsts.append(copy)
            keep = pltpu.make_async_copy(t_in[l].at[mine], t_own.at[l, mine], own.at[l])
            keep.start()
            keeps.append(keep)

        def arrive(l):
            for k in (1, 2, 3):
                px = x + (k // 2) * (1 - 2 * x)
                pc = c + (k % 2) * (1 - 2 * c)
                ref = t_own.at[l, px * 2 + pc]
                rcopy(
                    ref, ref, f_send.at[l, k - 1], f_recv.at[l, k - 1], {"xh": px, "co": pc}
                ).wait_recv()
            keeps[l].wait()

        def parts(l, kind):
            if kind == 0:
                return w_in[l], w_up.at[l]
            return t_own.at[l], t_up.at[l]

        def along(l, kind, d, dest):
            _, came = parts(l, kind)
            ref = came.at[d, dest]
            return ref, rcopy(
                ref, ref, z_send.at[l, kind, d, dest], z_recv.at[l, kind, d, dest],
                {"za": za + (1 - 2 * d)},
            )

        last = planes - 1
        for kind in (0, 1):
            if kind == 1:
                for l in range(layers):
                    arrive(l)
            for far in range(last):
                for l in reversed(range(layers)):
                    for d in (0, 1):
                        dest = last - far if d == 0 else far
                        held, came = parts(l, kind)
                        sends = (za < dest) if d == 0 else (za > dest)
                        inner = (za > 0) if d == 0 else (za < last)
                        ref, copy = along(l, kind, d, dest)

                        @pl.when(sends & inner)
                        def _():
                            copy.wait_recv()
                            came[d, dest] = (
                                came[d, dest].astype(F32) + held[dest].astype(F32)
                            ).astype(BF16)
                            copy.start()

                        @pl.when(sends & jnp.logical_not(inner))
                        def _():
                            rcopy(
                                held.at[dest], ref, z_send.at[l, kind, d, dest],
                                z_recv.at[l, kind, d, dest], {"za": za + (1 - 2 * d)},
                            ).start()

        def total(l, kind, result):
            _, came = parts(l, kind)
            for d in (0, 1):

                @pl.when((za > 0) if d == 0 else (za < last))
                def _():
                    ref = came.at[d, za]
                    rcopy(
                        ref, ref, z_send.at[l, kind, d, za], z_recv.at[l, kind, d, za],
                        {"za": za - (1 - 2 * d)},
                    ).wait_recv()
                    result[...] = (result[...].astype(F32) + came[d, za].astype(F32)).astype(BF16)

        outs = []
        for l in reversed(range(layers)):
            summed[l] = w_in[l][za]
            total(l, 0, summed.at[l])
            for k, (device, _, their_place) in enumerate(peers):
                copy = rcopy(
                    summed.at[l, their_place], w_out[l].at[group], p_send.at[l, k],
                    p_recv.at[l, k], device,
                )
                copy.start()
                outs.append(copy)
            w_out[l][group] = summed[l, place]
        for l in reversed(range(layers)):
            t_out[l][...] = t_own[l, za]
            total(l, 1, t_out[l])
        for l in reversed(range(layers)):
            for k, (device, their_group, _) in enumerate(peers):
                ref = w_out[l].at[their_group]
                rcopy(ref, ref, p_send.at[l, k], p_recv.at[l, k], device).wait_recv()
        for copy in firsts + outs:
            copy.wait_send()
        for kind in (0, 1):
            for l in range(layers):
                for d in (0, 1):
                    for far in range(last):
                        dest = last - far if d == 0 else far

                        @pl.when((za < dest) if d == 0 else (za > dest))
                        def _():
                            along(l, kind, d, dest)[1].wait_send()

    return pl.pallas_call(
        kernel,
        out_shape=[jax.ShapeDtypeStruct((8, count, width), BF16)] * layers
        + [jax.ShapeDtypeStruct((count, depth), BF16)] * layers,
        in_specs=[VMEM_SPEC] * (2 * layers),
        out_specs=[VMEM_SPEC] * (2 * layers),
        scratch_shapes=[
            pltpu.VMEM((layers, 2, planes, 8, count, width), BF16),
            pltpu.VMEM((layers, 4, count, depth), BF16),
            pltpu.VMEM((layers, 2, planes, count, depth), BF16),
            pltpu.VMEM((layers, 8, count, width), BF16),
            DMA((layers,)),
            DMA((layers, 3)),
            DMA((layers, 3)),
            DMA((layers, 2, 2, planes)),
            DMA((layers, 2, 2, planes)),
            DMA((layers, 7)),
            DMA((layers, 7)),
        ],
        compiler_params=comm_params(7),
        cost_estimate=busy(40),
        name="collect",
    )(*wide, *tall)


def row_codes(code_rows, first, local, slots, weights=None):
    blocks = []
    for e in range(local):
        code = code_rows(first + e)
        ids = lax.broadcasted_iota(jnp.int32, (slots, code.shape[1]), 0).astype(F32)
        value = 1.0 if weights is None else weights(first + e)
        blocks.append(jnp.where(ids == code, value, 0.0))
    return jnp.concatenate(blocks, axis=0).astype(BF16)


def column_codes(code, first, local, slots, weights=None):
    lanes = lax.broadcasted_iota(jnp.int32, code.shape, 1)
    blocks = []
    for e in range(local):
        chosen = lanes == first + e
        column = jnp.sum(jnp.where(chosen, code, 0.0), axis=1, keepdims=True)
        ids = lax.broadcasted_iota(jnp.int32, (code.shape[0], slots), 1).astype(F32)
        value = 1.0
        if weights is not None:
            value = jnp.sum(jnp.where(chosen, weights, 0.0), axis=1, keepdims=True)
        blocks.append(jnp.where(ids == column, value, 0.0))
    return jnp.concatenate(blocks, axis=1).astype(BF16)


def dot(a, b):
    return jnp.dot(a, b, preferred_element_type=F32)


def dot_t(a, b):
    return lax.dot_general(a, b, (((1,), (1,)), ((), ())), preferred_element_type=F32)


def plain_params(megabytes):
    return pltpu.CompilerParams(
        vmem_limit_bytes=megabytes << 20, dimension_semantics=("arbitrary",)
    )


def once(shape):
    return pl.BlockSpec(shape, lambda e: (0,) * len(shape), pipeline_mode=pl.Buffered(1))


def per_expert(shape):
    return pl.BlockSpec((1,) + shape, lambda e: (e,) + (0,) * len(shape))


def experts_forward(normed, codes, codes_t, router, gate_w, up_w, down_w, slots):
    blocks, count, width = normed.shape
    local, _, hidden_size = gate_w.shape
    lines = local * slots
    halves = 2
    share = blocks // halves

    def kernel(n_ref, c_ref, ct_ref, r_ref, gw_ref, uw_ref, dw_ref, out, g_out, u_out, p_out, pt_out, rows, back):
        e = pl.program_id(0)
        first = (lax.axis_index("za") * 2 + lax.axis_index("yb")) * local

        @pl.when(e == 0)
        def _():
            @pl.loop(0, blocks)
            def _(b):
                tokens = n_ref[b]
                logits = dot(tokens, r_ref[...])
                code = c_ref[b]
                routed = code >= 0.0
                highest = jnp.max(jnp.where(routed, logits, -1e30), axis=1, keepdims=True)
                raised = jnp.where(routed, jnp.exp(logits - highest), 0.0)
                probs = raised / jnp.sum(raised, axis=1, keepdims=True)
                p_out[b] = probs
                pt_out[b] = probs.T[: pt_out.shape[1]]
                back[b] = column_codes(code, first, local, slots, probs)
                ones = row_codes(lambda i: ct_ref[b, pl.ds(i, 1), :], first, local, slots)
                rows[b] = dot(ones, tokens).astype(BF16)

        mine = pl.ds(pl.multiple_of(e * slots, slots), slots)
        for h in range(halves):
            part = pl.ds(h * share, share)
            held = rows[part, mine, :].reshape(share * slots, width)
            gate = dot(held, gw_ref[0])
            up = dot(held, uw_ref[0])
            at = pl.ds(h * share * slots, share * slots)
            g_out[0, at, :] = gate
            u_out[0, at, :] = up
            hidden = (gate * jax.nn.sigmoid(gate) * up).astype(BF16)
            made = dot(hidden, dw_ref[0]).astype(BF16)
            rows[part, mine, :] = made.reshape(share, slots, width)

        @pl.when(e == local - 1)
        def _():
            @pl.loop(0, blocks)
            def _(b):
                out[b] = dot(back[b], rows[b]).astype(BF16)

    wide = (local, blocks * slots, hidden_size)
    return pl.pallas_call(
        kernel,
        grid=(local,),
        out_shape=[
            jax.ShapeDtypeStruct(normed.shape, BF16),
            jax.ShapeDtypeStruct(wide, F32),
            jax.ShapeDtypeStruct(wide, F32),
            jax.ShapeDtypeStruct(codes.shape, F32),
            jax.ShapeDtypeStruct(codes_t.shape, F32),
        ],
        in_specs=[
            once(normed.shape),
            once(codes.shape),
            once(codes_t.shape),
            once(router.shape),
            per_expert(gate_w.shape[1:]),
            per_expert(up_w.shape[1:]),
            per_expert(down_w.shape[1:]),
        ],
        out_specs=[
            once(normed.shape),
            per_expert(wide[1:]),
            per_expert(wide[1:]),
            once(codes.shape),
            once(codes_t.shape),
        ],
        scratch_shapes=[
            pltpu.VMEM((blocks, lines, width), BF16),
            pltpu.VMEM((blocks, count, lines), BF16),
        ],
        compiler_params=plain_params(56),
        cost_estimate=busy(16),
        name="experts_forward",
    )(normed, codes, codes_t, router, gate_w, up_w, down_w)


def experts_backward(
    normed, arrived, codes, codes_t, probs_t, gate_w, up_w, down_w, gate_part, up_part, slots, shares
):
    blocks, count, width = normed.shape
    local, _, hidden_size = gate_w.shape
    lines = local * slots
    total = blocks * slots
    band = width // shares
    split = band % 128 == 0

    def kernel(
        n_ref, a_ref, c_ref, ct_ref, pt_ref, gw_ref, uw_ref, dw_ref, g_ref, u_ref,
        out, dg_out, du_out, dd_out, rows, outs, back, marks,
    ):
        e = pl.program_id(0)
        first = (lax.axis_index("za") * 2 + lax.axis_index("yb")) * local

        @pl.when(e == 0)
        def _():
            @pl.loop(0, blocks)
            def _(b):
                def code(i):
                    return ct_ref[b, pl.ds(i, 1), :]

                def prob(i):
                    return pt_ref[b, pl.ds(i, 1), :]

                back[b] = column_codes(c_ref[b], first, local, slots)
                rows[b] = dot(row_codes(code, first, local, slots), n_ref[b]).astype(BF16)
                outs[b] = dot(row_codes(code, first, local, slots, prob), a_ref[b]).astype(BF16)

        mine = pl.ds(pl.multiple_of(e * slots, slots), slots)
        upstream = outs[:, mine, :].reshape(total, width)
        hidden_grad = dot_t(upstream, dw_ref[0])
        gate, up = g_ref[0], u_ref[0]
        logistic = jax.nn.sigmoid(gate)
        hidden = (gate * logistic * up).astype(BF16)
        gate_low = (hidden_grad * up * logistic * (1.0 + gate * (1.0 - logistic))).astype(BF16)
        up_low = (hidden_grad * gate * logistic).astype(BF16)
        weighted = jnp.sum(hidden.astype(F32) * hidden_grad, axis=1, keepdims=True)
        high = weighted.astype(BF16).astype(F32)
        lanes = lax.broadcasted_iota(jnp.int32, (total, 128), 1)
        mark = jnp.where(lanes == first + e, high, 0.0)
        mark = mark + jnp.where(lanes == first + e + 64, weighted - high, 0.0)
        marks[:, mine, :] = mark.astype(BF16).reshape(blocks, slots, 128)
        turned = rows[:, mine, :].reshape(total, width).T
        for f in range(shares):
            cut = turned[f * band : (f + 1) * band]
            dg_out[f, 0] = dot(cut, gate_low).astype(BF16)
            du_out[f, 0] = dot(cut, up_low).astype(BF16)
        down = dot(hidden.T, upstream).astype(BF16)
        if split:
            for f in range(shares):
                dd_out[f, 0] = down[:, f * band : (f + 1) * band]
        else:
            dd_out[0] = down
        back_rows = dot_t(gate_low, gw_ref[0]) + dot_t(up_low, uw_ref[0])
        rows[:, mine, :] = back_rows.astype(BF16).reshape(blocks, slots, width)

        @pl.when(e == local - 1)
        def _():
            @pl.loop(0, blocks)
            def _(b):
                out[b, :, :width] = dot(back[b], rows[b]).astype(BF16)
                out[b, :, width:] = dot(back[b], marks[b]).astype(BF16)

    cut_shape = (shares, local, band, hidden_size)
    cut_spec = pl.BlockSpec((shares, 1, band, hidden_size), lambda e: (0, e, 0, 0))
    if split:
        down_shape = (shares, local, hidden_size, band)
        down_spec = pl.BlockSpec((shares, 1, hidden_size, band), lambda e: (0, e, 0, 0))
    else:
        down_shape, down_spec = down_w.shape, per_expert(down_w.shape[1:])
    results = pl.pallas_call(
        kernel,
        grid=(local,),
        out_shape=[
            jax.ShapeDtypeStruct((blocks, count, width + 128), BF16),
            jax.ShapeDtypeStruct(cut_shape, BF16),
            jax.ShapeDtypeStruct(cut_shape, BF16),
            jax.ShapeDtypeStruct(down_shape, BF16),
        ],
        in_specs=[
            once(normed.shape),
            once(arrived.shape),
            once(codes.shape),
            once(codes_t.shape),
            once(probs_t.shape),
            per_expert(gate_w.shape[1:]),
            per_expert(up_w.shape[1:]),
            per_expert(down_w.shape[1:]),
            per_expert(gate_part.shape[1:]),
            per_expert(up_part.shape[1:]),
        ],
        out_specs=[once((blocks, count, width + 128)), cut_spec, cut_spec, down_spec],
        scratch_shapes=[
            pltpu.VMEM((blocks, lines, width), BF16),
            pltpu.VMEM((blocks, lines, width), BF16),
            pltpu.VMEM((blocks, count, lines), BF16),
            pltpu.VMEM((blocks, lines, 128), BF16),
        ],
        compiler_params=plain_params(60),
        cost_estimate=busy(30),
        name="experts_backward",
    )(normed, arrived, codes, codes_t, probs_t, gate_w, up_w, down_w, gate_part, up_part)
    row_sums, gate_term, up_term, down_term = results
    if not split:
        down_term = jnp.moveaxis(
            down_term.reshape(local, hidden_size, shares, band), 2, 0
        )
    return row_sums, gate_term, up_term, down_term


def norm_factor(stream):
    return lax.rsqrt(jnp.mean(stream * stream, axis=-1, keepdims=True) + EPSILON)


def norm_back(stream, factor, gain_row, upstream):
    scaled = gain_row * upstream
    inner_mean = jnp.mean(stream * scaled, axis=-1, keepdims=True)
    return factor * scaled - stream * (factor * factor * factor) * inner_mean


def rotate(source, cosine, sine):
    half = HEAD_SIZE // 2
    shaped = source.reshape(source.shape[0], -1, HEAD_SIZE)
    first, second = shaped[..., :half], shaped[..., half:]
    c, s = cosine[:, None, :], sine[:, None, :]
    turned = jnp.concatenate([first * c - second * s, second * c + first * s], axis=-1)
    return turned.reshape(source.shape)


def attend_blocks(length):
    rows = min(512, length)
    return [(i * rows, (i + 1) * rows) for i in range(length // rows)]


def masked(scores, documents, start, stop):
    ids = jnp.arange(stop, dtype=jnp.int32)
    allowed = (documents[start:stop, None] == documents[None, :stop]) & (
        ids[None, :] <= ids[start:stop, None]
    )
    return jnp.where(allowed[None], scores * (1.0 / math.sqrt(HEAD_SIZE)), -1e30)


def attend(queries, keys, values, documents):
    mixed, logs = [], []
    for start, stop in attend_blocks(queries.shape[0]):
        scores = masked(
            jnp.einsum(
                "qhd,kd->hqk", queries[start:stop], keys[:stop], preferred_element_type=F32
            ),
            documents,
            start,
            stop,
        )
        highest = jnp.max(scores, axis=-1, keepdims=True)
        weights = jnp.exp(scores - highest)
        totals = jnp.sum(weights, axis=-1, keepdims=True)
        probs = (weights / totals).astype(BF16)
        mixed.append(
            jnp.einsum("hqk,kd->qhd", probs, values[:stop], preferred_element_type=F32).astype(BF16)
        )
        logs.append(highest + jnp.log(totals))
    return jnp.concatenate(mixed, axis=0), logs


def attend_back(queries, keys, values, documents, logs, mixed_grad):
    scale = 1.0 / math.sqrt(HEAD_SIZE)
    key_sum = jnp.zeros(keys.shape, F32)
    value_sum = jnp.zeros(values.shape, F32)
    query_list = []
    for (start, stop), log in zip(attend_blocks(queries.shape[0]), logs):
        query_rows, upstream = queries[start:stop], mixed_grad[start:stop]
        scores = masked(
            jnp.einsum("qhd,kd->hqk", query_rows, keys[:stop], preferred_element_type=F32),
            documents,
            start,
            stop,
        )
        probs = jnp.exp(scores - log)
        prob_grad = jnp.einsum("qhd,kd->hqk", upstream, values[:stop], preferred_element_type=F32)
        centre = jnp.sum(probs * prob_grad, axis=-1, keepdims=True)
        score_grad = (probs * (prob_grad - centre)).astype(BF16)
        query_list.append(
            jnp.einsum("hqk,kd->qhd", score_grad, keys[:stop], preferred_element_type=F32) * scale
        )
        key_sum = key_sum.at[:stop].add(
            jnp.einsum("hqk,qhd->kd", score_grad, query_rows, preferred_element_type=F32) * scale
        )
        value_sum = value_sum.at[:stop].add(
            jnp.einsum("hqk,qhd->kd", probs.astype(BF16), upstream, preferred_element_type=F32)
        )
    return jnp.concatenate(query_list, axis=0).astype(BF16), key_sum.astype(BF16), value_sum.astype(BF16)


def per_device(
    layer_in,
    cotangent,
    doc_starts,
    routes,
    attn_gain,
    ffn_gain,
    query_weight,
    key_matrix,
    value_matrix,
    out_weight,
    router_weight,
    gate_weight,
    up_weight,
    down_weight,
):
    planes, groups = lax.axis_size("za"), lax.axis_size("grp")
    seq_count = 2 * planes
    place = lax.axis_index("za") * 2 + lax.axis_index("yb")
    count, width = layer_in.shape[1:]
    length = count * seq_count
    layers = attn_gain.shape[0]
    experts_all = router_weight.shape[2]
    local = gate_weight.shape[1]
    top = routes.shape[2]
    slots = -(-(count * top * 4 // (3 * experts_all) + 1) // 16) * 16
    heads = query_weight.shape[2] // HEAD_SIZE // 8
    columns = heads * HEAD_SIZE
    kv = key_matrix.shape[2] // 8
    bands = query_weight.shape[1]

    swap = [(a * 4 + f, f * 4 + a) for a in range(planes) for f in range(4)]

    def exchange(array):
        return lax.ppermute(array, ("za", "xh", "co"), swap)

    stream = exchange(layer_in[0]).astype(F32)
    upstream_low = exchange(cotangent[0])
    starts = exchange(doc_starts)[0]
    chosen = exchange(routes[0])

    small = jnp.stack([attn_gain, ffn_gain], axis=-1)
    used = columns + 2 * kv + experts_all + 2
    padded = -(-used // 128) * 128

    def whole_rows(array):
        if groups == 1:
            return array
        return jnp.moveaxis(lax.all_gather(array, "grp"), 0, 1).reshape(
            layers, groups * bands, array.shape[-1]
        )

    packed = jnp.concatenate(
        [
            jnp.moveaxis(query_weight.reshape(layers, bands, 8, columns), 2, 0),
            jnp.moveaxis(key_matrix.reshape(layers, bands, 8, kv), 2, 0),
            jnp.moveaxis(value_matrix.reshape(layers, bands, 8, kv), 2, 0),
            jnp.broadcast_to(
                jnp.concatenate(
                    [router_weight, small, jnp.zeros((layers, bands, padded - used), BF16)], axis=-1
                )[None],
                (8, layers, bands, padded - columns - 2 * kv),
            ),
        ],
        axis=-1,
    )
    pieces = packed
    if groups > 1:
        pieces = jnp.transpose(lax.all_gather(packed, "grp"), (1, 2, 0, 3, 4)).reshape(
            8, layers, groups * bands, padded
        )
    band_rows = groups * bands

    def in_order(array):
        if groups > 1:
            array = array.reshape(planes, 2, 4, groups, bands, padded)
            array = jnp.swapaxes(array, 2, 3)
        return array.reshape(width, padded)

    first, *later = spread_first(pieces, planes)
    slabs = [in_order(first)]

    def fetch_experts(layer):
        return (
            lax.all_gather(gate_weight[layer], ("grp", "xh", "co"), axis=1, tiled=True),
            lax.all_gather(up_weight[layer], ("grp", "xh", "co"), axis=1, tiled=True),
            lax.all_gather(down_weight[layer], ("grp", "xh", "co"), axis=2, tiled=True),
        )

    def sum_experts(gate_term, up_term, down_term):
        axes = ("grp", "xh", "co")
        return (
            lax.psum_scatter(gate_term, axes, scatter_dimension=0),
            lax.psum_scatter(up_term, axes, scatter_dimension=0),
            lax.psum_scatter(down_term, axes, scatter_dimension=0),
        )

    named = jnp.sum(
        (chosen[:, :, None] == jnp.arange(experts_all, dtype=jnp.int32)).astype(F32), axis=1
    )
    ids = jnp.arange(count, dtype=jnp.int32)
    before = (ids[None, :] < ids[:, None]).astype(BF16)
    rank = jnp.dot(before, named.astype(BF16), preferred_element_type=F32)
    codes = jnp.where(named > 0, rank, -1.0)
    codes = jnp.pad(codes, ((0, 0), (0, 128 - experts_all)), constant_values=-1.0).astype(BF16)
    codes_t = None

    positions = jnp.arange(length, dtype=jnp.int32)
    documents = jnp.sum((starts[None, :] <= positions[:, None]).astype(jnp.int32), axis=1) - 1
    inverse = 10000.0 ** (
        -2.0 * jnp.arange(HEAD_SIZE // 2, dtype=F32) / HEAD_SIZE
    )
    angles = positions.astype(F32)[:, None] * inverse[None, :]
    cosine, sine = jnp.cos(angles), jnp.sin(angles)

    states = []
    out_rows = None
    for layer in range(layers):
        gate_w, up_w, down_w = fetch_experts(layer)
        small_part = slabs[layer][:, columns + 2 * kv :]
        attn_row = small_part[:, experts_all].astype(F32)
        ffn_row = small_part[:, experts_all + 1].astype(F32)
        qkv_w = slabs[layer][:, : columns + 2 * kv]
        router_w = jnp.pad(small_part[:, :experts_all], ((0, 0), (0, 128 - experts_all)))
        factor_one = norm_factor(stream)
        own_one = (stream * factor_one * attn_row).astype(BF16)
        if layer == 0:
            normed_one, tall_rows, *rest = gather_plane_first(
                own_one, later, whole_rows(out_weight), planes
            )
            slabs += [in_order(array) for array in rest]
            tall_rows = tall_rows.reshape(4, layers, groups, bands, width)
            out_rows = jnp.transpose(tall_rows, (1, 2, 0, 3, 4)).reshape(layers, columns, width)
        else:
            normed_one = gather_plane(own_one)
        normed_one = normed_one.reshape(length, width)
        qkv = jnp.dot(normed_one, qkv_w, preferred_element_type=F32)
        queries = rotate(qkv[:, :columns], cosine, sine).astype(BF16)
        keys = rotate(qkv[:, columns : columns + kv], cosine, sine).astype(BF16)
        values = qkv[:, columns + kv :].astype(BF16)
        queries = queries.reshape(length, heads, HEAD_SIZE)
        mixed, logs = attend(queries, keys, values, documents)
        mixed = mixed.reshape(length, columns)
        branch = jnp.dot(mixed, out_rows[layer], preferred_element_type=F32).astype(BF16)
        middle = stream + scatter_plane(branch.reshape(8, count, width))
        factor_two = norm_factor(middle)
        own_two = (middle * factor_two * ffn_row).astype(BF16)
        if layer == 0:
            both = gather_group(jnp.concatenate([own_two, codes], axis=1), planes, 8)
            normed_two, codes = both[..., :width], both[..., width:].astype(F32)
            codes_t = jnp.swapaxes(codes[..., :32], 1, 2)
        else:
            normed_two = gather_group(own_two, planes)
        total, gate_part, up_part, gate_probs, probs_t = experts_forward(
            normed_two, codes, codes_t, router_w, gate_w, up_w, down_w, slots
        )
        own_probs = lax.dynamic_index_in_dim(gate_probs, place, 0, keepdims=False)[:, :experts_all]
        states.append(
            (
                stream, factor_one, normed_one, queries, keys, values, logs, mixed, middle,
                factor_two, own_two, normed_two, own_probs, probs_t, gate_part, up_part,
                gate_w, up_w, down_w, attn_row, ffn_row, qkv_w, router_w,
            )
        )
        stream = middle + scatter_group(total, planes, 1)

    result = exchange(stream.astype(BF16))[None]

    upstream = upstream_low.astype(F32)
    expert_out, previous = [None] * layers, None
    wide_terms, tall_terms = [None] * layers, [None] * layers
    for layer in reversed(range(layers)):
        (
            stream, factor_one, normed_one, queries, keys, values, logs, mixed, middle,
            factor_two, own_two, normed_two, own_probs, probs_t, gate_part, up_part,
            gate_w, up_w, down_w, attn_row, ffn_row, qkv_w, router_w,
        ) = states[layer]
        arrived = gather_group(upstream.astype(BF16), planes)
        row_sums, gate_term, up_term, down_term = experts_backward(
            normed_two, arrived, codes, codes_t, probs_t, gate_w, up_w, down_w, gate_part, up_part,
            slots, 4 * groups,
        )
        terms = (gate_term, up_term, down_term)
        if previous is not None:
            terms, expert_out[layer + 1] = lax.optimization_barrier((terms, previous))
        previous = expert_out[layer] = sum_experts(*terms)
        summed = scatter_group(row_sums, planes, 2)
        weighted = summed[:, width : width + experts_all]
        weighted = weighted + summed[:, width + 64 : width + 64 + experts_all]
        logit_grad = weighted - own_probs * jnp.sum(weighted, axis=-1, keepdims=True)
        router_term = jnp.einsum("td,te->de", own_two.astype(F32), logit_grad, precision=HIGHEST)
        normed_two_grad = summed[:, :width] + jnp.einsum(
            "te,de->td", logit_grad, router_w[:, :experts_all].astype(F32), precision=HIGHEST
        )
        ffn_gain_term = jnp.sum(normed_two_grad * middle * factor_two, axis=0)
        middle_grad = upstream + norm_back(middle, factor_two, ffn_row, normed_two_grad)
        branch_low = gather_plane(middle_grad.astype(BF16)).reshape(length, width)
        out_term = jnp.einsum("tc,td->cd", mixed, branch_low, preferred_element_type=F32)
        mixed_grad = jnp.einsum(
            "td,cd->tc", branch_low, out_rows[layer], preferred_element_type=F32
        ).astype(BF16)
        query_grad, key_grad, value_grad = attend_back(
            queries, keys, values, documents, logs, mixed_grad.reshape(length, heads, HEAD_SIZE)
        )
        query_grad = query_grad.reshape(length, columns)
        low = jnp.concatenate(
            [
                rotate(query_grad.astype(F32), cosine, -sine).astype(BF16),
                rotate(key_grad.astype(F32), cosine, -sine).astype(BF16),
                value_grad,
            ],
            axis=1,
        )
        qkv_term = jnp.einsum("td,tc->dc", normed_one, low, preferred_element_type=F32)
        partial = jnp.einsum(
            "tc,dc->td", low, qkv_w, preferred_element_type=F32
        ).astype(BF16)
        rest = jnp.concatenate([router_term, ffn_gain_term[:, None]], axis=1)
        rest = jnp.pad(rest, ((0, 0), (0, 32 - experts_all - 1)))
        high = rest.astype(BF16)
        low_part = (rest - high.astype(F32)).astype(BF16)
        qkv_term = jnp.concatenate([qkv_term.astype(BF16), high, low_part], axis=1)
        partial, qkv_term, out_term = lax.optimization_barrier(
            (partial, qkv_term, out_term.astype(BF16))
        )
        normed_one_grad = scatter_plane(partial.reshape(8, count, width))
        upstream = middle_grad + norm_back(stream, factor_one, attn_row, normed_one_grad)
        if groups > 1:
            qkv_term = jnp.swapaxes(
                qkv_term.reshape(planes, 2, groups, 4, bands, padded), 2, 3
            )
            out_term = jnp.swapaxes(out_term.reshape(groups, 4, bands, width), 0, 1)
        wide_terms[layer] = qkv_term.reshape(planes, 8, band_rows, padded)
        tall_terms[layer] = out_term.reshape(4, band_rows, width)

    sums = collect(wide_terms, tall_terms, planes)
    if groups > 1:
        sums = [
            lax.psum_scatter(array, "grp", scatter_dimension=array.ndim - 2, tiled=True)
            for array in sums
        ]
    wide_sums = jnp.stack(sums[:layers]).astype(F32)

    def by_heads(start, stop):
        return jnp.swapaxes(wide_sums[..., start:stop], 1, 2).reshape(layers, bands, -1)

    query_out = by_heads(0, columns)
    key_out = by_heads(columns, columns + kv)
    value_out = by_heads(columns + kv, columns + 2 * kv)
    rest = jnp.sum(wide_sums[..., columns + 2 * kv :], axis=1)
    rest = rest[..., :32] + rest[..., 32:64]
    attn_out = (
        jnp.sum(query_weight.astype(F32) * query_out, axis=-1)
        + jnp.sum(key_matrix.astype(F32) * key_out, axis=-1)
        + jnp.sum(value_matrix.astype(F32) * value_out, axis=-1)
    ) / attn_gain.astype(F32)

    def stacked(lists, i):
        return jnp.stack([lists[layer][i] for layer in range(layers)]).astype(F32)

    return (
        result,
        exchange(upstream.astype(BF16)).astype(F32)[None],
        attn_out,
        rest[..., experts_all],
        query_out,
        key_out,
        value_out,
        jnp.stack(sums[layers:]).astype(F32),
        rest[..., :experts_all],
        stacked(expert_out, 0),
        stacked(expert_out, 1),
        stacked(expert_out, 2),
    )


def solution(mesh):
    seq, fsdp = mesh.shape["seq"], mesh.shape["fsdp"]
    split = Mesh(mesh.devices.reshape(seq // 2, 2, fsdp // 4, 2, 2), AX)
    s, f = ("za", "yb"), ("grp", "xh", "co")
    token = P(f, s, None)
    dense = P(None, s + f, None)
    gain = P(None, s + f)
    wide, tall = P(None, s, f, None), P(None, s, None, f)
    return jax.shard_map(
        per_device,
        mesh=split,
        in_specs=(token, token, P(f, None), token, gain, gain, dense, dense, dense, dense, dense, wide, wide, tall),
        out_specs=(token, token, gain, gain, dense, dense, dense, dense, dense, wide, wide, tall),
        check_vma=False,
    )
```

```python
import functools, math
import jax, jax.numpy as jnp
from jax import lax
from jax.experimental import pallas as pl
from jax.experimental.pallas import tpu as pltpu
from jax.sharding import Mesh, PartitionSpec as P
MESH = pl.DeviceIdType.MESH
AX=("za","yb","grp","xh","co")

class Ring8:
    def __init__(self, na):
        self.n=2*na; self.na=na
        za=lax.axis_index("za"); yb=lax.axis_index("yb")
        self.rho = za + yb*(2*na-1-2*za)
    def pos(self, r):
        r = lax.rem(r+2*self.n, self.n)
        yb = r//self.na
        za = r + yb*(2*self.na-1-2*r)
        return za, yb
    def dev(self, r):
        za,yb=self.pos(r); return {"za":za,"yb":yb}
    def slot(self, r):
        za,yb=self.pos(r); return za*2+yb

class Ring4:
    def __init__(self):
        self.n=4
        x=lax.axis_index("xh"); b=lax.axis_index("yb"); self.c=lax.axis_index("co")
        self.rho = 2*x + (x+b-2*x*b)
    def pos(self, r):
        r = lax.rem(r+2*self.n, self.n)
        x = r//2; m=lax.rem(r,2)
        return x, m+x-2*x*m
    def dev(self, r):
        x,b=self.pos(r); return {"xh":x,"yb":b}
    def slot(self, r, sib=False):
        x,b=self.pos(r); c = (1-self.c) if sib else self.c
        return (x*2+c)*2+b
    def sib_dev(self):
        return {"co":1-self.c}

def barrier(devs):
    sem = pltpu.get_barrier_semaphore()
    for d in devs:
        pl.semaphore_signal(sem, inc=1, device_id=d, device_id_type=MESH)
    pl.semaphore_wait(sem, len(devs))

def rcopy(src, dst, ss, rs, dev):
    return pltpu.make_async_remote_copy(src_ref=src, dst_ref=dst, send_sem=ss, recv_sem=rs, device_id=dev, device_id_type=MESH)

def ag_ring(ring, K, own, out, send, recv, sib=None, beside=None):
    n=ring.n; S=n//2; T=own.shape[0]; rows=T//K; rho=ring.rho
    def chunks(d,s): return range(K) if s<S else (range(K//2) if d==0 else range(K//2,K))
    def mk(d,s,c):
        sg=1-2*d
        slot=ring.slot(rho-(s-1)*sg)
        sl=pl.ds(c*rows,rows)
        src = own.at[sl] if s==1 else out.at[slot,sl]
        return rcopy(src, out.at[slot,sl], send.at[d,s-1,c], recv.at[d,s-1,c], ring.dev(rho+sg))
    def rd(d,s,c):
        sg=1-2*d
        slot=ring.slot(rho-s*sg); sl=pl.ds(c*rows,rows)
        return rcopy(out.at[slot,sl], out.at[slot,sl], send.at[d,s-1,c], recv.at[d,s-1,c], ring.dev(rho-sg))
    started=[]
    def sibcopy(slot, slot_src, c, idx, src):
        ss,rs=sib
        cp=rcopy(src, out.at[slot,pl.ds(c*rows,rows)], ss.at[idx,c], rs.at[idx,c], ring.sib_dev())
        cp.start(); started.append(cp)
    def arrived(d,s,c):
        rd(d,s,c).wait_recv()
        if sib is not None:
            sg=1-2*d
            slot=ring.slot(rho-s*sg)
            idx = s*sg % n
            sibcopy(slot, None, c, idx, out.at[slot,pl.ds(c*rows,rows)])
    sends=[]
    for s in range(1,S+1):
        for c in range(K):
            for d in (0,1):
                if c in chunks(d,s):
                    if s>1: arrived(d,s-1,c)
                    cp=mk(d,s,c); cp.start(); sends.append(cp)
        if beside is not None: beside(s)
        if s==1 and sib is not None:
            for c in range(K): sibcopy(ring.slot(rho), None, c, 0, own.at[pl.ds(c*rows,rows)])
    for s in (S-1,S):
        for c in range(K):
            for d in (0,1):
                if s==S and c in chunks(d,S): arrived(d,S,c)
                if s==S-1 and S>1 and c not in chunks(d,S): arrived(d,S-1,c)
    if sib is not None:
        ss,rs=sib
        for idx in range(n):
            for c in range(K):
                slot=ring.slot(rho-idx, True); sl=pl.ds(c*rows,rows)
                rcopy(out.at[slot,sl],out.at[slot,sl],ss.at[idx,c],rs.at[idx,c],ring.sib_dev()).wait_recv()
    for cp in sends+started: cp.wait_send()

class RingGather:
    def __init__(self, ring, chunks, own, out, send, recv):
        self.ring, self.k, self.own, self.out, self.send, self.recv = ring, chunks, own, out, send, recv
        self.last = ring.n // 2
        self.rows = own.shape[0] // chunks

    def chunks(self, d, s):
        if s < self.last:
            return range(self.k)
        return range(self.k // 2) if d == 0 else range(self.k // 2, self.k)

    def copy(self, d, s, c):
        sign = 1 - 2 * d
        slot = self.ring.slot(self.ring.rho - (s - 1) * sign)
        part = pl.ds(c * self.rows, self.rows)
        source = self.own.at[part] if s == 1 else self.out.at[slot, part]
        return rcopy(
            source, self.out.at[slot, part], self.send.at[d, s - 1, c], self.recv.at[d, s - 1, c],
            self.ring.dev(self.ring.rho + sign),
        )

    def arrive(self, d, s, c):
        sign = 1 - 2 * d
        ref = self.out.at[self.ring.slot(self.ring.rho - s * sign), pl.ds(c * self.rows, self.rows)]
        rcopy(
            ref, ref, self.send.at[d, s - 1, c], self.recv.at[d, s - 1, c],
            self.ring.dev(self.ring.rho - sign),
        ).wait_recv()

    def step(self, s):
        for c in range(self.k):
            for d in (0, 1):
                if c in self.chunks(d, s):
                    if s > 1:
                        self.arrive(d, s - 1, c)
                    self.copy(d, s, c).start()

    def finish(self):
        for s in (self.last - 1, self.last):
            for c in range(self.k):
                for d in (0, 1):
                    if c in self.chunks(d, s) and (s == self.last or c not in self.chunks(d, s + 1)):
                        self.arrive(d, s, c)
        for s in range(1, self.last + 1):
            for c in range(self.k):
                for d in (0, 1):
                    if c in self.chunks(d, s):
                        self.copy(d, s, c).wait_send()


def rs_ring(ring, K, part, buf, send, recv, slotf, beside=None):
    n=ring.n; S=n//2; T=buf.shape[2]; rows=T//K; rho=ring.rho
    def chunks(d,s): return range(K) if s>1 else (range(K//2) if d==0 else range(K//2,K))
    sends=[]
    def rd(d,s,c):
        sl=pl.ds(c*rows,rows)
        return rcopy(buf.at[d,s-1,sl],buf.at[d,s-1,sl],send.at[d,s-1,c],recv.at[d,s-1,c],ring.dev(rho-(1-2*d)))
    for s in range(1,S+1):
        order=list(range(K))
        if s==2:
            pass
        for c in order:
            for d in (0,1):
                if c not in chunks(d,s): continue
                sg=1-2*d
                dest=rho+sg*(S+1-s)
                sl=pl.ds(c*rows,rows)
                if s>1 and c in chunks(d,s-1):
                    rd(d,s-1,c).wait_recv()
                    buf[d,s-2,sl,:] = (buf[d,s-2,sl,:].astype(jnp.float32)+part[slotf(dest),sl,:].astype(jnp.float32)).astype(buf.dtype)
                    src=buf.at[d,s-2,sl]
                else:
                    src=part.at[slotf(dest),sl]
                cp=rcopy(src,buf.at[d,s-1,sl],send.at[d,s-1,c],recv.at[d,s-1,c],ring.dev(rho+sg))
                cp.start(); sends.append(cp)
        if beside is not None: beside(s+1)
    for c in range(K):
        for d in (0,1):
            rd(d,S,c).wait_recv()
    for cp in sends: cp.wait_send()

HEAD_SIZE = 64
EPSILON = 1e-05
HIGHEST = lax.Precision.HIGHEST
F32 = jnp.float32
BF16 = jnp.bfloat16
ANY_SPEC = pl.BlockSpec(memory_space=pl.ANY)
VMEM_SPEC = pl.BlockSpec(memory_space=pltpu.VMEM)
CHUNKS = 4
DMA = pltpu.SemaphoreType.DMA


class ShareGather:
    def __init__(self, source, out, sems):
        self.source, self.out = source, out
        self.x_send, self.x_recv, self.s_send, self.s_recv, self.own, self.room = sems
        x, c = lax.axis_index("xh"), lax.axis_index("co")
        self.mine, self.across = x * 2 + c, (1 - x) * 2 + c
        self.beside, self.beside_across = x * 2 + 1 - c, (1 - x) * 2 + 1 - c
        self.chip, self.core = {"xh": 1 - x}, {"co": 1 - c}
        self.parts = source.shape[0]

    def to_chip(self, e):
        return rcopy(
            self.source.at[e], self.out.at[self.mine, e], self.x_send.at[e], self.x_recv.at[e],
            self.chip,
        )

    def to_core(self, e):
        if e == self.parts:
            source, target = self.source, self.out.at[self.mine]
        else:
            source = target = self.out.at[self.across, e]
        return rcopy(source, target, self.s_send.at[e], self.s_recv.at[e], self.core)

    def keep(self, half):
        ends = (self.source, self.room) if half == 0 else (self.room, self.out.at[self.mine])
        return pltpu.make_async_copy(*ends, self.own.at[half])

    def start(self):
        for e in range(self.parts):
            self.to_chip(e).start()
        self.to_core(self.parts).start()
        self.keep(0).start()

    def forward(self):
        self.keep(0).wait()
        self.keep(1).start()
        for e in range(self.parts):
            ref = self.out.at[self.across, e]
            rcopy(ref, ref, self.x_send.at[e], self.x_recv.at[e], self.chip).wait_recv()
            self.to_core(e).start()

    def finish(self):
        for e in range(self.parts + 1):
            ref = self.out.at[self.beside_across, e] if e < self.parts else self.out.at[self.beside]
            rcopy(ref, ref, self.s_send.at[e], self.s_recv.at[e], self.core).wait_recv()
        for e in range(self.parts):
            self.to_chip(e).wait_send()
        for e in range(self.parts + 1):
            self.to_core(e).wait_send()
        self.keep(1).wait()


def share_devices():
    return [{"xh": 1 - lax.axis_index("xh")}, {"co": 1 - lax.axis_index("co")}]


def share_shapes(share):
    if share is None:
        return [], [], []
    array = share[0]
    parts = array.shape[1]
    return (
        [array],
        [jax.ShapeDtypeStruct((4,) + array.shape[1:], BF16)],
        [
            DMA((parts,)),
            DMA((parts,)),
            DMA((parts + 1,)),
            DMA((parts + 1,)),
            DMA((2,)),
            pltpu.VMEM(array.shape[1:], BF16),
        ],
    )


def comm_params(number):
    return pltpu.CompilerParams(
        collective_id=number, has_side_effects=True, vmem_limit_bytes=40 << 20
    )


def busy(microseconds):
    return pl.CostEstimate(flops=0, bytes_accessed=microseconds * 3_690_000, transcendentals=0)


def gather_group(rows, planes, number, share=None):
    count, width = rows.shape
    more, outs, sems = share_shapes(share)

    def kernel(x_ref, *refs):
        if more:
            w_ref, o_ref, b_ref, send, recv, own, *rest = refs
        else:
            o_ref, send, recv, own = refs
        ring = Ring8(planes)
        devices = [ring.dev(ring.rho + 1), ring.dev(ring.rho - 1)]
        barrier(devices + share_devices() * len(more))
        local = pltpu.make_async_copy(x_ref, o_ref.at[ring.slot(ring.rho)], own)
        local.start()
        if more:
            carried = ShareGather(w_ref.at[share[1]], b_ref, rest)
            carried.start()
        ag_ring(ring, CHUNKS, x_ref, o_ref, send, recv)
        if more:
            carried.forward()
            carried.finish()
        local.wait()

    results = pl.pallas_call(
        kernel,
        out_shape=[jax.ShapeDtypeStruct((2 * planes, count, width), BF16)] + outs,
        in_specs=[VMEM_SPEC] + [ANY_SPEC] * len(more),
        out_specs=[ANY_SPEC] * (1 + len(more)),
        scratch_shapes=[DMA((2, planes, CHUNKS)), DMA((2, planes, CHUNKS)), DMA] + sems,
        compiler_params=comm_params(number),
        cost_estimate=busy(33),
        name="gather_group",
    )(rows, *more)
    return results if more else results[0]


def scatter_group(parts, planes, number, share=None):
    _, count, width = parts.shape
    more, outs, sems = share_shapes(share)

    def kernel(p_ref, *refs):
        if more:
            w_ref, o_ref, b_ref, buf, send, recv, *rest = refs
        else:
            o_ref, buf, send, recv = refs
        ring = Ring8(planes)
        devices = [ring.dev(ring.rho + 1), ring.dev(ring.rho - 1)]
        barrier(devices + share_devices() * len(more))
        if more:
            carried = ShareGather(w_ref.at[share[1]], b_ref, rest)
            carried.start()
        rs_ring(ring, CHUNKS, p_ref, buf, send, recv, ring.slot)
        last = planes - 1
        o_ref[...] = (
            buf[0, last].astype(F32) + buf[1, last].astype(F32)
        ) + p_ref[ring.slot(ring.rho)].astype(F32)
        if more:
            carried.forward()
            carried.finish()

    results = pl.pallas_call(
        kernel,
        out_shape=[jax.ShapeDtypeStruct((count, width), F32)] + outs,
        in_specs=[VMEM_SPEC] + [ANY_SPEC] * len(more),
        out_specs=[VMEM_SPEC] + [ANY_SPEC] * len(more),
        scratch_shapes=[
            pltpu.VMEM((2, planes, count, width), BF16),
            DMA((2, planes, CHUNKS)),
            DMA((2, planes, CHUNKS)),
        ]
        + sems,
        compiler_params=comm_params(number),
        cost_estimate=busy(32),
        name="scatter_group",
    )(parts, *more)
    return results if more else results[0]


def gather_plane(rows, tall=None):
    count, width = rows.shape
    more = tall is not None

    def kernel(x_ref, *refs):
        if more:
            w_ref, o_ref, t_ref, *refs = refs
            *refs, f_send, f_recv, f_own = refs
        else:
            o_ref, *refs = refs
        send, recv, sib_send, sib_recv, own = refs
        ring = Ring4()
        if more:
            barrier([peer[0] for peer in plane_peers()])
        else:
            barrier([ring.dev(ring.rho + 1), ring.dev(ring.rho - 1), ring.sib_dev()])
        local = pltpu.make_async_copy(x_ref, o_ref.at[ring.slot(ring.rho)], own)
        local.start()
        ends = []

        def beside(turn):
            if turn == 1 and more:
                ends.append(hand_over(w_ref, t_ref, f_send, f_recv, f_own))

        ag_ring(ring, CHUNKS, x_ref, o_ref, send, recv, (sib_send, sib_recv), beside)
        local.wait()
        for end in ends:
            end()

    shapes = [jax.ShapeDtypeStruct((8, count, width), BF16)]
    if more:
        shapes.append(jax.ShapeDtypeStruct(tall.shape, BF16))
    results = pl.pallas_call(
        kernel,
        out_shape=shapes,
        in_specs=[VMEM_SPEC] * len(shapes),
        out_specs=[ANY_SPEC] + [VMEM_SPEC] * (len(shapes) - 1),
        scratch_shapes=[
            DMA((2, 2, CHUNKS)),
            DMA((2, 2, CHUNKS)),
            DMA((4, CHUNKS)),
            DMA((4, CHUNKS)),
            DMA,
        ]
        + [DMA((3,)), DMA((3,)), DMA] * more,
        compiler_params=comm_params(10 if more else 3),
        cost_estimate=busy(20),
        name="gather_plane",
    )(rows, *([tall] if more else []))
    return results if more else results[0]


def scatter_plane(parts):
    return scatter_plane_call(parts, [], 1, 4, None)[0]


def scatter_plane_first(parts, slabs, out_weight, planes, share):
    return scatter_plane_call(parts, [out_weight, *slabs], planes, 9, share)


def scatter_plane_call(parts, beside, planes, number, share):
    _, count, width = parts.shape
    extra = len(beside)
    more, outs, sems = share_shapes(share)

    def kernel(p_ref, *refs):
        if more:
            w_ref, refs = refs[0], refs[1:]
        b_refs, o_ref, refs = refs[:extra], refs[extra], refs[extra + 1 :]
        if more:
            blocks, refs = refs[0], refs[1:]
        if extra:
            stores, refs = refs[:extra], refs[extra:]
        pair, buf, send, recv, sib_send, sib_recv, refs = *refs[:6], refs[6:]
        ring = Ring4()
        if extra:
            put, z_send, z_recv, *refs = refs
            line_barrier(planes, [peer[0] for peer in plane_peers()])
            if more:
                carried = ShareGather(w_ref.at[share[1]], blocks, refs)
                carried.start()
            za = lax.axis_index("za")
            puts = [
                pltpu.make_async_copy(b_refs[i], stores[i].at[za], put.at[i]) for i in range(extra)
            ]
            for copy in puts:
                copy.start()
            line = LineGather(planes, stores, z_send, z_recv)
        else:
            barrier([ring.dev(ring.rho + 1), ring.dev(ring.rho - 1), ring.sib_dev()])

        def chip(r):
            x, b = ring.pos(r)
            return x * 2 + b

        copies = []
        for i in (2, 1, 3, 0):
            copy = rcopy(
                p_ref.at[ring.slot(ring.rho + i, True)],
                pair.at[chip(ring.rho + i)],
                sib_send.at[i],
                sib_recv.at[i],
                ring.sib_dev(),
            )
            copy.start()
            copies.append(copy)
        if extra:
            for copy in puts:
                copy.wait()
            line.step(1)
        for i, copy in zip((2, 1, 3, 0), copies):
            place = chip(ring.rho + i)
            copy.wait_recv()
            pair[place] = (
                pair[place].astype(F32) + p_ref[ring.slot(ring.rho + i)].astype(F32)
            ).astype(BF16)
        rs_ring(ring, CHUNKS, pair, buf, send, recv, chip, line.step if extra else None)
        o_ref[...] = (
            buf[0, 1].astype(F32) + buf[1, 1].astype(F32)
        ) + pair[chip(ring.rho)].astype(F32)
        for copy in copies:
            copy.wait_send()
        if extra:
            for turn in range(4, planes):
                line.step(turn)
            line.finish()
        if more:
            carried.forward()
            carried.finish()

    shapes, scratch = [], []
    if extra:
        shapes = [
            jax.ShapeDtypeStruct((planes,) + array.shape, BF16) for array in beside
        ]
        scratch = [
            DMA((extra,)),
            DMA((extra, 2, planes - 1)),
            DMA((extra, 2, planes - 1)),
        ]
    return pl.pallas_call(
        kernel,
        out_shape=[jax.ShapeDtypeStruct((count, width), F32)] + outs + shapes,
        in_specs=[VMEM_SPEC] + [ANY_SPEC] * len(more) + [VMEM_SPEC] * extra,
        out_specs=[VMEM_SPEC] + [ANY_SPEC] * len(more) + [VMEM_SPEC] * len(shapes),
        scratch_shapes=[
            pltpu.VMEM((4, count, width), BF16),
            pltpu.VMEM((2, 2, count, width), BF16),
            DMA((2, 2, CHUNKS)),
            DMA((2, 2, CHUNKS)),
            DMA((4,)),
            DMA((4,)),
        ]
        + scratch
        + sems,
        compiler_params=comm_params(number),
        cost_estimate=busy(20),
        name="scatter_plane_first" if extra else "scatter_plane",
    )(parts, *more, *beside)


def plane_peers():
    x, c, b = lax.axis_index("xh"), lax.axis_index("co"), lax.axis_index("yb")
    peers = []
    for k in range(1, 8):
        px = x + (k // 4) * (1 - 2 * x)
        pc = c + (k // 2 % 2) * (1 - 2 * c)
        pb = b + (k % 2) * (1 - 2 * b)
        peers.append(
            ({"xh": px, "co": pc, "yb": pb}, (px * 2 + pc) * 2 + pb, pb * 4 + px * 2 + pc)
        )
    return peers


def own_places():
    x, c, b = lax.axis_index("xh"), lax.axis_index("co"), lax.axis_index("yb")
    return (x * 2 + c) * 2 + b, b * 4 + x * 2 + c


def line_barrier(planes, devices):
    za = lax.axis_index("za")
    sem = pltpu.get_barrier_semaphore()
    for device in devices:
        pl.semaphore_signal(sem, inc=1, device_id=device, device_id_type=MESH)

    @pl.when(za > 0)
    def _():
        pl.semaphore_signal(sem, inc=1, device_id={"za": za - 1}, device_id_type=MESH)

    @pl.when(za < planes - 1)
    def _():
        pl.semaphore_signal(sem, inc=1, device_id={"za": za + 1}, device_id_type=MESH)

    below, above = (za + planes - 1) // planes, (2 * planes - 2 - za) // planes
    pl.semaphore_wait(sem, len(devices) + below + above)


class LineGather:
    def __init__(self, planes, stores, send, recv):
        self.planes, self.stores, self.send, self.recv = planes, stores, send, recv
        self.za = lax.axis_index("za")

    def copy(self, i, d, s):
        sign = 1 - 2 * d
        block = self.za - (s - 1) * sign
        return rcopy(
            self.stores[i].at[block],
            self.stores[i].at[block],
            self.send.at[i, d, s - 1],
            self.recv.at[i, d, s - 1],
            {"za": self.za + sign},
        )

    def sends(self, d, s):
        za, last = self.za, self.planes - 1
        if d == 0:
            return (za < last) & (za >= s - 1)
        return (za > 0) & (za <= last - (s - 1))

    def step(self, s):
        for i in range(len(self.stores)):
            for d in (0, 1):
                if s > 1:
                    self.wait_arrival(i, d, s - 1)

                @pl.when(self.sends(d, s))
                def _():
                    self.copy(i, d, s).start()

    def wait_arrival(self, i, d, s):
        za, last, sign = self.za, self.planes - 1, 1 - 2 * d
        has = (za >= s) if d == 0 else (za <= last - s)

        @pl.when(has)
        def _():
            block = za - s * sign
            ref = self.stores[i].at[block]
            rcopy(
                ref, ref, self.send.at[i, d, s - 1], self.recv.at[i, d, s - 1],
                {"za": za - sign},
            ).wait_recv()

    def finish(self):
        for i in range(len(self.stores)):
            for d in (0, 1):
                self.wait_arrival(i, d, self.planes - 1)
        self.finish_sends()

    def finish_sends(self):
        for i in range(len(self.stores)):
            for d in (0, 1):
                for s in range(1, self.planes):

                    @pl.when(self.sends(d, s))
                    def _():
                        self.copy(i, d, s).wait_send()


def flat_peers():
    x, c = lax.axis_index("xh"), lax.axis_index("co")
    peers = []
    for k in (1, 2, 3):
        px = x + (k // 2) * (1 - 2 * x)
        pc = c + (k % 2) * (1 - 2 * c)
        peers.append(({"xh": px, "co": pc}, px * 2 + pc))
    return peers, x * 2 + c


def hand_over(stage, target, send, recv, own):
    peers, mine = flat_peers()
    copies = []
    for k, (device, f) in enumerate(peers):
        copies.append(rcopy(stage.at[f], target.at[mine], send.at[k], recv.at[k], device))
        copies[-1].start()
    keep = pltpu.make_async_copy(stage.at[mine], target.at[mine], own)
    keep.start()
    return lambda: hand_over_end(peers, target, send, recv, keep, copies)


def hand_over_end(peers, target, send, recv, keep, copies):
    keep.wait()
    for k, (device, f) in enumerate(peers):
        ref = target.at[f]
        rcopy(ref, ref, send.at[k], recv.at[k], device).wait_recv()
    for copy in copies:
        copy.wait_send()


def enter(tokens, heads_part, other_part, out_weight, gain_lane, planes, share):
    count, width = tokens.shape
    more, outs, sems = share_shapes(share)
    layers, rows = heads_part.shape[1:3]
    extra = layers - 1

    def kernel(x_ref, a_ref, b_ref, w_ref, *refs):
        if more:
            s_ref, refs = refs[0], refs[1:]
        o_ref, stream_ref, t_ref, a_out, b_out, refs = *refs[:5], refs[5:]
        a_late, b_late, refs = refs[:extra], refs[extra : 2 * extra], refs[2 * extra :]
        if more:
            blocks, refs = refs[0], refs[1:]
        (
            stage, normed, swap_send, swap_recv, send, recv, own, ring_send, ring_recv, sib_send,
            sib_recv, put, za_send, za_recv, f_send, f_recv, *rest
        ) = refs
        za = lax.axis_index("za")
        x, c = lax.axis_index("xh"), lax.axis_index("co")
        f = x * 2 + c
        px, pc = za // 2, lax.rem(za, 2)
        partner = {"za": f, "xh": px, "co": pc}
        apart = ((za - f) * (za - f) + 8) // 9
        ring = Ring4()
        peers = plane_peers()
        group, place = own_places()

        sem = pltpu.get_barrier_semaphore()
        for peer in peers:
            pl.semaphore_signal(sem, inc=1, device_id=peer[0], device_id_type=MESH)

        @pl.when(za > 0)
        def _():
            pl.semaphore_signal(sem, inc=1, device_id={"za": za - 1}, device_id_type=MESH)

        @pl.when(za < planes - 1)
        def _():
            pl.semaphore_signal(sem, inc=1, device_id={"za": za + 1}, device_id_type=MESH)

        @pl.when(za != f)
        def _():
            pl.semaphore_signal(sem, inc=1, device_id=partner, device_id_type=MESH)

        below, above = (za + planes - 1) // planes, (2 * planes - 2 - za) // planes
        pl.semaphore_wait(sem, len(peers) + below + above + apart)

        def swap():
            return rcopy(x_ref, stream_ref, swap_send, swap_recv, partner)

        @pl.when(za != f)
        def _():
            swap().start()

        keep = pltpu.make_async_copy(x_ref, stream_ref, own.at[2 * layers])

        @pl.when(za == f)
        def _():
            keep.start()

        copies = []

        def target(kind, layer, at):
            if layer == 0:
                return (a_out, b_out)[kind].at[za, at]
            return (a_late, b_late)[kind][layer - 1].at[at]

        def scatter(kind, layer):
            source = (a_ref, b_ref)[kind]
            for k, (device, their_group, _) in enumerate(peers):
                copy = rcopy(
                    source.at[their_group, layer], target(kind, layer, place),
                    send.at[kind, layer, k], recv.at[kind, layer, k], device,
                )
                copy.start()
                copies.append(copy)
            local = pltpu.make_async_copy(
                source.at[group, layer], target(kind, layer, place), own.at[kind * layers + layer]
            )
            local.start()
            return local

        def arrivals(kind, layer, local):
            for k, (device, _, their_place) in enumerate(peers):
                ref = target(kind, layer, their_place)
                rcopy(
                    ref, ref, send.at[kind, layer, k], recv.at[kind, layer, k], device
                ).wait_recv()
            local.wait()

        w_put = pltpu.make_async_copy(w_ref, stage.at[za], put)
        w_put.start()
        b_local = scatter(1, 0)
        a_local = scatter(0, 0)
        if more:
            carried = ShareGather(s_ref.at[share[1]], blocks, rest)
            carried.start()
        tall = LineGather(planes, [stage], za_send.at[pl.ds(2, 1)], za_recv.at[pl.ds(2, 1)])
        small = LineGather(planes, [b_out], za_send.at[pl.ds(0, 1)], za_recv.at[pl.ds(0, 1)])
        line = LineGather(planes, [a_out], za_send.at[pl.ds(1, 1)], za_recv.at[pl.ds(1, 1)])
        arrivals(1, 0, b_local)
        for turn in range(1, planes):
            small.step(turn)
        w_put.wait()
        tall.step(1)
        arrivals(0, 0, a_local)
        line.step(1)
        for d in (0, 1):
            small.wait_arrival(0, d, planes - 1)
        columns = b_out[...].reshape(width, 128).astype(F32)
        gain = columns.T[gain_lane : gain_lane + 1, :]

        @pl.when(za != f)
        def _():
            swap().wait()

        @pl.when(za == f)
        def _():
            keep.wait()

        stream = stream_ref[...].astype(F32)
        factor = lax.rsqrt(jnp.mean(stream * stream, axis=1, keepdims=True) + EPSILON)
        normed[...] = (stream * factor * gain).astype(BF16)
        local = pltpu.make_async_copy(normed, o_ref.at[ring.slot(ring.rho)], own.at[2 * layers])
        local.start()
        ends = []

        def beside(turn):
            if turn <= 2:
                tall.step(turn + 1)
                line.step(turn + 1)
            if turn == 2:
                for layer in range(1, layers):
                    for kind in (1, 0):
                        ends.append((kind, layer, scatter(kind, layer)))

        ag_ring(ring, CHUNKS, normed, o_ref, ring_send, ring_recv, (sib_send, sib_recv), beside)
        for turn in range(4, planes):
            tall.step(turn)
            line.step(turn)
        tall.finish()
        handed = hand_over(stage, t_ref, f_send, f_recv, own.at[2 * layers + 1])
        local.wait()
        line.finish()
        small.finish_sends()
        for kind, layer, local in ends:
            arrivals(kind, layer, local)
        for copy in copies:
            copy.wait_send()
        handed()
        if more:
            carried.forward()
            carried.finish()

    late = [
        jax.ShapeDtypeStruct((8, rows, part.shape[-1]), BF16)
        for part in (heads_part, other_part)
        for _ in range(extra)
    ]
    results = pl.pallas_call(
        kernel,
        out_shape=[
            jax.ShapeDtypeStruct((8, count, width), BF16),
            jax.ShapeDtypeStruct((count, width), BF16),
            jax.ShapeDtypeStruct((4,) + out_weight.shape, BF16),
            jax.ShapeDtypeStruct((planes, 8, rows, heads_part.shape[-1]), BF16),
            jax.ShapeDtypeStruct((planes, 8, rows, other_part.shape[-1]), BF16),
        ]
        + late
        + outs,
        in_specs=[VMEM_SPEC] * 4 + [ANY_SPEC] * len(more),
        out_specs=[ANY_SPEC] + [VMEM_SPEC] * (4 + len(late)) + [ANY_SPEC] * len(more),
        scratch_shapes=[
            pltpu.VMEM((planes,) + out_weight.shape, BF16),
            pltpu.VMEM((count, width), BF16),
            DMA,
            DMA,
            DMA((2, layers, 7)),
            DMA((2, layers, 7)),
            DMA((2 * layers + 2,)),
            DMA((2, 2, CHUNKS)),
            DMA((2, 2, CHUNKS)),
            DMA((4, CHUNKS)),
            DMA((4, CHUNKS)),
            DMA,
            DMA((3, 2, planes - 1)),
            DMA((3, 2, planes - 1)),
            DMA((3,)),
            DMA((3,)),
        ]
        + sems,
        compiler_params=comm_params(5),
        cost_estimate=busy(40),
        name="enter",
    )(tokens, heads_part, other_part, out_weight, *more)
    first, rest = results[:5], results[5:]
    return first, rest[:extra], rest[extra : 2 * extra], rest[2 * extra :]


def collect(wide, tall, planes):
    layers = len(wide)
    count, width = wide[0].shape[2:]
    depth = tall[0].shape[2]

    def kernel(*refs):
        w_in, refs = refs[:layers], refs[layers:]
        t_in, refs = refs[:layers], refs[layers:]
        w_out, refs = refs[:layers], refs[layers:]
        t_out, refs = refs[:layers], refs[layers:]
        w_up, t_own, t_up, summed, own, f_send, f_recv, z_send, z_recv, p_send, p_recv = refs
        za = lax.axis_index("za")
        x, c = lax.axis_index("xh"), lax.axis_index("co")
        mine = x * 2 + c
        peers = plane_peers()
        line_barrier(planes, [peer[0] for peer in peers])
        group, place = own_places()
        firsts, keeps = [], []
        for l in range(layers):
            for k in (1, 2, 3):
                px = x + (k // 2) * (1 - 2 * x)
                pc = c + (k % 2) * (1 - 2 * c)
                copy = rcopy(
                    t_in[l].at[px * 2 + pc], t_own.at[l, mine], f_send.at[l, k - 1],
                    f_recv.at[l, k - 1], {"xh": px, "co": pc},
                )
                copy.start()
                firsts.append(copy)
            keep = pltpu.make_async_copy(t_in[l].at[mine], t_own.at[l, mine], own.at[l])
            keep.start()
            keeps.append(keep)

        def arrive(l):
            for k in (1, 2, 3):
                px = x + (k // 2) * (1 - 2 * x)
                pc = c + (k % 2) * (1 - 2 * c)
                ref = t_own.at[l, px * 2 + pc]
                rcopy(
                    ref, ref, f_send.at[l, k - 1], f_recv.at[l, k - 1], {"xh": px, "co": pc}
                ).wait_recv()
            keeps[l].wait()

        def parts(l, kind):
            if kind == 0:
                return w_in[l], w_up.at[l]
            return t_own.at[l], t_up.at[l]

        def along(l, kind, d, dest):
            _, came = parts(l, kind)
            ref = came.at[d, dest]
            return ref, rcopy(
                ref, ref, z_send.at[l, kind, d, dest], z_recv.at[l, kind, d, dest],
                {"za": za + (1 - 2 * d)},
            )

        last = planes - 1
        for kind in (0, 1):
            if kind == 1:
                for l in range(layers):
                    arrive(l)
            for far in range(last):
                for l in reversed(range(layers)):
                    for d in (0, 1):
                        dest = last - far if d == 0 else far
                        held, came = parts(l, kind)
                        sends = (za < dest) if d == 0 else (za > dest)
                        inner = (za > 0) if d == 0 else (za < last)
                        ref, copy = along(l, kind, d, dest)

                        @pl.when(sends & inner)
                        def _():
                            copy.wait_recv()
                            came[d, dest] = (
                                came[d, dest].astype(F32) + held[dest].astype(F32)
                            ).astype(BF16)
                            copy.start()

                        @pl.when(sends & jnp.logical_not(inner))
                        def _():
                            rcopy(
                                held.at[dest], ref, z_send.at[l, kind, d, dest],
                                z_recv.at[l, kind, d, dest], {"za": za + (1 - 2 * d)},
                            ).start()

        def total(l, kind, result):
            _, came = parts(l, kind)
            for d in (0, 1):

                @pl.when((za > 0) if d == 0 else (za < last))
                def _():
                    ref = came.at[d, za]
                    rcopy(
                        ref, ref, z_send.at[l, kind, d, za], z_recv.at[l, kind, d, za],
                        {"za": za - (1 - 2 * d)},
                    ).wait_recv()
                    result[...] = (result[...].astype(F32) + came[d, za].astype(F32)).astype(BF16)

        outs = []
        for l in reversed(range(layers)):
            summed[l] = w_in[l][za]
            total(l, 0, summed.at[l])
            for k, (device, _, their_place) in enumerate(peers):
                copy = rcopy(
                    summed.at[l, their_place], w_out[l].at[group], p_send.at[l, k],
                    p_recv.at[l, k], device,
                )
                copy.start()
                outs.append(copy)
            w_out[l][group] = summed[l, place]
        for l in reversed(range(layers)):
            t_out[l][...] = t_own[l, za]
            total(l, 1, t_out[l])
        for l in reversed(range(layers)):
            for k, (device, their_group, _) in enumerate(peers):
                ref = w_out[l].at[their_group]
                rcopy(ref, ref, p_send.at[l, k], p_recv.at[l, k], device).wait_recv()
        for copy in firsts + outs:
            copy.wait_send()
        for kind in (0, 1):
            for l in range(layers):
                for d in (0, 1):
                    for far in range(last):
                        dest = last - far if d == 0 else far

                        @pl.when((za < dest) if d == 0 else (za > dest))
                        def _():
                            along(l, kind, d, dest)[1].wait_send()

    return pl.pallas_call(
        kernel,
        out_shape=[jax.ShapeDtypeStruct((8, count, width), BF16)] * layers
        + [jax.ShapeDtypeStruct((count, depth), BF16)] * layers,
        in_specs=[VMEM_SPEC] * (2 * layers),
        out_specs=[VMEM_SPEC] * (2 * layers),
        scratch_shapes=[
            pltpu.VMEM((layers, 2, planes, 8, count, width), BF16),
            pltpu.VMEM((layers, 4, count, depth), BF16),
            pltpu.VMEM((layers, 2, planes, count, depth), BF16),
            pltpu.VMEM((layers, 8, count, width), BF16),
            DMA((layers,)),
            DMA((layers, 3)),
            DMA((layers, 3)),
            DMA((layers, 2, 2, planes)),
            DMA((layers, 2, 2, planes)),
            DMA((layers, 7)),
            DMA((layers, 7)),
        ],
        compiler_params=comm_params(7),
        cost_estimate=busy(40),
        name="collect",
    )(*wide, *tall)


def row_codes(code_rows, first, local, slots, weights=None):
    blocks = []
    for e in range(local):
        code = code_rows(first + e)
        ids = lax.broadcasted_iota(jnp.int32, (slots, code.shape[1]), 0).astype(F32)
        value = 1.0 if weights is None else weights(first + e)
        blocks.append(jnp.where(ids == code, value, 0.0))
    return jnp.concatenate(blocks, axis=0).astype(BF16)


def column_codes(code, first, local, slots, weights=None):
    lanes = lax.broadcasted_iota(jnp.int32, code.shape, 1)
    blocks = []
    for e in range(local):
        chosen = lanes == first + e
        column = jnp.sum(jnp.where(chosen, code, 0.0), axis=1, keepdims=True)
        ids = lax.broadcasted_iota(jnp.int32, (code.shape[0], slots), 1).astype(F32)
        value = 1.0
        if weights is not None:
            value = jnp.sum(jnp.where(chosen, weights, 0.0), axis=1, keepdims=True)
        blocks.append(jnp.where(ids == column, value, 0.0))
    return jnp.concatenate(blocks, axis=1).astype(BF16)


def dot(a, b):
    return jnp.dot(a, b, preferred_element_type=F32)


def dot_t(a, b):
    return lax.dot_general(a, b, (((1,), (1,)), ((), ())), preferred_element_type=F32)


def plain_params(megabytes, number=None):
    return pltpu.CompilerParams(
        vmem_limit_bytes=megabytes << 20,
        dimension_semantics=("arbitrary",),
        collective_id=number,
        has_side_effects=number is not None,
    )


def once(shape):
    return pl.BlockSpec(shape, lambda e: (0,) * len(shape), pipeline_mode=pl.Buffered(1))


def per_expert(shape):
    return pl.BlockSpec((1,) + shape, lambda e: (e,) + (0,) * len(shape))


def shares_of_expert(shape):
    return pl.BlockSpec((shape[0], 1) + shape[2:], lambda e: (0, e, 0, 0))


def side_by_side(ref):
    return jnp.concatenate([ref[i, 0] for i in range(ref.shape[0])], axis=1)


def experts_forward(normed, codes, codes_t, router, gate_w, up_w, down_w, beside, slots, planes, number, share=None):
    blocks, count, width = normed.shape
    _, local, _, hidden_size = gate_w.shape
    more, extra_outs, sems = share_shapes(share)
    lines = local * slots
    halves = 2
    span = blocks // halves

    def kernel(
        n_ref, c_ref, ct_ref, r_ref, gw_ref, uw_ref, dw_ref, x_ref, *refs
    ):
        if more:
            s_ref, refs = refs[0], refs[1:]
        out, g_out, u_out, p_out, pt_out, b_out, *refs = refs
        if more:
            carried = ShareGather(s_ref.at[share[1]], refs[0], refs[6:])
            refs = refs[1:]
        rows, back, send, recv, own = refs[:5]
        e = pl.program_id(0)
        ring = Ring8(planes)
        gather = RingGather(ring, 2, x_ref, b_out, send, recv)
        keep = pltpu.make_async_copy(x_ref, b_out.at[ring.slot(ring.rho)], own)
        first = (lax.axis_index("za") * 2 + lax.axis_index("yb")) * local

        @pl.when(e == 0)
        def _():
            devices = [ring.dev(ring.rho + 1), ring.dev(ring.rho - 1)]
            barrier(devices + share_devices() * len(more))
            keep.start()
            gather.step(1)
            if more:
                carried.start()

            @pl.loop(0, blocks)
            def _(b):
                tokens = n_ref[b]
                logits = dot(tokens, r_ref[...])
                code = c_ref[b]
                routed = code >= 0.0
                highest = jnp.max(jnp.where(routed, logits, -1e30), axis=1, keepdims=True)
                raised = jnp.where(routed, jnp.exp(logits - highest), 0.0)
                probs = raised / jnp.sum(raised, axis=1, keepdims=True)
                p_out[b] = probs
                pt_out[b] = probs.T[: pt_out.shape[1]]
                back[b] = column_codes(code, first, local, slots, probs)
                ones = row_codes(lambda i: ct_ref[b, pl.ds(i, 1), :], first, local, slots)
                rows[b] = dot(ones, tokens).astype(BF16)

            gather.step(2)

        mine = pl.ds(pl.multiple_of(e * slots, slots), slots)
        for h in range(halves):
            part = pl.ds(h * span, span)
            held = rows[part, mine, :].reshape(span * slots, width)
            gate = dot(held, gw_ref[:, 0].reshape(width, hidden_size))
            up = dot(held, uw_ref[:, 0].reshape(width, hidden_size))
            at = pl.ds(h * span * slots, span * slots)
            g_out[0, at, :] = gate
            u_out[0, at, :] = up
            hidden = (gate * jax.nn.sigmoid(gate) * up).astype(BF16)
            made = dot(hidden, side_by_side(dw_ref)).astype(BF16)
            rows[part, mine, :] = made.reshape(span, slots, width)

        for turn in range(3, planes + 1):

            @pl.when(e == min(turn - 3, local - 1))
            def _():
                gather.step(turn)

        @pl.when(e == local - 1)
        def _():
            @pl.loop(0, blocks)
            def _(b):
                out[b] = dot(back[b], rows[b]).astype(BF16)

            gather.finish()
            keep.wait()
            if more:
                carried.forward()
                carried.finish()

    wide = (local, blocks * slots, hidden_size)
    return pl.pallas_call(
        kernel,
        grid=(local,),
        out_shape=[
            jax.ShapeDtypeStruct(normed.shape, BF16),
            jax.ShapeDtypeStruct(wide, F32),
            jax.ShapeDtypeStruct(wide, F32),
            jax.ShapeDtypeStruct(codes.shape, F32),
            jax.ShapeDtypeStruct(codes_t.shape, F32),
            jax.ShapeDtypeStruct((blocks,) + beside.shape, BF16),
        ]
        + extra_outs,
        in_specs=[
            once(normed.shape),
            once(codes.shape),
            once(codes_t.shape),
            once(router.shape),
            shares_of_expert(gate_w.shape),
            shares_of_expert(up_w.shape),
            shares_of_expert(down_w.shape),
            ANY_SPEC,
        ]
        + [ANY_SPEC] * len(more),
        out_specs=[
            once(normed.shape),
            per_expert(wide[1:]),
            per_expert(wide[1:]),
            once(codes.shape),
            once(codes_t.shape),
            ANY_SPEC,
        ]
        + [ANY_SPEC] * len(more),
        scratch_shapes=[
            pltpu.VMEM((blocks, lines, width), BF16),
            pltpu.VMEM((blocks, count, lines), BF16),
            DMA((2, planes, 2)),
            DMA((2, planes, 2)),
            DMA,
        ]
        + sems,
        compiler_params=plain_params(56, number),
        cost_estimate=busy(16),
        name="experts_forward",
    )(normed, codes, codes_t, router, gate_w, up_w, down_w, beside, *more)


def experts_backward(
    normed, arrived, codes, codes_t, probs_t, gate_w, up_w, down_w, gate_part, up_part, slots, shares
):
    blocks, count, width = normed.shape
    pieces = len(arrived)
    _, local, _, hidden_size = gate_w.shape
    lines = local * slots
    total = blocks * slots
    band = width // shares
    split = band % 128 == 0

    def kernel(
        n_ref, c_ref, ct_ref, pt_ref, gw_ref, uw_ref, dw_ref, g_ref, u_ref, *refs
    ):
        a_refs, (out, dg_out, du_out, dd_out, rows, outs, back, marks) = refs[:pieces], refs[pieces:]
        e = pl.program_id(0)
        first = (lax.axis_index("za") * 2 + lax.axis_index("yb")) * local

        @pl.when(e == 0)
        def _():
            @pl.loop(0, blocks)
            def _(b):
                def code(i):
                    return ct_ref[b, pl.ds(i, 1), :]

                def prob(i):
                    return pt_ref[b, pl.ds(i, 1), :]

                back[b] = column_codes(c_ref[b], first, local, slots)
                rows[b] = dot(row_codes(code, first, local, slots), n_ref[b]).astype(BF16)
                upstream = jnp.concatenate([ref[b] for ref in a_refs], axis=0)
                outs[b] = dot(row_codes(code, first, local, slots, prob), upstream).astype(BF16)

        mine = pl.ds(pl.multiple_of(e * slots, slots), slots)
        upstream = outs[:, mine, :].reshape(total, width)
        hidden_grad = dot_t(upstream, side_by_side(dw_ref))
        gate, up = g_ref[0], u_ref[0]
        logistic = jax.nn.sigmoid(gate)
        hidden = (gate * logistic * up).astype(BF16)
        gate_low = (hidden_grad * up * logistic * (1.0 + gate * (1.0 - logistic))).astype(BF16)
        up_low = (hidden_grad * gate * logistic).astype(BF16)
        weighted = jnp.sum(hidden.astype(F32) * hidden_grad, axis=1, keepdims=True)
        high = weighted.astype(BF16).astype(F32)
        lanes = lax.broadcasted_iota(jnp.int32, (total, 128), 1)
        mark = jnp.where(lanes == first + e, high, 0.0)
        mark = mark + jnp.where(lanes == first + e + 64, weighted - high, 0.0)
        marks[:, mine, :] = mark.astype(BF16).reshape(blocks, slots, 128)
        turned = rows[:, mine, :].reshape(total, width).T
        for f in range(shares):
            cut = turned[f * band : (f + 1) * band]
            dg_out[f, 0] = dot(cut, gate_low).astype(BF16)
            du_out[f, 0] = dot(cut, up_low).astype(BF16)
        down = dot(hidden.T, upstream).astype(BF16)
        if split:
            for f in range(shares):
                dd_out[f, 0] = down[:, f * band : (f + 1) * band]
        else:
            dd_out[0] = down
        back_rows = dot_t(gate_low, gw_ref[:, 0].reshape(width, hidden_size))
        back_rows = back_rows + dot_t(up_low, uw_ref[:, 0].reshape(width, hidden_size))
        rows[:, mine, :] = back_rows.astype(BF16).reshape(blocks, slots, width)

        @pl.when(e == local - 1)
        def _():
            @pl.loop(0, blocks)
            def _(b):
                out[b, :, :width] = dot(back[b], rows[b]).astype(BF16)
                out[b, :, width:] = dot(back[b], marks[b]).astype(BF16)

    cut_shape = (shares, local, band, hidden_size)
    cut_spec = pl.BlockSpec((shares, 1, band, hidden_size), lambda e: (0, e, 0, 0))
    if split:
        down_shape = (shares, local, hidden_size, band)
        down_spec = pl.BlockSpec((shares, 1, hidden_size, band), lambda e: (0, e, 0, 0))
    else:
        down_shape = (local, hidden_size, width)
        down_spec = per_expert(down_shape[1:])
    results = pl.pallas_call(
        kernel,
        grid=(local,),
        out_shape=[
            jax.ShapeDtypeStruct((blocks, count, width + 128), BF16),
            jax.ShapeDtypeStruct(cut_shape, BF16),
            jax.ShapeDtypeStruct(cut_shape, BF16),
            jax.ShapeDtypeStruct(down_shape, BF16),
        ],
        in_specs=[
            once(normed.shape),
            once(codes.shape),
            once(codes_t.shape),
            once(probs_t.shape),
            shares_of_expert(gate_w.shape),
            shares_of_expert(up_w.shape),
            shares_of_expert(down_w.shape),
            per_expert(gate_part.shape[1:]),
            per_expert(up_part.shape[1:]),
        ]
        + [once(array.shape) for array in arrived],
        out_specs=[once((blocks, count, width + 128)), cut_spec, cut_spec, down_spec],
        scratch_shapes=[
            pltpu.VMEM((blocks, lines, width), BF16),
            pltpu.VMEM((blocks, lines, width), BF16),
            pltpu.VMEM((blocks, count, lines), BF16),
            pltpu.VMEM((blocks, lines, 128), BF16),
        ],
        compiler_params=plain_params(60),
        cost_estimate=busy(30),
        name="experts_backward",
    )(normed, codes, codes_t, probs_t, gate_w, up_w, down_w, gate_part, up_part, *arrived)
    row_sums, gate_term, up_term, down_term = results
    if not split:
        down_term = jnp.moveaxis(
            down_term.reshape(local, hidden_size, shares, band), 2, 0
        )
    return row_sums, gate_term, up_term, down_term


def norm_factor(stream):
    return lax.rsqrt(jnp.mean(stream * stream, axis=-1, keepdims=True) + EPSILON)


def norm_back(stream, factor, gain_row, upstream):
    scaled = gain_row * upstream
    inner_mean = jnp.mean(stream * scaled, axis=-1, keepdims=True)
    return factor * scaled - stream * (factor * factor * factor) * inner_mean


def rotate(source, cosine, sine):
    half = HEAD_SIZE // 2
    shaped = source.reshape(source.shape[0], -1, HEAD_SIZE)
    first, second = shaped[..., :half], shaped[..., half:]
    c, s = cosine[:, None, :], sine[:, None, :]
    turned = jnp.concatenate([first * c - second * s, second * c + first * s], axis=-1)
    return turned.reshape(source.shape)


def attend_blocks(length):
    rows = min(512, length)
    return [(i * rows, (i + 1) * rows) for i in range(length // rows)]


def masked(scores, documents, start, stop):
    ids = jnp.arange(stop, dtype=jnp.int32)
    allowed = (documents[start:stop, None] == documents[None, :stop]) & (
        ids[None, :] <= ids[start:stop, None]
    )
    return jnp.where(allowed[None], scores * (1.0 / math.sqrt(HEAD_SIZE)), -1e30)


def attend(queries, keys, values, documents):
    mixed, logs = [], []
    for start, stop in attend_blocks(queries.shape[0]):
        scores = masked(
            jnp.einsum(
                "qhd,kd->hqk", queries[start:stop], keys[:stop], preferred_element_type=F32
            ),
            documents,
            start,
            stop,
        )
        highest = jnp.max(scores, axis=-1, keepdims=True)
        weights = jnp.exp(scores - highest)
        totals = jnp.sum(weights, axis=-1, keepdims=True)
        probs = (weights / totals).astype(BF16)
        mixed.append(
            jnp.einsum("hqk,kd->qhd", probs, values[:stop], preferred_element_type=F32).astype(BF16)
        )
        logs.append(highest + jnp.log(totals))
    return jnp.concatenate(mixed, axis=0), logs


def attend_back(queries, keys, values, documents, logs, mixed_grad):
    scale = 1.0 / math.sqrt(HEAD_SIZE)
    key_sum = jnp.zeros(keys.shape, F32)
    value_sum = jnp.zeros(values.shape, F32)
    query_list = []
    for (start, stop), log in zip(attend_blocks(queries.shape[0]), logs):
        query_rows, upstream = queries[start:stop], mixed_grad[start:stop]
        scores = masked(
            jnp.einsum("qhd,kd->hqk", query_rows, keys[:stop], preferred_element_type=F32),
            documents,
            start,
            stop,
        )
        probs = jnp.exp(scores - log)
        prob_grad = jnp.einsum("qhd,kd->hqk", upstream, values[:stop], preferred_element_type=F32)
        centre = jnp.sum(probs * prob_grad, axis=-1, keepdims=True)
        score_grad = (probs * (prob_grad - centre)).astype(BF16)
        query_list.append(
            jnp.einsum("hqk,kd->qhd", score_grad, keys[:stop], preferred_element_type=F32) * scale
        )
        key_sum = key_sum.at[:stop].add(
            jnp.einsum("hqk,qhd->kd", score_grad, query_rows, preferred_element_type=F32) * scale
        )
        value_sum = value_sum.at[:stop].add(
            jnp.einsum("hqk,qhd->kd", probs.astype(BF16), upstream, preferred_element_type=F32)
        )
    return jnp.concatenate(query_list, axis=0).astype(BF16), key_sum.astype(BF16), value_sum.astype(BF16)


def per_device(
    layer_in,
    cotangent,
    doc_starts,
    routes,
    attn_gain,
    ffn_gain,
    query_weight,
    key_matrix,
    value_matrix,
    out_weight,
    router_weight,
    gate_weight,
    up_weight,
    down_weight,
):
    planes, groups = lax.axis_size("za"), lax.axis_size("grp")
    seq_count = 2 * planes
    place = lax.axis_index("za") * 2 + lax.axis_index("yb")
    count, width = layer_in.shape[1:]
    length = count * seq_count
    layers = attn_gain.shape[0]
    experts_all = router_weight.shape[2]
    local = gate_weight.shape[1]
    top = routes.shape[2]
    slots = -(-(count * top * 4 // (3 * experts_all) + 1) // 16) * 16
    heads = query_weight.shape[2] // HEAD_SIZE // 8
    columns = heads * HEAD_SIZE
    kv = key_matrix.shape[2] // 8
    bands = query_weight.shape[1]

    swap = [(a * 4 + f, f * 4 + a) for a in range(planes) for f in range(4)]

    def exchange(array):
        return lax.ppermute(array, ("za", "xh", "co"), swap)

    starts = exchange(doc_starts)[0]
    chosen = exchange(routes[0])

    small = jnp.stack([attn_gain, ffn_gain], axis=-1)
    used = columns + 2 * kv + experts_all + 2
    padded = -(-used // 128) * 128

    def whole_rows(array):
        if groups == 1:
            return array
        return jnp.moveaxis(lax.all_gather(array, "grp"), 0, 1).reshape(
            layers, groups * bands, array.shape[-1]
        )

    packed = jnp.concatenate(
        [
            jnp.moveaxis(query_weight.reshape(layers, bands, 8, columns), 2, 0),
            jnp.moveaxis(key_matrix.reshape(layers, bands, 8, kv), 2, 0),
            jnp.moveaxis(value_matrix.reshape(layers, bands, 8, kv), 2, 0),
            jnp.broadcast_to(
                jnp.concatenate(
                    [router_weight, small, jnp.zeros((layers, bands, padded - used), BF16)], axis=-1
                )[None],
                (8, layers, bands, padded - columns - 2 * kv),
            ),
        ],
        axis=-1,
    )
    pieces = packed
    if groups > 1:
        pieces = jnp.transpose(lax.all_gather(packed, "grp"), (1, 2, 0, 3, 4)).reshape(
            8, layers, groups * bands, padded
        )
    band_rows = groups * bands

    def in_order(array):
        if groups > 1:
            array = array.reshape(planes, 2, 4, groups, bands, -1)
            array = jnp.swapaxes(array, 2, 3)
        return array.reshape(width, -1)

    all_out = whole_rows(out_weight)
    def carry(array, layer):
        return (array, layer) if groups == 1 and layer < layers else None

    firsts, late_heads, late_others, carried = enter(
        layer_in[0],
        pieces[..., : padded - 128],
        pieces[..., padded - 128 :],
        all_out[0],
        used - 2 - (padded - 128),
        planes,
        carry(gate_weight, 0),
    )
    normed_first, stream, tall_rows, heads_slab, other_slab = firsts
    stream = stream.astype(F32)
    slabs = [(in_order(heads_slab), in_order(other_slab))]
    upstream_low, tall_rows = lax.optimization_barrier((cotangent[0], tall_rows))
    upstream_low = exchange(upstream_low)

    def sum_experts(gate_term, up_term, down_term):
        axes = ("grp", "xh", "co")
        return (
            lax.psum_scatter(gate_term, axes, scatter_dimension=0),
            lax.psum_scatter(up_term, axes, scatter_dimension=0),
            lax.psum_scatter(down_term, axes, scatter_dimension=0),
        )

    named = jnp.sum(
        (chosen[:, :, None] == jnp.arange(experts_all, dtype=jnp.int32)).astype(F32), axis=1
    )
    ids = jnp.arange(count, dtype=jnp.int32)
    before = (ids[None, :] < ids[:, None]).astype(BF16)
    rank = jnp.dot(before, named.astype(BF16), preferred_element_type=F32)
    codes = jnp.where(named > 0, rank, -1.0)
    codes = jnp.pad(codes, ((0, 0), (0, 128 - experts_all)), constant_values=-1.0).astype(BF16)
    codes_t = None

    positions = jnp.arange(length, dtype=jnp.int32)
    documents = jnp.sum((starts[None, :] <= positions[:, None]).astype(jnp.int32), axis=1) - 1
    inverse = 10000.0 ** (
        -2.0 * jnp.arange(HEAD_SIZE // 2, dtype=F32) / HEAD_SIZE
    )
    angles = positions.astype(F32)[:, None] * inverse[None, :]
    cosine, sine = jnp.cos(angles), jnp.sin(angles)

    def fetch_experts(layer):
        axes = ("grp", "xh", "co")
        return [
            lax.all_gather(gate_weight[layer], axes, axis=1, tiled=True)[None],
            lax.all_gather(up_weight[layer], axes, axis=1, tiled=True)[None],
            lax.all_gather(down_weight[layer], axes, axis=2, tiled=True)[None],
        ]

    states, arrived = [], []
    out_rows = []
    for layer in range(layers):
        if groups > 1:
            carried = fetch_experts(layer)
        slab = jnp.concatenate(slabs[layer], axis=1)
        small_part = slab[:, columns + 2 * kv :]
        attn_row = small_part[:, experts_all].astype(F32)
        ffn_row = small_part[:, experts_all + 1].astype(F32)
        qkv_w = slab[:, : columns + 2 * kv]
        router_w = jnp.pad(small_part[:, :experts_all], ((0, 0), (0, 128 - experts_all)))
        factor_one = norm_factor(stream)
        if layer == 0:
            normed_one = normed_first
        else:
            own_one = (stream * factor_one * attn_row).astype(BF16)
            normed_one, tall_rows = gather_plane(own_one, tall_rows)
        tall_rows = jnp.swapaxes(tall_rows.reshape(4, groups, bands, width), 0, 1)
        out_rows.append(tall_rows.reshape(columns, width))
        normed_one = normed_one.reshape(length, width)
        qkv = jnp.dot(normed_one, qkv_w, preferred_element_type=F32)
        queries = rotate(qkv[:, :columns], cosine, sine).astype(BF16)
        keys = rotate(qkv[:, columns : columns + kv], cosine, sine).astype(BF16)
        values = qkv[:, columns + kv :].astype(BF16)
        queries = queries.reshape(length, heads, HEAD_SIZE)
        mixed, logs = attend(queries, keys, values, documents)
        mixed = mixed.reshape(length, columns)
        branch = jnp.dot(mixed, out_rows[layer], preferred_element_type=F32).astype(BF16)
        branch = branch.reshape(8, count, width)
        if layer + 1 < layers:
            share = carry(up_weight, 0) if layer == 0 else None
            branch, *later = scatter_plane_first(
                branch, (late_heads[layer], late_others[layer]), all_out[layer + 1], planes, share
            )
            if share is not None:
                carried, later = [carried[0], later[0]], later[1:]
            tall_rows, *later = later
            slabs.append([in_order(array) for array in later])
        else:
            branch = scatter_plane(branch)
        middle = stream + branch
        factor_two = norm_factor(middle)
        own_two = (middle * factor_two * ffn_row).astype(BF16)
        if layer == 0:
            both = jnp.concatenate([own_two, codes], axis=1)
            both = gather_group(both, planes, 8, carry(down_weight, 0))
            if groups == 1:
                both, last = both
                carried = [*carried, last]
            normed_two, codes = both[..., :width], both[..., width:].astype(F32)
            codes_t = jnp.swapaxes(codes[..., :32], 1, 2)
        else:
            share = carry(down_weight, layer)
            normed_two = gather_group(own_two, planes, 12, share)
            if share is not None:
                normed_two, last = normed_two
                carried = [*carried, last]
        share = count // layers
        gate_w, up_w, down_w = carried
        share = count // layers
        total, gate_part, up_part, gate_probs, probs_t, gathered, *carried = experts_forward(
            normed_two, codes, codes_t, router_w, gate_w, up_w, down_w,
            upstream_low[layer * share : (layer + 1) * share], slots, planes,
            11 if layer == 0 else 13, carry(gate_weight, layer + 1),
        )
        arrived.append(gathered)
        own_probs = lax.dynamic_index_in_dim(gate_probs, place, 0, keepdims=False)[:, :experts_all]
        states.append(
            (
                stream, factor_one, normed_one, queries, keys, values, logs, mixed, middle,
                factor_two, own_two, normed_two, own_probs, probs_t, gate_part, up_part,
                gate_w, up_w, down_w, attn_row, ffn_row, qkv_w, router_w,
            )
        )
        share = carry(up_weight, layer + 1)
        added = scatter_group(total, planes, 14 if share is not None else 1, share)
        if share is not None:
            added, last = added
            carried = [*carried, last]
        stream = middle + added

    result = exchange(stream.astype(BF16))[None]

    upstream = upstream_low.astype(F32)
    expert_out, previous = [None] * layers, None
    wide_terms, tall_terms = [None] * layers, [None] * layers
    for layer in reversed(range(layers)):
        (
            stream, factor_one, normed_one, queries, keys, values, logs, mixed, middle,
            factor_two, own_two, normed_two, own_probs, probs_t, gate_part, up_part,
            gate_w, up_w, down_w, attn_row, ffn_row, qkv_w, router_w,
        ) = states[layer]
        if layer + 1 < layers:
            arrived = [gather_group(upstream.astype(BF16), planes, 0)]
        row_sums, gate_term, up_term, down_term = experts_backward(
            normed_two, arrived, codes, codes_t, probs_t, gate_w, up_w, down_w, gate_part, up_part,
            slots, 4 * groups,
        )
        terms = (gate_term, up_term, down_term)
        if previous is not None:
            terms, expert_out[layer + 1] = lax.optimization_barrier((terms, previous))
        previous = expert_out[layer] = sum_experts(*terms)
        summed = scatter_group(row_sums, planes, 2)
        weighted = summed[:, width : width + experts_all]
        weighted = weighted + summed[:, width + 64 : width + 64 + experts_all]
        logit_grad = weighted - own_probs * jnp.sum(weighted, axis=-1, keepdims=True)
        router_term = jnp.einsum("td,te->de", own_two.astype(F32), logit_grad, precision=HIGHEST)
        normed_two_grad = summed[:, :width] + jnp.einsum(
            "te,de->td", logit_grad, router_w[:, :experts_all].astype(F32), precision=HIGHEST
        )
        ffn_gain_term = jnp.sum(normed_two_grad * middle * factor_two, axis=0)
        middle_grad = upstream + norm_back(middle, factor_two, ffn_row, normed_two_grad)
        branch_low = gather_plane(middle_grad.astype(BF16)).reshape(length, width)
        out_term = jnp.einsum("tc,td->cd", mixed, branch_low, preferred_element_type=F32)
        mixed_grad = jnp.einsum(
            "td,cd->tc", branch_low, out_rows[layer], preferred_element_type=F32
        ).astype(BF16)
        query_grad, key_grad, value_grad = attend_back(
            queries, keys, values, documents, logs, mixed_grad.reshape(length, heads, HEAD_SIZE)
        )
        query_grad = query_grad.reshape(length, columns)
        low = jnp.concatenate(
            [
                rotate(query_grad.astype(F32), cosine, -sine).astype(BF16),
                rotate(key_grad.astype(F32), cosine, -sine).astype(BF16),
                value_grad,
            ],
            axis=1,
        )
        qkv_term = jnp.einsum("td,tc->dc", normed_one, low, preferred_element_type=F32)
        partial = jnp.einsum(
            "tc,dc->td", low, qkv_w, preferred_element_type=F32
        ).astype(BF16)
        rest = jnp.concatenate([router_term, ffn_gain_term[:, None]], axis=1)
        rest = jnp.pad(rest, ((0, 0), (0, 32 - experts_all - 1)))
        high = rest.astype(BF16)
        low_part = (rest - high.astype(F32)).astype(BF16)
        qkv_term = jnp.concatenate([qkv_term.astype(BF16), high, low_part], axis=1)
        partial, qkv_term, out_term = lax.optimization_barrier(
            (partial, qkv_term, out_term.astype(BF16))
        )
        normed_one_grad = scatter_plane(partial.reshape(8, count, width))
        upstream = middle_grad + norm_back(stream, factor_one, attn_row, normed_one_grad)
        if groups > 1:
            qkv_term = jnp.swapaxes(
                qkv_term.reshape(planes, 2, groups, 4, bands, padded), 2, 3
            )
            out_term = jnp.swapaxes(out_term.reshape(groups, 4, bands, width), 0, 1)
        wide_terms[layer] = qkv_term.reshape(planes, 8, band_rows, padded)
        tall_terms[layer] = out_term.reshape(4, band_rows, width)

    sums = collect(wide_terms, tall_terms, planes)
    if groups > 1:
        sums = [
            lax.psum_scatter(array, "grp", scatter_dimension=array.ndim - 2, tiled=True)
            for array in sums
        ]
    wide_sums = jnp.stack(sums[:layers]).astype(F32)

    def by_heads(start, stop):
        return jnp.swapaxes(wide_sums[..., start:stop], 1, 2).reshape(layers, bands, -1)

    query_out = by_heads(0, columns)
    key_out = by_heads(columns, columns + kv)
    value_out = by_heads(columns + kv, columns + 2 * kv)
    rest = jnp.sum(wide_sums[..., columns + 2 * kv :], axis=1)
    rest = rest[..., :32] + rest[..., 32:64]
    attn_out = (
        jnp.sum(query_weight.astype(F32) * query_out, axis=-1)
        + jnp.sum(key_matrix.astype(F32) * key_out, axis=-1)
        + jnp.sum(value_matrix.astype(F32) * value_out, axis=-1)
    ) / attn_gain.astype(F32)

    def stacked(lists, i):
        return jnp.stack([lists[layer][i] for layer in range(layers)]).astype(F32)

    return (
        result,
        exchange(upstream.astype(BF16)).astype(F32)[None],
        attn_out,
        rest[..., experts_all],
        query_out,
        key_out,
        value_out,
        jnp.stack(sums[layers:]).astype(F32),
        rest[..., :experts_all],
        stacked(expert_out, 0),
        stacked(expert_out, 1),
        stacked(expert_out, 2),
    )


def solution(mesh):
    seq, fsdp = mesh.shape["seq"], mesh.shape["fsdp"]
    split = Mesh(mesh.devices.reshape(seq // 2, 2, fsdp // 4, 2, 2), AX)
    s, f = ("za", "yb"), ("grp", "xh", "co")
    token = P(f, s, None)
    dense = P(None, s + f, None)
    gain = P(None, s + f)
    wide, tall = P(None, s, f, None), P(None, s, None, f)
    return jax.shard_map(
        per_device,
        mesh=split,
        in_specs=(token, token, P(f, None), token, gain, gain, dense, dense, dense, dense, dense, wide, wide, tall),
        out_specs=(token, token, gain, gain, dense, dense, dense, dense, dense, wide, wide, tall),
        check_vma=False,
    )
```

```python
import math

import numpy as np
import jax, jax.numpy as jnp
from jax import lax
from jax.experimental import pallas as pl
from jax.experimental.pallas import tpu as pltpu
from jax.sharding import Mesh, PartitionSpec as P
MESH = pl.DeviceIdType.MESH
AX=("za","yb","grp","xh","co")

class Ring8:
    def __init__(self, na):
        self.n=2*na; self.na=na
        za=lax.axis_index("za"); yb=lax.axis_index("yb")
        self.rho = za + yb*(2*na-1-2*za)
    def pos(self, r):
        r = lax.rem(r+2*self.n, self.n)
        yb = r//self.na
        za = r + yb*(2*self.na-1-2*r)
        return za, yb
    def dev(self, r):
        za,yb=self.pos(r); return {"za":za,"yb":yb}
    def slot(self, r):
        za,yb=self.pos(r); return za*2+yb

class Ring4:
    def __init__(self):
        self.n=4
        x=lax.axis_index("xh"); b=lax.axis_index("yb"); self.c=lax.axis_index("co")
        self.rho = 2*x + (x+b-2*x*b)
    def pos(self, r):
        r = lax.rem(r+2*self.n, self.n)
        x = r//2; m=lax.rem(r,2)
        return x, m+x-2*x*m
    def dev(self, r):
        x,b=self.pos(r); return {"xh":x,"yb":b}
    def slot(self, r, sib=False):
        x,b=self.pos(r); c = (1-self.c) if sib else self.c
        return (x*2+c)*2+b
    def sib_dev(self):
        return {"co":1-self.c}

def barrier(devs):
    sem = pltpu.get_barrier_semaphore()
    for d in devs:
        pl.semaphore_signal(sem, inc=1, device_id=d, device_id_type=MESH)
    pl.semaphore_wait(sem, len(devs))

def rcopy(src, dst, ss, rs, dev):
    return pltpu.make_async_remote_copy(src_ref=src, dst_ref=dst, send_sem=ss, recv_sem=rs, device_id=dev, device_id_type=MESH)

def ag_ring(ring, K, own, out, send, recv, sib=None, beside=None):
    n=ring.n; S=n//2; T=own.shape[0]; rows=T//K; rho=ring.rho
    def chunks(d,s): return range(K) if s<S else (range(K//2) if d==0 else range(K//2,K))
    def mk(d,s,c):
        sg=1-2*d
        slot=ring.slot(rho-(s-1)*sg)
        sl=pl.ds(c*rows,rows)
        src = own.at[sl] if s==1 else out.at[slot,sl]
        return rcopy(src, out.at[slot,sl], send.at[d,s-1,c], recv.at[d,s-1,c], ring.dev(rho+sg))
    def rd(d,s,c):
        sg=1-2*d
        slot=ring.slot(rho-s*sg); sl=pl.ds(c*rows,rows)
        return rcopy(out.at[slot,sl], out.at[slot,sl], send.at[d,s-1,c], recv.at[d,s-1,c], ring.dev(rho-sg))
    started=[]
    def sibcopy(slot, slot_src, c, idx, src):
        ss,rs=sib
        cp=rcopy(src, out.at[slot,pl.ds(c*rows,rows)], ss.at[idx,c], rs.at[idx,c], ring.sib_dev())
        cp.start(); started.append(cp)
    def arrived(d,s,c):
        rd(d,s,c).wait_recv()
        if sib is not None:
            sg=1-2*d
            slot=ring.slot(rho-s*sg)
            idx = s*sg % n
            sibcopy(slot, None, c, idx, out.at[slot,pl.ds(c*rows,rows)])
    sends=[]
    for s in range(1,S+1):
        for c in range(K):
            for d in (0,1):
                if c in chunks(d,s):
                    if s>1: arrived(d,s-1,c)
                    cp=mk(d,s,c); cp.start(); sends.append(cp)
        if beside is not None: beside(s)
        if s==1 and sib is not None:
            for c in range(K): sibcopy(ring.slot(rho), None, c, 0, own.at[pl.ds(c*rows,rows)])
    for s in (S-1,S):
        for c in range(K):
            for d in (0,1):
                if s==S and c in chunks(d,S): arrived(d,S,c)
                if s==S-1 and S>1 and c not in chunks(d,S): arrived(d,S-1,c)
    if sib is not None:
        ss,rs=sib
        for idx in range(n):
            for c in range(K):
                slot=ring.slot(rho-idx, True); sl=pl.ds(c*rows,rows)
                rcopy(out.at[slot,sl],out.at[slot,sl],ss.at[idx,c],rs.at[idx,c],ring.sib_dev()).wait_recv()
    for cp in sends+started: cp.wait_send()

class RingGather:
    def __init__(self, ring, chunks, own, out, send, recv):
        self.ring, self.k, self.own, self.out, self.send, self.recv = ring, chunks, own, out, send, recv
        self.last = ring.n // 2
        self.rows = own.shape[0] // chunks

    def chunks(self, d, s):
        if s < self.last:
            return range(self.k)
        return range(self.k // 2) if d == 0 else range(self.k // 2, self.k)

    def copy(self, d, s, c):
        sign = 1 - 2 * d
        slot = self.ring.slot(self.ring.rho - (s - 1) * sign)
        part = pl.ds(c * self.rows, self.rows)
        source = self.own.at[part] if s == 1 else self.out.at[slot, part]
        return rcopy(
            source, self.out.at[slot, part], self.send.at[d, s - 1, c], self.recv.at[d, s - 1, c],
            self.ring.dev(self.ring.rho + sign),
        )

    def arrive(self, d, s, c):
        sign = 1 - 2 * d
        ref = self.out.at[self.ring.slot(self.ring.rho - s * sign), pl.ds(c * self.rows, self.rows)]
        rcopy(
            ref, ref, self.send.at[d, s - 1, c], self.recv.at[d, s - 1, c],
            self.ring.dev(self.ring.rho - sign),
        ).wait_recv()

    def step(self, s):
        for c in range(self.k):
            for d in (0, 1):
                if c in self.chunks(d, s):
                    if s > 1:
                        self.arrive(d, s - 1, c)
                    self.copy(d, s, c).start()

    def finish(self):
        for s in (self.last - 1, self.last):
            for c in range(self.k):
                for d in (0, 1):
                    if c in self.chunks(d, s) and (s == self.last or c not in self.chunks(d, s + 1)):
                        self.arrive(d, s, c)
        for s in range(1, self.last + 1):
            for c in range(self.k):
                for d in (0, 1):
                    if c in self.chunks(d, s):
                        self.copy(d, s, c).wait_send()


class RingScatter:
    def __init__(self, ring, chunks, part, buf, stage, send, recv, load):
        self.ring, self.k, self.part, self.buf, self.stage = ring, chunks, part, buf, stage
        self.send, self.recv, self.load = send, recv, load
        self.last = ring.n // 2
        self.rows = stage.shape[1] // chunks

    def chunks(self, d, s):
        if s > 1:
            return range(self.k)
        return range(self.k // 2) if d == 0 else range(self.k // 2, self.k)

    def slot(self, d, s):
        return self.ring.slot(self.ring.rho + (1 - 2 * d) * (self.last + 1 - s))

    def loading(self, d, s):
        return pltpu.make_async_copy(
            self.part.at[self.slot(d, s)], self.stage.at[d], self.load.at[d]
        )

    def copy(self, d, s, c):
        rows = pl.ds(c * self.rows, self.rows)
        if s > 1 and c in self.chunks(d, s - 1):
            source = self.buf.at[d, s - 2, rows]
        else:
            source = self.part.at[self.slot(d, s), rows]
        return rcopy(
            source, self.buf.at[d, s - 1, rows], self.send.at[d, s - 1, c],
            self.recv.at[d, s - 1, c], self.ring.dev(self.ring.rho + 1 - 2 * d),
        )

    def arrive(self, d, s, c):
        ref = self.buf.at[d, s - 1, pl.ds(c * self.rows, self.rows)]
        rcopy(
            ref, ref, self.send.at[d, s - 1, c], self.recv.at[d, s - 1, c],
            self.ring.dev(self.ring.rho - (1 - 2 * d)),
        ).wait_recv()

    def step(self, s):
        if s > 1:
            for d in (0, 1):
                self.loading(d, s).wait()
        for c in range(self.k):
            for d in (0, 1):
                if c not in self.chunks(d, s):
                    continue
                if s > 1 and c in self.chunks(d, s - 1):
                    self.arrive(d, s - 1, c)
                    rows = pl.ds(c * self.rows, self.rows)
                    self.buf[d, s - 2, rows, :] = (
                        self.buf[d, s - 2, rows, :].astype(F32)
                        + self.stage[d, rows, :].astype(F32)
                    ).astype(BF16)
                self.copy(d, s, c).start()
        for d in (0, 1):
            if s < self.last or d == 0:
                self.loading(d, s + 1).start()

    def finish(self):
        self.loading(0, self.last + 1).wait()
        for d in (0, 1):
            for c in range(self.k):
                self.arrive(d, self.last, c)
        for s in range(1, self.last + 1):
            for d in (0, 1):
                for c in self.chunks(d, s):
                    self.copy(d, s, c).wait_send()
        return (
            self.buf[0, self.last - 1].astype(F32) + self.buf[1, self.last - 1].astype(F32)
        ) + self.stage[0].astype(F32)


def rs_ring(ring, K, part, buf, send, recv, slotf, beside=None):
    n=ring.n; S=n//2; T=buf.shape[2]; rows=T//K; rho=ring.rho
    def chunks(d,s): return range(K) if s>1 else (range(K//2) if d==0 else range(K//2,K))
    sends=[]
    def rd(d,s,c):
        sl=pl.ds(c*rows,rows)
        return rcopy(buf.at[d,s-1,sl],buf.at[d,s-1,sl],send.at[d,s-1,c],recv.at[d,s-1,c],ring.dev(rho-(1-2*d)))
    for s in range(1,S+1):
        order=list(range(K))
        if s==2:
            pass
        for c in order:
            for d in (0,1):
                if c not in chunks(d,s): continue
                sg=1-2*d
                dest=rho+sg*(S+1-s)
                sl=pl.ds(c*rows,rows)
                if s>1 and c in chunks(d,s-1):
                    rd(d,s-1,c).wait_recv()
                    buf[d,s-2,sl,:] = (buf[d,s-2,sl,:].astype(jnp.float32)+part[slotf(dest),sl,:].astype(jnp.float32)).astype(buf.dtype)
                    src=buf.at[d,s-2,sl]
                else:
                    src=part.at[slotf(dest),sl]
                cp=rcopy(src,buf.at[d,s-1,sl],send.at[d,s-1,c],recv.at[d,s-1,c],ring.dev(rho+sg))
                cp.start(); sends.append(cp)
        if beside is not None: beside(s+1)
    for c in range(K):
        for d in (0,1):
            rd(d,S,c).wait_recv()
    for cp in sends: cp.wait_send()

HEAD_SIZE = 64
EPSILON = 1e-05
HIGHEST = lax.Precision.HIGHEST
F32 = jnp.float32
BF16 = jnp.bfloat16
ANY_SPEC = pl.BlockSpec(memory_space=pltpu.HBM)
GATHERED_SPEC = pl.BlockSpec(memory_space=pl.ANY)
VMEM_SPEC = pl.BlockSpec(memory_space=pltpu.VMEM)
CHUNKS = 4
DMA = pltpu.SemaphoreType.DMA


class ShareGather:
    def __init__(self, source, out, sems):
        self.source, self.out = source, out
        self.x_send, self.x_recv, self.s_send, self.s_recv, self.own, self.room = sems
        x, c = lax.axis_index("xh"), lax.axis_index("co")
        self.mine, self.across = x * 2 + c, (1 - x) * 2 + c
        self.beside, self.beside_across = x * 2 + 1 - c, (1 - x) * 2 + 1 - c
        self.chip, self.core = {"xh": 1 - x}, {"co": 1 - c}
        self.parts = source.shape[0]

    def to_chip(self, e):
        return rcopy(
            self.source.at[e], self.out.at[self.mine, e], self.x_send.at[e], self.x_recv.at[e],
            self.chip,
        )

    def to_core(self, e):
        if e == self.parts:
            source, target = self.source, self.out.at[self.mine]
        else:
            source = target = self.out.at[self.across, e]
        return rcopy(source, target, self.s_send.at[e], self.s_recv.at[e], self.core)

    def keep(self, half):
        ends = (self.source, self.room) if half == 0 else (self.room, self.out.at[self.mine])
        return pltpu.make_async_copy(*ends, self.own.at[half])

    def start(self):
        for e in range(self.parts):
            self.to_chip(e).start()
        self.to_core(self.parts).start()
        self.keep(0).start()

    def middle(self):
        self.keep(0).wait()
        self.keep(1).start()

    def end(self):
        self.forward()
        self.finish()

    def forward(self):
        for e in range(self.parts):
            ref = self.out.at[self.across, e]
            rcopy(ref, ref, self.x_send.at[e], self.x_recv.at[e], self.chip).wait_recv()
            self.to_core(e).start()

    def finish(self):
        for e in range(self.parts + 1):
            ref = self.out.at[self.beside_across, e] if e < self.parts else self.out.at[self.beside]
            rcopy(ref, ref, self.s_send.at[e], self.s_recv.at[e], self.core).wait_recv()
        for e in range(self.parts):
            self.to_chip(e).wait_send()
        for e in range(self.parts + 1):
            self.to_core(e).wait_send()
        self.keep(1).wait()


class ShareScatter:
    def __init__(self, source, out, rest):
        self.source, self.out = source, out
        (
            self.own, self.came, self.far, self.load, self.s_send, self.s_recv, self.x_send,
            self.x_recv, self.put,
        ) = rest
        x, c = lax.axis_index("xh"), lax.axis_index("co")
        self.mine = ((1 - x) * 2 + c, x * 2 + c)
        self.theirs = ((1 - x) * 2 + 1 - c, x * 2 + 1 - c)
        self.chip, self.core = {"xh": 1 - x}, {"co": 1 - c}
        self.parts = source.shape[1]

    def loading(self, k):
        return pltpu.make_async_copy(self.source.at[self.mine[k]], self.own.at[k], self.load.at[k])

    def to_core(self, k, e):
        return rcopy(
            self.source.at[self.theirs[k], e], self.came.at[k, e], self.s_send.at[k, e],
            self.s_recv.at[k, e], self.core,
        )

    def to_chip(self, e):
        return rcopy(
            self.own.at[0, e], self.far.at[e], self.x_send.at[e], self.x_recv.at[e], self.chip
        )

    def start(self):
        for k in (0, 1):
            self.loading(k).start()
            for e in range(self.parts):
                self.to_core(k, e).start()

    def middle(self):
        self.loading(0).wait()
        for e in range(self.parts):
            self.to_core(0, e).wait_recv()
            self.own[0, e] = (
                self.own[0, e].astype(F32) + self.came[0, e].astype(F32)
            ).astype(BF16)
            self.to_chip(e).start()

    def end(self):
        self.loading(1).wait()
        for e in range(self.parts):
            self.to_core(1, e).wait_recv()
            self.to_chip(e).wait_recv()
            self.own[1, e] = (
                self.own[1, e].astype(F32) + self.came[1, e].astype(F32) + self.far[e].astype(F32)
            ).astype(BF16)
        store = pltpu.make_async_copy(self.own.at[1], self.out, self.put)
        store.start()
        for e in range(self.parts):
            self.to_chip(e).wait_send()
            for k in (0, 1):
                self.to_core(k, e).wait_send()
        store.wait()


def carrier(share, source, out, rest):
    if share[1] is None:
        return ShareScatter(source, out, rest)
    return ShareGather(source.at[share[1]], out, rest)


def share_devices():
    return [{"xh": 1 - lax.axis_index("xh")}, {"co": 1 - lax.axis_index("co")}]


def share_shapes(share):
    if share is None:
        return [], [], []
    array = share[0]
    parts = array.shape[1]
    if share[1] is None:
        return (
            [array],
            [jax.ShapeDtypeStruct(array.shape[1:], BF16)],
            [
                pltpu.VMEM((2,) + array.shape[1:], BF16),
                pltpu.VMEM((2,) + array.shape[1:], BF16),
                pltpu.VMEM(array.shape[1:], BF16),
                DMA((2,)),
                DMA((2, parts)),
                DMA((2, parts)),
                DMA((parts,)),
                DMA((parts,)),
                DMA,
            ],
        )
    return (
        [array],
        [jax.ShapeDtypeStruct((4,) + array.shape[1:], BF16)],
        [
            DMA((parts,)),
            DMA((parts,)),
            DMA((parts + 1,)),
            DMA((parts + 1,)),
            DMA((2,)),
            pltpu.VMEM(array.shape[1:], BF16),
        ],
    )


def comm_params(number, megabytes=40):
    return pltpu.CompilerParams(
        collective_id=number, has_side_effects=True, vmem_limit_bytes=megabytes << 20
    )


def busy(microseconds):
    return pl.CostEstimate(flops=0, bytes_accessed=microseconds * 3_690_000, transcendentals=0)


def gather_group(rows, planes, number, share=None, beside=None):
    count, width = rows.shape
    more, outs, sems = share_shapes(share)
    extra = [] if beside is None else [beside]

    def kernel(x_ref, *refs):
        if more:
            w_ref, refs = refs[0], refs[1:]
        if extra:
            y_ref, refs = refs[0], refs[1:]
        o_ref, refs = refs[0], refs[1:]
        if more:
            b_ref, refs = refs[0], refs[1:]
        if extra:
            yo_ref, refs = refs[0], refs[1:]
        send, recv, own, *rest = refs
        if extra:
            y_send, y_recv, y_own, *rest = rest
        ring = Ring8(planes)
        devices = [ring.dev(ring.rho + 1), ring.dev(ring.rho - 1)]
        barrier(devices + share_devices() * len(more))
        local = pltpu.make_async_copy(x_ref, o_ref.at[ring.slot(ring.rho)], own)
        local.start()
        if more:
            carried = carrier(share, w_ref, b_ref, rest)
            carried.start()


        if extra:
            y_local = pltpu.make_async_copy(y_ref, yo_ref.at[ring.slot(ring.rho)], y_own)
            y_local.start()
            small = RingGather(ring, 2, y_ref, yo_ref, y_send, y_recv)

        def turn_of(turn):
            if extra:
                small.step(turn)
            if turn == 1 and more:
                carried.middle()

        ag_ring(ring, CHUNKS, x_ref, o_ref, send, recv, None, turn_of)
        if extra:
            small.finish()
            y_local.wait()
        if more:
            carried.end()
        local.wait()

    results = pl.pallas_call(
        kernel,
        out_shape=[jax.ShapeDtypeStruct((2 * planes, count, width), BF16)]
        + outs
        + [jax.ShapeDtypeStruct((2 * planes,) + array.shape, BF16) for array in extra],
        in_specs=[VMEM_SPEC] + [ANY_SPEC] * len(more) + [VMEM_SPEC] * len(extra),
        out_specs=[GATHERED_SPEC] + [ANY_SPEC] * len(more) + [VMEM_SPEC] * len(extra),
        scratch_shapes=[DMA((2, planes, CHUNKS)), DMA((2, planes, CHUNKS)), DMA]
        + [DMA((2, planes, 2)), DMA((2, planes, 2)), DMA] * len(extra)
        + sems,
        compiler_params=comm_params(number),
        cost_estimate=busy(33),
        name="gather_group",
    )(rows, *more, *extra)
    return results if more or extra else results[0]


def scatter_group(parts, planes, number, shares=()):
    _, count, width = parts.shape
    held = [share_shapes(share) for share in shares]
    more = [array for arrays, _, _ in held for array in arrays]

    def kernel(p_ref, *refs):
        w_refs, o_ref, refs = refs[: len(more)], refs[len(more)], refs[len(more) + 1 :]
        b_refs, refs = refs[: len(more)], refs[len(more) :]
        buf, send, recv, *rest = refs
        ring = Ring8(planes)
        devices = [ring.dev(ring.rho + 1), ring.dev(ring.rho - 1)]
        barrier(devices + share_devices() * (len(more) > 0))
        carried = []
        for i, share in enumerate(shares):
            some, rest = rest[: len(held[i][2])], rest[len(held[i][2]) :]
            carried.append(carrier(share, w_refs[i], b_refs[i], some))
            carried[-1].start()

        def beside(turn):
            if turn - 2 < len(carried):
                carried[turn - 2].middle()

        rs_ring(ring, CHUNKS, p_ref, buf, send, recv, ring.slot, beside)
        last = planes - 1
        o_ref[...] = (
            buf[0, last].astype(F32) + buf[1, last].astype(F32)
        ) + p_ref[ring.slot(ring.rho)].astype(F32)
        for one in carried:
            one.end()

    results = pl.pallas_call(
        kernel,
        out_shape=[jax.ShapeDtypeStruct((count, width), F32)]
        + [shape for _, shapes, _ in held for shape in shapes],
        in_specs=[VMEM_SPEC] + [ANY_SPEC] * len(more),
        out_specs=[VMEM_SPEC] + [ANY_SPEC] * len(more),
        scratch_shapes=[
            pltpu.VMEM((2, planes, count, width), BF16),
            DMA((2, planes, CHUNKS)),
            DMA((2, planes, CHUNKS)),
        ]
        + [one for _, _, scratch in held for one in scratch],
        compiler_params=comm_params(number),
        cost_estimate=busy(32),
        name="scatter_group",
    )(parts, *more)
    return results if more else results[0]


def gather_plane(rows, tall=None, swap=None, planes=None):
    count, width = rows.shape
    more, trades = tall is not None, swap is not None

    def kernel(x_ref, *refs):
        if more:
            w_ref, o_ref, t_ref, *refs = refs
            *refs, f_send, f_recv, f_own = refs
        elif trades:
            y_ref, o_ref, yo_ref, *refs = refs
            *refs, y_send, y_recv = refs
        else:
            o_ref, *refs = refs
        send, recv, sib_send, sib_recv, own = refs
        ring = Ring4()
        if more:
            barrier([peer[0] for peer in plane_peers()])
        elif trades:
            line_barrier(planes, [peer[0] for peer in plane_peers()], True)
            trade(y_ref, yo_ref, y_send, y_recv, lambda copy: copy.start())
        else:
            barrier([ring.dev(ring.rho + 1), ring.dev(ring.rho - 1), ring.sib_dev()])
        local = pltpu.make_async_copy(x_ref, o_ref.at[ring.slot(ring.rho)], own)
        local.start()
        ends = []

        def beside(turn):
            if turn == 1 and more:
                ends.append(hand_over(w_ref, t_ref, f_send, f_recv, f_own))

        ag_ring(ring, CHUNKS, x_ref, o_ref, send, recv, (sib_send, sib_recv), beside)
        local.wait()
        for end in ends:
            end()
        if trades:
            trade(y_ref, yo_ref, y_send, y_recv, lambda copy: copy.wait())

    shapes = [jax.ShapeDtypeStruct((8, count, width), BF16)]
    if more:
        shapes.append(jax.ShapeDtypeStruct(tall.shape, BF16))
    if trades:
        shapes.append(jax.ShapeDtypeStruct(swap.shape, BF16))
    results = pl.pallas_call(
        kernel,
        out_shape=shapes,
        in_specs=[VMEM_SPEC] * len(shapes),
        out_specs=[ANY_SPEC] + [VMEM_SPEC] * (len(shapes) - 1),
        scratch_shapes=[
            DMA((2, 2, CHUNKS)),
            DMA((2, 2, CHUNKS)),
            DMA((4, CHUNKS)),
            DMA((4, CHUNKS)),
            DMA,
        ]
        + [DMA((3,)), DMA((3,)), DMA] * more
        + [DMA, DMA] * trades,
        compiler_params=comm_params(10 if more else 16 if trades else 3),
        cost_estimate=busy(20),
        name="gather_plane",
    )(rows, *([tall] if more else []), *([swap] if trades else []))
    return results if more or trades else results[0]


def scatter_plane(parts, share=None):
    results = scatter_plane_call(parts, [], 1, 4 if share is None else 17, share)
    return results[0] if share is None else results


def scatter_plane_first(parts, slabs, out_weight, planes, share):
    return scatter_plane_call(parts, [out_weight, *slabs], planes, 9, share)


def scatter_plane_call(parts, beside, planes, number, share):
    _, count, width = parts.shape
    extra = len(beside)
    more, outs, sems = share_shapes(share)

    def kernel(p_ref, *refs):
        if more:
            w_ref, refs = refs[0], refs[1:]
        b_refs, o_ref, refs = refs[:extra], refs[extra], refs[extra + 1 :]
        if more:
            blocks, refs = refs[0], refs[1:]
        if extra:
            stores, refs = refs[:extra], refs[extra:]
        pair, buf, send, recv, sib_send, sib_recv, refs = *refs[:6], refs[6:]
        ring = Ring4()
        if extra:
            put, z_send, z_recv, *refs = refs
            line_barrier(planes, [peer[0] for peer in plane_peers()])
            if more:
                carried = carrier(share, w_ref, blocks, refs)
                carried.start()
            za = lax.axis_index("za")
            puts = [
                pltpu.make_async_copy(b_refs[i], stores[i].at[za], put.at[i]) for i in range(extra)
            ]
            for copy in puts:
                copy.start()
            line = LineGather(planes, stores, z_send, z_recv)
        else:
            barrier([ring.dev(ring.rho + 1), ring.dev(ring.rho - 1), ring.sib_dev()])

        def chip(r):
            x, b = ring.pos(r)
            return x * 2 + b

        copies = []
        for i in (2, 1, 3, 0):
            copy = rcopy(
                p_ref.at[ring.slot(ring.rho + i, True)],
                pair.at[chip(ring.rho + i)],
                sib_send.at[i],
                sib_recv.at[i],
                ring.sib_dev(),
            )
            copy.start()
            copies.append(copy)
        if more and not extra:
            carried = carrier(share, w_ref, blocks, refs)
            carried.start()
        if extra:
            for copy in puts:
                copy.wait()
            line.step(1)
        for i, copy in zip((2, 1, 3, 0), copies):
            place = chip(ring.rho + i)
            copy.wait_recv()
            pair[place] = (
                pair[place].astype(F32) + p_ref[ring.slot(ring.rho + i)].astype(F32)
            ).astype(BF16)
        if more and extra:
            carried.middle()

        def beside(turn):
            if extra:
                line.step(turn)
            elif more and turn == 2:
                carried.middle()

        rs_ring(ring, CHUNKS, pair, buf, send, recv, chip, beside)
        o_ref[...] = (
            buf[0, 1].astype(F32) + buf[1, 1].astype(F32)
        ) + pair[chip(ring.rho)].astype(F32)
        for copy in copies:
            copy.wait_send()
        if extra:
            for turn in range(4, planes):
                line.step(turn)
            line.finish()
        if more:
            carried.end()

    shapes, scratch = [], []
    if extra:
        shapes = [
            jax.ShapeDtypeStruct((planes,) + array.shape, BF16) for array in beside
        ]
        scratch = [
            DMA((extra,)),
            DMA((extra, 2, planes - 1)),
            DMA((extra, 2, planes - 1)),
        ]
    return pl.pallas_call(
        kernel,
        out_shape=[jax.ShapeDtypeStruct((count, width), F32)] + outs + shapes,
        in_specs=[VMEM_SPEC] + [ANY_SPEC] * len(more) + [VMEM_SPEC] * extra,
        out_specs=[VMEM_SPEC] + [ANY_SPEC] * len(more) + [VMEM_SPEC] * len(shapes),
        scratch_shapes=[
            pltpu.VMEM((4, count, width), BF16),
            pltpu.VMEM((2, 2, count, width), BF16),
            DMA((2, 2, CHUNKS)),
            DMA((2, 2, CHUNKS)),
            DMA((4,)),
            DMA((4,)),
        ]
        + scratch
        + sems,
        compiler_params=comm_params(number),
        cost_estimate=busy(20),
        name="scatter_plane_first" if extra else "scatter_plane",
    )(parts, *more, *beside)


def plane_peers():
    x, c, b = lax.axis_index("xh"), lax.axis_index("co"), lax.axis_index("yb")
    peers = []
    for k in range(1, 8):
        px = x + (k // 4) * (1 - 2 * x)
        pc = c + (k // 2 % 2) * (1 - 2 * c)
        pb = b + (k % 2) * (1 - 2 * b)
        peers.append(
            ({"xh": px, "co": pc, "yb": pb}, (px * 2 + pc) * 2 + pb, pb * 4 + px * 2 + pc)
        )
    return peers


def own_places():
    x, c, b = lax.axis_index("xh"), lax.axis_index("co"), lax.axis_index("yb")
    return (x * 2 + c) * 2 + b, b * 4 + x * 2 + c


def trade(source, target, send, recv, act):
    za = lax.axis_index("za")
    f = lax.axis_index("xh") * 2 + lax.axis_index("co")

    @pl.when(za != f)
    def _():
        act(rcopy(source, target, send, recv, swap_partner()))

    @pl.when(za == f)
    def _():
        act(pltpu.make_async_copy(source, target, send))


def swap_partner():
    za = lax.axis_index("za")
    f = lax.axis_index("xh") * 2 + lax.axis_index("co")
    return {"za": f, "xh": za // 2, "co": lax.rem(za, 2)}


def line_barrier(planes, devices, swaps=False):
    za = lax.axis_index("za")
    f = lax.axis_index("xh") * 2 + lax.axis_index("co")
    sem = pltpu.get_barrier_semaphore()
    for device in devices:
        pl.semaphore_signal(sem, inc=1, device_id=device, device_id_type=MESH)

    @pl.when(za > 0)
    def _():
        pl.semaphore_signal(sem, inc=1, device_id={"za": za - 1}, device_id_type=MESH)

    @pl.when(za < planes - 1)
    def _():
        pl.semaphore_signal(sem, inc=1, device_id={"za": za + 1}, device_id_type=MESH)

    below, above = (za + planes - 1) // planes, (2 * planes - 2 - za) // planes
    apart = 0
    if swaps:

        @pl.when(za != f)
        def _():
            pl.semaphore_signal(sem, inc=1, device_id=swap_partner(), device_id_type=MESH)

        apart = ((za - f) * (za - f) + 8) // 9
    pl.semaphore_wait(sem, len(devices) + below + above + apart)


class LineGather:
    def __init__(self, planes, stores, send, recv):
        self.planes, self.stores, self.send, self.recv = planes, stores, send, recv
        self.za = lax.axis_index("za")

    def copy(self, i, d, s):
        sign = 1 - 2 * d
        block = self.za - (s - 1) * sign
        return rcopy(
            self.stores[i].at[block],
            self.stores[i].at[block],
            self.send.at[i, d, s - 1],
            self.recv.at[i, d, s - 1],
            {"za": self.za + sign},
        )

    def sends(self, d, s):
        za, last = self.za, self.planes - 1
        if d == 0:
            return (za < last) & (za >= s - 1)
        return (za > 0) & (za <= last - (s - 1))

    def step(self, s):
        for i in range(len(self.stores)):
            for d in (0, 1):
                if s > 1:
                    self.wait_arrival(i, d, s - 1)

                @pl.when(self.sends(d, s))
                def _():
                    self.copy(i, d, s).start()

    def wait_arrival(self, i, d, s):
        za, last, sign = self.za, self.planes - 1, 1 - 2 * d
        has = (za >= s) if d == 0 else (za <= last - s)

        @pl.when(has)
        def _():
            block = za - s * sign
            ref = self.stores[i].at[block]
            rcopy(
                ref, ref, self.send.at[i, d, s - 1], self.recv.at[i, d, s - 1],
                {"za": za - sign},
            ).wait_recv()

    def finish(self):
        for i in range(len(self.stores)):
            for d in (0, 1):
                self.wait_arrival(i, d, self.planes - 1)
        self.finish_sends()

    def finish_sends(self):
        for i in range(len(self.stores)):
            for d in (0, 1):
                for s in range(1, self.planes):

                    @pl.when(self.sends(d, s))
                    def _():
                        self.copy(i, d, s).wait_send()


def flat_peers():
    x, c = lax.axis_index("xh"), lax.axis_index("co")
    peers = []
    for k in (1, 2, 3):
        px = x + (k // 2) * (1 - 2 * x)
        pc = c + (k % 2) * (1 - 2 * c)
        peers.append(({"xh": px, "co": pc}, px * 2 + pc))
    return peers, x * 2 + c


def hand_over(stage, target, send, recv, own):
    peers, mine = flat_peers()
    copies = []
    for k, (device, f) in enumerate(peers):
        copies.append(rcopy(stage.at[f], target.at[mine], send.at[k], recv.at[k], device))
        copies[-1].start()
    keep = pltpu.make_async_copy(stage.at[mine], target.at[mine], own)
    keep.start()
    return lambda: hand_over_end(peers, target, send, recv, keep, copies)


def hand_over_end(peers, target, send, recv, keep, copies):
    keep.wait()
    for k, (device, f) in enumerate(peers):
        ref = target.at[f]
        rcopy(ref, ref, send.at[k], recv.at[k], device).wait_recv()
    for copy in copies:
        copy.wait_send()


def enter(tokens, heads_part, other_part, out_weight, others, gain_lane, planes, share):
    count, width = tokens.shape
    more, outs, sems = share_shapes(share)
    also = len(others)
    layers, rows = heads_part.shape[1:3]
    extra = layers - 1

    def kernel(x_ref, a_ref, b_ref, w_ref, *refs):
        y_refs, refs = refs[:also], refs[also:]
        if more:
            s_ref, refs = refs[0], refs[1:]
        o_ref, stream_ref, t_ref, a_out, b_out, refs = *refs[:5], refs[5:]
        a_late, b_late, refs = refs[:extra], refs[extra : 2 * extra], refs[2 * extra :]
        y_outs, refs = refs[:also], refs[also:]
        if more:
            blocks, refs = refs[0], refs[1:]
        (
            stage, normed, swap_send, swap_recv, send, recv, own, ring_send, ring_recv, sib_send,
            sib_recv, put, za_send, za_recv, f_send, f_recv, *rest
        ) = refs
        za = lax.axis_index("za")
        x, c = lax.axis_index("xh"), lax.axis_index("co")
        f = x * 2 + c
        partner = swap_partner()
        ring = Ring4()
        peers = plane_peers()
        group, place = own_places()
        line_barrier(planes, [peer[0] for peer in peers], True)

        trades = [(x_ref, stream_ref), *zip(y_refs, y_outs)]

        def trade(i, act):
            source, target = trades[i]

            @pl.when(za != f)
            def _():
                act(rcopy(source, target, swap_send.at[i], swap_recv.at[i], partner))

            @pl.when(za == f)
            def _():
                act(pltpu.make_async_copy(source, target, swap_send.at[i]))

        trade(0, lambda copy: copy.start())

        copies = []

        def target(kind, layer, at):
            if layer == 0:
                return (a_out, b_out)[kind].at[za, at]
            return (a_late, b_late)[kind][layer - 1].at[at]

        def scatter(kind, layer):
            source = (a_ref, b_ref)[kind]
            for k, (device, their_group, _) in enumerate(peers):
                copy = rcopy(
                    source.at[their_group, layer], target(kind, layer, place),
                    send.at[kind, layer, k], recv.at[kind, layer, k], device,
                )
                copy.start()
                copies.append(copy)
            local = pltpu.make_async_copy(
                source.at[group, layer], target(kind, layer, place), own.at[kind * layers + layer]
            )
            local.start()
            return local

        def arrivals(kind, layer, local):
            for k, (device, _, their_place) in enumerate(peers):
                ref = target(kind, layer, their_place)
                rcopy(
                    ref, ref, send.at[kind, layer, k], recv.at[kind, layer, k], device
                ).wait_recv()
            local.wait()

        w_put = pltpu.make_async_copy(w_ref, stage.at[za], put)
        w_put.start()
        b_local = scatter(1, 0)
        a_local = scatter(0, 0)
        if more:
            carried = carrier(share, s_ref, blocks, rest)
            carried.start()
        tall = LineGather(planes, [stage], za_send.at[pl.ds(2, 1)], za_recv.at[pl.ds(2, 1)])
        small = LineGather(planes, [b_out], za_send.at[pl.ds(0, 1)], za_recv.at[pl.ds(0, 1)])
        line = LineGather(planes, [a_out], za_send.at[pl.ds(1, 1)], za_recv.at[pl.ds(1, 1)])
        arrivals(1, 0, b_local)
        for turn in range(1, planes):
            small.step(turn)
        w_put.wait()
        tall.step(1)
        arrivals(0, 0, a_local)
        line.step(1)
        for d in (0, 1):
            small.wait_arrival(0, d, planes - 1)
        if more:
            carried.middle()
        columns = b_out[...].reshape(width, 128).astype(F32)
        gain = columns.T[gain_lane : gain_lane + 1, :]

        trade(0, lambda copy: copy.wait())
        for i in range(1, 1 + also):
            trade(i, lambda copy: copy.start())
        stream = stream_ref[...].astype(F32)
        factor = lax.rsqrt(jnp.mean(stream * stream, axis=1, keepdims=True) + EPSILON)
        normed[...] = (stream * factor * gain).astype(BF16)
        local = pltpu.make_async_copy(normed, o_ref.at[ring.slot(ring.rho)], own.at[2 * layers])
        local.start()
        ends = []

        def beside(turn):
            if turn <= 2:
                tall.step(turn + 1)
                line.step(turn + 1)
            if turn == 2:
                for layer in range(1, layers):
                    for kind in (1, 0):
                        ends.append((kind, layer, scatter(kind, layer)))

        ag_ring(ring, CHUNKS, normed, o_ref, ring_send, ring_recv, (sib_send, sib_recv), beside)
        for turn in range(4, planes):
            tall.step(turn)
            line.step(turn)
        tall.finish()
        handed = hand_over(stage, t_ref, f_send, f_recv, own.at[2 * layers + 1])
        local.wait()
        line.finish()
        small.finish_sends()
        for kind, layer, local in ends:
            arrivals(kind, layer, local)
        for copy in copies:
            copy.wait_send()
        handed()
        for i in range(1, 1 + also):
            trade(i, lambda copy: copy.wait())
        if more:
            carried.end()

    late = [
        jax.ShapeDtypeStruct((8, rows, part.shape[-1]), BF16)
        for part in (heads_part, other_part)
        for _ in range(extra)
    ]
    results = pl.pallas_call(
        kernel,
        out_shape=[
            jax.ShapeDtypeStruct((8, count, width), BF16),
            jax.ShapeDtypeStruct((count, width), BF16),
            jax.ShapeDtypeStruct((4,) + out_weight.shape, BF16),
            jax.ShapeDtypeStruct((planes, 8, rows, heads_part.shape[-1]), BF16),
            jax.ShapeDtypeStruct((planes, 8, rows, other_part.shape[-1]), BF16),
        ]
        + late
        + [jax.ShapeDtypeStruct(array.shape, array.dtype) for array in others]
        + outs,
        in_specs=[VMEM_SPEC] * (4 + also) + [ANY_SPEC] * len(more),
        out_specs=[GATHERED_SPEC] + [VMEM_SPEC] * (4 + len(late) + also) + [ANY_SPEC] * len(more),
        scratch_shapes=[
            pltpu.VMEM((planes,) + out_weight.shape, BF16),
            pltpu.VMEM((count, width), BF16),
            DMA((1 + also,)),
            DMA((1 + also,)),
            DMA((2, layers, 7)),
            DMA((2, layers, 7)),
            DMA((2 * layers + 2,)),
            DMA((2, 2, CHUNKS)),
            DMA((2, 2, CHUNKS)),
            DMA((4, CHUNKS)),
            DMA((4, CHUNKS)),
            DMA,
            DMA((3, 2, planes - 1)),
            DMA((3, 2, planes - 1)),
            DMA((3,)),
            DMA((3,)),
        ]
        + sems,
        compiler_params=comm_params(5),
        cost_estimate=busy(40),
        name="enter",
    )(tokens, heads_part, other_part, out_weight, *others, *more)
    first, rest = results[:5], results[5:]
    late_heads, late_others, rest = rest[:extra], rest[extra : 2 * extra], rest[2 * extra :]
    return first, late_heads, late_others, rest[:also], rest[also:]


def collect(wide, tall, planes, shares=(), weights=None, tokens=None):
    layers = len(wide)
    count, width = wide[0].shape[2:]
    depth = tall[0].shape[2]
    held = [share_shapes(share) for share in shares]
    more = [array for arrays, _, _ in held for array in arrays]
    more_outs = [shape for _, shapes, _ in held for shape in shapes]
    last_stage = weights is not None
    sizes = [array.shape[2] for array in weights] if last_stage else []

    def kernel(*refs):
        w_in, refs = refs[:layers], refs[layers:]
        t_in, refs = refs[:layers], refs[layers:]
        own_refs, refs = refs[: len(sizes)], refs[len(sizes) :]
        if last_stage:
            x_ref, refs = refs[0], refs[1:]
        g_in, refs = refs[: len(more)], refs[len(more) :]
        f_out, refs = refs[: 2 + len(sizes)], refs[(2 + len(sizes)) * last_stage :]
        if last_stage:
            y_ref, refs = refs[0], refs[1:]
            g_out, refs = refs[: len(more)], refs[len(more) :]
        w_out, refs = refs[:layers], refs[layers:]
        t_out, refs = refs[:layers], refs[layers:]
        if not last_stage:
            g_out, refs = refs[: len(more)], refs[len(more) :]
        w_up, t_own, t_up, summed, own, f_send, f_recv, z_send, z_recv, p_send, p_recv, *rest = refs
        za = lax.axis_index("za")
        x, c = lax.axis_index("xh"), lax.axis_index("co")
        mine = x * 2 + c
        peers = plane_peers()
        f = x * 2 + c
        line_barrier(planes, [peer[0] for peer in peers], last_stage)
        group, place = own_places()
        if last_stage:
            swap_send, swap_recv, *rest = rest

        def trade(act):
            @pl.when(za != f)
            def _():
                act(rcopy(x_ref, y_ref, swap_send, swap_recv, swap_partner()))

            @pl.when(za == f)
            def _():
                act(pltpu.make_async_copy(x_ref, y_ref, swap_send))

        if last_stage:
            trade(lambda copy: copy.start())
        carried = []
        for i, share in enumerate(shares):
            some, rest = rest[: len(held[i][2])], rest[len(held[i][2]) :]
            carried.append(carrier(share, g_in[i], g_out[i], some))
            carried[-1].start()
        firsts, keeps = [], []
        for l in range(layers):
            for k in (1, 2, 3):
                px = x + (k // 2) * (1 - 2 * x)
                pc = c + (k % 2) * (1 - 2 * c)
                copy = rcopy(
                    t_in[l].at[px * 2 + pc], t_own.at[l, mine], f_send.at[l, k - 1],
                    f_recv.at[l, k - 1], {"xh": px, "co": pc},
                )
                copy.start()
                firsts.append(copy)
            keep = pltpu.make_async_copy(t_in[l].at[mine], t_own.at[l, mine], own.at[l])
            keep.start()
            keeps.append(keep)

        def arrive(l):
            for k in (1, 2, 3):
                px = x + (k // 2) * (1 - 2 * x)
                pc = c + (k % 2) * (1 - 2 * c)
                ref = t_own.at[l, px * 2 + pc]
                rcopy(
                    ref, ref, f_send.at[l, k - 1], f_recv.at[l, k - 1], {"xh": px, "co": pc}
                ).wait_recv()
            keeps[l].wait()

        def parts(l, kind):
            if kind == 0:
                return w_in[l], w_up.at[l]
            return t_own.at[l], t_up.at[l]

        def along(l, kind, d, dest):
            _, came = parts(l, kind)
            ref = came.at[d, dest]
            return ref, rcopy(
                ref, ref, z_send.at[l, kind, d, dest], z_recv.at[l, kind, d, dest],
                {"za": za + (1 - 2 * d)},
            )

        last = planes - 1
        def pass_on(l, kind, d, dest):
            held, came = parts(l, kind)
            sends = (za < dest) if d == 0 else (za > dest)
            inner = (za > 0) if d == 0 else (za < last)
            ref, copy = along(l, kind, d, dest)

            @pl.when(sends & inner)
            def _():
                copy.wait_recv()
                came[d, dest] = (
                    came[d, dest].astype(F32) + held[dest].astype(F32)
                ).astype(BF16)
                copy.start()

            @pl.when(sends & jnp.logical_not(inner))
            def _():
                rcopy(
                    held.at[dest], ref, z_send.at[l, kind, d, dest],
                    z_recv.at[l, kind, d, dest], {"za": za + (1 - 2 * d)},
                ).start()

        for far in range(last):
            for kind in (0, 1):
                if kind == 1 and far == 0:
                    for l in range(layers):
                        arrive(l)
                for l in reversed(range(layers)):
                    for d in (0, 1):
                        pass_on(l, kind, d, last - far if d == 0 else far)
            if far < len(carried):
                carried[far].middle()

        def total(l, kind, result):
            _, came = parts(l, kind)
            for d in (0, 1):

                @pl.when((za > 0) if d == 0 else (za < last))
                def _():
                    ref = came.at[d, za]
                    rcopy(
                        ref, ref, z_send.at[l, kind, d, za], z_recv.at[l, kind, d, za],
                        {"za": za - (1 - 2 * d)},
                    ).wait_recv()
                    result[...] = (result[...].astype(F32) + came[d, za].astype(F32)).astype(BF16)

        def finish_layer(l):
            heads = [w_out[l][h].astype(F32) for h in range(8)]
            start, product = 0, jnp.zeros((count, 1), F32)
            for i, size in enumerate(sizes):
                stop = start + size // 8
                made = jnp.concatenate([head[:, start:stop] for head in heads], axis=1)
                f_out[i][l] = made
                product = product + jnp.sum(own_refs[i][l].astype(F32) * made, axis=1, keepdims=True)
                start = stop
            f_out[len(sizes)][l] = t_out[l][...].astype(F32)
            rest = sum(heads[1:], heads[0])[:, width - 128 :]
            rest = pltpu.roll(rest, 64, 1) + pltpu.roll(rest, 32, 1)
            lanes = lax.broadcasted_iota(jnp.int32, rest.shape, 1)
            f_out[len(sizes) + 1][l] = jnp.where(lanes == 32, product, rest)

        outs = []
        for l in reversed(range(layers)):
            summed[l] = w_in[l][za]
            total(l, 0, summed.at[l])
            for k, (device, _, their_place) in enumerate(peers):
                copy = rcopy(
                    summed.at[l, their_place], w_out[l].at[group], p_send.at[l, k],
                    p_recv.at[l, k], device,
                )
                copy.start()
                outs.append(copy)
            w_out[l][group] = summed[l, place]
        for l in reversed(range(layers)):
            t_out[l][...] = t_own[l, za]
            total(l, 1, t_out[l])
        for l in reversed(range(layers)):
            for k, (device, their_group, _) in enumerate(peers):
                ref = w_out[l].at[their_group]
                rcopy(ref, ref, p_send.at[l, k], p_recv.at[l, k], device).wait_recv()
        for copy in firsts + outs:
            copy.wait_send()
        for kind in (0, 1):
            for l in range(layers):
                for d in (0, 1):
                    for far in range(last):
                        dest = last - far if d == 0 else far

                        @pl.when((za < dest) if d == 0 else (za > dest))
                        def _():
                            along(l, kind, d, dest)[1].wait_send()

        if last_stage:
            trade(lambda copy: copy.wait())
            for l in range(layers):
                finish_layer(l)
        for one in carried:
            one.end()

    final_outs, plain_outs, plain_scratch = [], [], []
    sums = [((8, count, width), BF16)] * layers + [((count, depth), BF16)] * layers
    if last_stage:
        final_outs = [
            jax.ShapeDtypeStruct((layers, count, size), F32) for size in [*sizes, depth, 128]
        ] + [jax.ShapeDtypeStruct(tokens.shape, BF16)]
        plain_scratch = [pltpu.VMEM(*one) for one in sums]
    else:
        plain_outs = [jax.ShapeDtypeStruct(*one) for one in sums]
    return pl.pallas_call(
        kernel,
        out_shape=final_outs + plain_outs + more_outs,
        in_specs=[VMEM_SPEC] * (2 * layers + len(sizes) + last_stage) + [ANY_SPEC] * len(more),
        out_specs=[VMEM_SPEC] * len(final_outs + plain_outs) + [ANY_SPEC] * len(more),
        scratch_shapes=plain_scratch
        + [
            pltpu.VMEM((layers, 2, planes, 8, count, width), BF16),
            pltpu.VMEM((layers, 4, count, depth), BF16),
            pltpu.VMEM((layers, 2, planes, count, depth), BF16),
            pltpu.VMEM((layers, 8, count, width), BF16),
            DMA((layers,)),
            DMA((layers, 3)),
            DMA((layers, 3)),
            DMA((layers, 2, 2, planes)),
            DMA((layers, 2, 2, planes)),
            DMA((layers, 7)),
            DMA((layers, 7)),
        ]
        + [DMA, DMA] * last_stage
        + [one for _, _, scratch in held for one in scratch],
        compiler_params=comm_params(7, 58),
        cost_estimate=busy(40),
        name="collect",
    )(*wide, *tall, *(weights or []), *([tokens] if last_stage else []), *more)


def row_codes(code_rows, first, local, slots, weights=None):
    blocks = []
    for e in range(local):
        code = code_rows(first + e)
        ids = lax.broadcasted_iota(jnp.int32, (slots, code.shape[1]), 0).astype(F32)
        value = 1.0 if weights is None else weights(first + e)
        blocks.append(jnp.where(ids == code, value, 0.0))
    return jnp.concatenate(blocks, axis=0).astype(BF16)


def column_codes(code, first, local, slots, weights=None):
    lanes = lax.broadcasted_iota(jnp.int32, code.shape, 1)
    blocks = []
    for e in range(local):
        chosen = lanes == first + e
        column = jnp.sum(jnp.where(chosen, code, 0.0), axis=1, keepdims=True)
        ids = lax.broadcasted_iota(jnp.int32, (code.shape[0], slots), 1).astype(F32)
        value = 1.0
        if weights is not None:
            value = jnp.sum(jnp.where(chosen, weights, 0.0), axis=1, keepdims=True)
        blocks.append(jnp.where(ids == column, value, 0.0))
    return jnp.concatenate(blocks, axis=1).astype(BF16)


def dot(a, b):
    return jnp.dot(a, b, preferred_element_type=F32)


def dot_t(a, b):
    return lax.dot_general(a, b, (((1,), (1,)), ((), ())), preferred_element_type=F32)


def plain_params(megabytes, number=None):
    return pltpu.CompilerParams(
        vmem_limit_bytes=megabytes << 20,
        dimension_semantics=("arbitrary",),
        collective_id=number,
        has_side_effects=number is not None,
    )


def once(shape):
    return pl.BlockSpec(shape, lambda e: (0,) * len(shape), pipeline_mode=pl.Buffered(1))


def per_expert(shape):
    return pl.BlockSpec((1,) + shape, lambda e: (e,) + (0,) * len(shape))


def shares_of_expert(shape):
    return pl.BlockSpec((shape[0], 1) + shape[2:], lambda e: (0, e, 0, 0))


def side_by_side(ref):
    return jnp.concatenate([ref[i, 0] for i in range(ref.shape[0])], axis=1)


def experts_forward(normed, codes, router, gate_w, up_w, down_w, beside, slots, planes, number, share=None):
    blocks, count, width = normed.shape
    _, local, _, hidden_size = gate_w.shape
    more, extra_outs, sems = share_shapes(share)
    lines = local * slots
    halves = 2
    span = blocks // halves

    def kernel(
        n_ref, c_ref, r_ref, gw_ref, uw_ref, dw_ref, x_ref, *refs
    ):
        if more:
            s_ref, refs = refs[0], refs[1:]
        out, g_out, u_out, p_out, pt_out, b_out, *refs = refs
        if more:
            carried = carrier(share, s_ref, refs[0], refs[7:])
            refs = refs[1:]
        rows, back, codes_t, send, recv, own = refs[:6]
        e = pl.program_id(0)
        ring = Ring8(planes)
        gather = RingGather(ring, 2, x_ref, b_out, send, recv)
        keep = pltpu.make_async_copy(x_ref, b_out.at[ring.slot(ring.rho)], own)
        first = (lax.axis_index("za") * 2 + lax.axis_index("yb")) * local

        @pl.when(e == 0)
        def _():
            devices = [ring.dev(ring.rho + 1), ring.dev(ring.rho - 1)]
            barrier(devices + share_devices() * len(more))
            keep.start()
            gather.step(1)
            if more:
                carried.start()

            @pl.loop(0, blocks)
            def _(b):
                tokens = n_ref[b]
                logits = pltpu.roll(dot(tokens, r_ref[...]), 128 - HEAD_SIZE, 1)
                code = c_ref[b].astype(F32)
                codes_t[...] = code.T
                routed = code >= 0.0
                highest = jnp.max(jnp.where(routed, logits, -1e30), axis=1, keepdims=True)
                raised = jnp.where(routed, jnp.exp(logits - highest), 0.0)
                probs = raised / jnp.sum(raised, axis=1, keepdims=True)
                p_out[b] = probs
                pt_out[b] = probs.T[: pt_out.shape[1]]
                back[b] = column_codes(code, first, local, slots, probs)
                ones = row_codes(lambda i: codes_t[pl.ds(i, 1), :], first, local, slots)
                rows[b] = dot(ones, tokens).astype(BF16)

            gather.step(2)
            if more:
                carried.middle()

        mine = pl.ds(pl.multiple_of(e * slots, slots), slots)
        for h in range(halves):
            part = pl.ds(h * span, span)
            held = rows[part, mine, :].reshape(span * slots, width)
            gate = dot(held, gw_ref[:, 0].reshape(width, hidden_size))
            up = dot(held, uw_ref[:, 0].reshape(width, hidden_size))
            at = pl.ds(h * span * slots, span * slots)
            g_out[0, at, :] = gate
            u_out[0, at, :] = up
            hidden = (gate * jax.nn.sigmoid(gate) * up).astype(BF16)
            made = dot(hidden, side_by_side(dw_ref)).astype(BF16)
            rows[part, mine, :] = made.reshape(span, slots, width)

        for turn in range(3, planes + 1):

            @pl.when(e == min(turn - 3, local - 1))
            def _():
                gather.step(turn)

        @pl.when(e == local - 1)
        def _():
            @pl.loop(0, blocks)
            def _(b):
                out[b] = dot(back[b], rows[b]).astype(BF16)

            gather.finish()
            keep.wait()
            if more:
                carried.end()

    wide = (local, blocks * slots, hidden_size)
    return pl.pallas_call(
        kernel,
        grid=(local,),
        out_shape=[
            jax.ShapeDtypeStruct(normed.shape, BF16),
            jax.ShapeDtypeStruct(wide, F32),
            jax.ShapeDtypeStruct(wide, F32),
            jax.ShapeDtypeStruct(codes.shape, F32),
            jax.ShapeDtypeStruct((blocks, 32, count), F32),
            jax.ShapeDtypeStruct((blocks,) + beside.shape, BF16),
        ]
        + extra_outs,
        in_specs=[
            once(normed.shape),
            once(codes.shape),
            once(router.shape),
            shares_of_expert(gate_w.shape),
            shares_of_expert(up_w.shape),
            shares_of_expert(down_w.shape),
            ANY_SPEC,
        ]
        + [ANY_SPEC] * len(more),
        out_specs=[
            once(normed.shape),
            per_expert(wide[1:]),
            per_expert(wide[1:]),
            once(codes.shape),
            once((blocks, 32, count)),
            ANY_SPEC,
        ]
        + [ANY_SPEC] * len(more),
        scratch_shapes=[
            pltpu.VMEM((blocks, lines, width), BF16),
            pltpu.VMEM((blocks, count, lines), BF16),
            pltpu.VMEM((codes.shape[2], count), F32),
            DMA((2, planes, 2)),
            DMA((2, planes, 2)),
            DMA,
        ]
        + sems,
        compiler_params=plain_params(56, number),
        cost_estimate=busy(16),
        name="experts_forward",
    )(normed, codes, router, gate_w, up_w, down_w, beside, *more)


def experts_backward(
    normed, arrived, codes, probs_t, gate_w, up_w, down_w, gate_part, up_part, slots, shares,
    late=None, planes=None,
):
    blocks, count, width = normed.shape
    pieces = len(arrived)
    more = [] if late is None else [late]
    _, local, _, hidden_size = gate_w.shape
    lines = local * slots
    total = blocks * slots
    band = width // shares
    split = band % 128 == 0

    def kernel(
        n_ref, c_ref, pt_ref, gw_ref, uw_ref, dw_ref, g_ref, u_ref, *refs
    ):
        a_refs, refs = refs[:pieces], refs[pieces:]
        if more:
            l_ref, refs = refs[0], refs[1:]
        out, dg_out, du_out, dd_out, *refs = refs
        if more:
            l_out, refs = refs[0], refs[1:]
        rows, outs, back, marks, codes_t, *refs = refs
        if more:
            ring = Ring8(planes)
            scatter = RingScatter(ring, 2, l_ref, *refs)
        e = pl.program_id(0)
        first = (lax.axis_index("za") * 2 + lax.axis_index("yb")) * local

        @pl.when(e == 0)
        def _():
            if more:
                barrier([ring.dev(ring.rho + 1), ring.dev(ring.rho - 1)])
                scatter.step(1)

            @pl.loop(0, blocks)
            def _(b):
                codes_t[...] = c_ref[b].astype(F32).T

                def code(i):
                    return codes_t[pl.ds(i, 1), :]

                def prob(i):
                    return pt_ref[b, pl.ds(i, 1), :]

                back[b] = column_codes(c_ref[b].astype(F32), first, local, slots)
                rows[b] = dot(row_codes(code, first, local, slots), n_ref[b]).astype(BF16)
                upstream = jnp.concatenate([ref[b] for ref in a_refs], axis=0)
                outs[b] = dot(row_codes(code, first, local, slots, prob), upstream).astype(BF16)

            if more:
                scatter.step(2)

        mine = pl.ds(pl.multiple_of(e * slots, slots), slots)
        upstream = outs[:, mine, :].reshape(total, width)
        hidden_grad = dot_t(upstream, side_by_side(dw_ref))
        gate, up = g_ref[0], u_ref[0]
        logistic = jax.nn.sigmoid(gate)
        hidden = (gate * logistic * up).astype(BF16)
        gate_low = (hidden_grad * up * logistic * (1.0 + gate * (1.0 - logistic))).astype(BF16)
        up_low = (hidden_grad * gate * logistic).astype(BF16)
        weighted = jnp.sum(hidden.astype(F32) * hidden_grad, axis=1, keepdims=True)
        high = weighted.astype(BF16).astype(F32)
        lanes = lax.broadcasted_iota(jnp.int32, (total, 128), 1)
        mark = jnp.where(lanes == first + e, high, 0.0)
        mark = mark + jnp.where(lanes == first + e + 64, weighted - high, 0.0)
        marks[:, mine, :] = mark.astype(BF16).reshape(blocks, slots, 128)
        turned = rows[:, mine, :].reshape(total, width).T
        for f in range(shares):
            cut = turned[f * band : (f + 1) * band]
            dg_out[f, 0] = dot(cut, gate_low).astype(BF16)
            du_out[f, 0] = dot(cut, up_low).astype(BF16)
        down = dot(hidden.T, upstream).astype(BF16)
        if split:
            for f in range(shares):
                dd_out[f, 0] = down[:, f * band : (f + 1) * band]
        else:
            dd_out[0] = down
        back_rows = dot_t(gate_low, gw_ref[:, 0].reshape(width, hidden_size))
        back_rows = back_rows + dot_t(up_low, uw_ref[:, 0].reshape(width, hidden_size))
        rows[:, mine, :] = back_rows.astype(BF16).reshape(blocks, slots, width)

        if more:
            for turn in range(3, planes + 1):

                @pl.when(e == min(turn - 3, local - 1))
                def _():
                    scatter.step(turn)

        @pl.when(e == local - 1)
        def _():
            if more:
                l_out[...] = scatter.finish()

            @pl.loop(0, blocks)
            def _(b):
                out[b, :, :width] = dot(back[b], rows[b]).astype(BF16)
                out[b, :, width:] = dot(back[b], marks[b]).astype(BF16)

    cut_shape = (shares, local, band, hidden_size)
    cut_spec = pl.BlockSpec((shares, 1, band, hidden_size), lambda e: (0, e, 0, 0))
    if split:
        down_shape = (shares, local, hidden_size, band)
        down_spec = pl.BlockSpec((shares, 1, hidden_size, band), lambda e: (0, e, 0, 0))
    else:
        down_shape = (local, hidden_size, width)
        down_spec = per_expert(down_shape[1:])
    late_scratch = []
    if more:
        late_scratch = [
            pltpu.VMEM((2, planes, count, width), BF16),
            pltpu.VMEM((2, count, width), BF16),
            DMA((2, planes, 2)),
            DMA((2, planes, 2)),
            DMA((2,)),
        ]
    results = pl.pallas_call(
        kernel,
        grid=(local,),
        out_shape=[
            jax.ShapeDtypeStruct((blocks, count, width + 128), BF16),
            jax.ShapeDtypeStruct(cut_shape, BF16),
            jax.ShapeDtypeStruct(cut_shape, BF16),
            jax.ShapeDtypeStruct(down_shape, BF16),
        ]
        + [jax.ShapeDtypeStruct((count, width), F32)] * len(more),
        in_specs=[
            once(normed.shape),
            once(codes.shape),
            once(probs_t.shape),
            shares_of_expert(gate_w.shape),
            shares_of_expert(up_w.shape),
            shares_of_expert(down_w.shape),
            per_expert(gate_part.shape[1:]),
            per_expert(up_part.shape[1:]),
        ]
        + [once(array.shape) for array in arrived]
        + [ANY_SPEC] * len(more),
        out_specs=[once((blocks, count, width + 128)), cut_spec, cut_spec, down_spec]
        + [once((count, width))] * len(more),
        scratch_shapes=[
            pltpu.VMEM((blocks, lines, width), BF16),
            pltpu.VMEM((blocks, lines, width), BF16),
            pltpu.VMEM((blocks, count, lines), BF16),
            pltpu.VMEM((blocks, lines, 128), BF16),
            pltpu.VMEM((codes.shape[2], count), F32),
        ]
        + late_scratch,
        compiler_params=plain_params(62, 15 if more else None),
        cost_estimate=busy(30),
        name="experts_backward",
    )(normed, codes, probs_t, gate_w, up_w, down_w, gate_part, up_part, *arrived, *more)
    row_sums, gate_term, up_term, down_term, *added = results
    if not split:
        down_term = jnp.moveaxis(
            down_term.reshape(local, hidden_size, shares, band), 2, 0
        )
    return row_sums, gate_term, up_term, down_term, *added


GROUP = 4 * HEAD_SIZE


def turn_heads(values, cosine, sine, sign):
    half = HEAD_SIZE // 2
    lanes = lax.broadcasted_iota(jnp.int32, values.shape, 1)
    first = lax.rem(lanes, HEAD_SIZE) < half
    other = jnp.where(
        first, -pltpu.roll(values, GROUP - half, 1), pltpu.roll(values, half, 1)
    )
    return values * cosine + sign * other * sine


def spread_head(values, place):
    lanes = lax.broadcasted_iota(jnp.int32, values.shape, 1) // HEAD_SIZE
    alone = jnp.where(lanes == place, values, jnp.zeros_like(values))
    return (
        alone
        + pltpu.roll(alone, HEAD_SIZE, 1)
        + pltpu.roll(alone, 2 * HEAD_SIZE, 1)
        + pltpu.roll(alone, 3 * HEAD_SIZE, 1)
    )


def only_head(values, h):
    lanes = lax.broadcasted_iota(jnp.int32, values.shape, 1) // HEAD_SIZE
    return jnp.where(lanes == h, values, jnp.zeros_like(values))


def may_attend(starts_ref, first, rows, stop):
    here = first + lax.broadcasted_iota(jnp.int32, (rows, 1), 0)
    there = lax.broadcasted_iota(jnp.int32, (1, stop), 1)
    mine, theirs = jnp.zeros_like(here), jnp.zeros_like(there)
    for i in range(starts_ref.shape[1]):
        start = starts_ref[0, i]
        mine = mine + jnp.where(here >= start, 1, 0)
        theirs = theirs + jnp.where(there >= start, 1, 0)
    return (mine == theirs) & (there <= here)


def probabilities(query_rows, keys, allowed):
    scores = jnp.where(allowed, dot_t(query_rows, keys) * (1.0 / math.sqrt(HEAD_SIZE)), -1e30)
    weights = jnp.exp(scores - jnp.max(scores, axis=1, keepdims=True))
    return weights / jnp.sum(weights, axis=1, keepdims=True)


SMEM_SPEC = pl.BlockSpec(memory_space=pltpu.SMEM)
ROWS = 256


def attention_forward(normed, slab, out_rows, starts, cosine, sine):
    length, width = normed.shape
    rows = min(ROWS, length)

    def kernel(starts_ref, x_ref, w_ref, wv_ref, o_ref, c_ref, s_ref, out, heads, values, mixed, keys, spread):
        @pl.loop(0, length // rows)
        def _(i):
            part = pl.ds(pl.multiple_of(i * rows, rows), rows)
            turned = turn_heads(dot(x_ref[part, :], w_ref[...]), c_ref[part, :], s_ref[part, :], 1.0).astype(BF16)
            heads[part, :] = turned
            tail = dot(x_ref[part, :], wv_ref[...])
            lanes = lax.broadcasted_iota(jnp.int32, tail.shape, 1)
            value = jnp.where(lanes < HEAD_SIZE, tail, 0.0)
            values[part, :] = value.astype(BF16)
            keys[part, :] = spread_head(turned.astype(F32), 3).astype(BF16)
            both = jnp.concatenate([value, jnp.zeros_like(value)], axis=1)
            spread[part, :] = spread_head(both, 0).astype(BF16)

        for i in range(length // rows):
            first, stop = i * rows, (i + 1) * rows
            allowed = may_attend(starts_ref, first, rows, stop)
            queries = heads[first:stop, :]
            total = jnp.zeros((rows, GROUP), F32)
            for h in range(3):
                probs = probabilities(only_head(queries, h), keys[:stop, :], allowed).astype(BF16)
                total = total + dot(probs, only_head(spread[:stop, :], h))
            low = total.astype(BF16)
            mixed[first:stop, :] = low
            out[first:stop, :] = dot(low[:, : 3 * HEAD_SIZE], o_ref[...]).astype(BF16)

    return pl.pallas_call(
        kernel,
        out_shape=[
            jax.ShapeDtypeStruct((length, width), BF16),
            jax.ShapeDtypeStruct((length, GROUP), BF16),
            jax.ShapeDtypeStruct((length, 128), BF16),
            jax.ShapeDtypeStruct((length, GROUP), BF16),
        ],
        in_specs=[SMEM_SPEC] + [VMEM_SPEC] * 6,
        out_specs=[VMEM_SPEC] * 4,
        scratch_shapes=[pltpu.VMEM((length, GROUP), BF16), pltpu.VMEM((length, GROUP), BF16)],
        compiler_params=pltpu.CompilerParams(vmem_limit_bytes=40 << 20),
        cost_estimate=busy(10),
        name="attend_forward",
    )(starts, normed, *slab, out_rows, cosine, sine)


def attention_backward(normed, slab, out_rows, starts, cosine, sine, heads, values, mixed, branch, rest):
    length, width = normed.shape
    rows = min(ROWS, length)
    scale = 1.0 / math.sqrt(HEAD_SIZE)
    used = 3 * HEAD_SIZE

    def kernel(
        starts_ref, x_ref, w_ref, wv_ref, o_ref, c_ref, s_ref, h_ref, v_ref, m_ref, b_ref, r_ref,
        out, wide, tall, keys, spread, grads, key_sum, value_sum, low,
    ):
        @pl.loop(0, length // rows)
        def _(i):
            part = pl.ds(pl.multiple_of(i * rows, rows), rows)
            keys[part, :] = spread_head(h_ref[part, :].astype(F32), 3).astype(BF16)
            value = v_ref[part, :].astype(F32)
            both = jnp.concatenate([value, jnp.zeros_like(value)], axis=1)
            spread[part, :] = spread_head(both, 0).astype(BF16)
            grad = dot_t(b_ref[part, :], o_ref[...])
            grads[part, :] = jnp.concatenate(
                [grad, jnp.zeros((rows, HEAD_SIZE), F32)], axis=1
            ).astype(BF16)
            key_sum[part, :] = jnp.zeros((rows, GROUP), F32)
            value_sum[part, :] = jnp.zeros((rows, GROUP), F32)

        for i in range(length // rows):
            first, stop = i * rows, (i + 1) * rows
            allowed = may_attend(starts_ref, first, rows, stop)
            queries, upstream = h_ref[first:stop, :], grads[first:stop, :]
            query_grad = jnp.zeros((rows, GROUP), F32)
            for h in range(3):
                query_rows, grad_rows = only_head(queries, h), only_head(upstream, h)
                probs = probabilities(query_rows, keys[:stop, :], allowed)
                prob_grad = dot_t(grad_rows, spread[:stop, :])
                centre = jnp.sum(probs * prob_grad, axis=1, keepdims=True)
                score_grad = (probs * (prob_grad - centre)).astype(BF16)
                query_grad = query_grad + dot(score_grad, only_head(keys[:stop, :], h))
                key_sum[:stop, :] += dot(score_grad.T, query_rows)
                value_sum[:stop, :] += dot(probs.astype(BF16).T, grad_rows)
            low[first:stop, :GROUP] = (query_grad * scale).astype(BF16)

        @pl.loop(0, length // rows)
        def _(i):
            part = pl.ds(pl.multiple_of(i * rows, rows), rows)
            keyed = key_sum[part, :]
            keyed = (
                pltpu.roll(keyed, HEAD_SIZE, 1)
                + pltpu.roll(keyed, 2 * HEAD_SIZE, 1)
                + pltpu.roll(keyed, 3 * HEAD_SIZE, 1)
            ) * scale
            lanes = lax.broadcasted_iota(jnp.int32, keyed.shape, 1)
            raw = jnp.where(lanes < used, low[part, :GROUP].astype(F32), keyed)
            raw = raw.astype(BF16).astype(F32)
            low[part, :GROUP] = turn_heads(raw, c_ref[part, :], s_ref[part, :], -1.0).astype(BF16)
            valued = value_sum[part, :]
            valued = (
                valued
                + pltpu.roll(valued, GROUP - HEAD_SIZE, 1)
                + pltpu.roll(valued, GROUP - 2 * HEAD_SIZE, 1)
            )[:, :128]
            lanes = lax.broadcasted_iota(jnp.int32, valued.shape, 1)
            low[part, GROUP:] = jnp.where(lanes < HEAD_SIZE, valued, 0.0).astype(BF16)
            grad = dot_t(low[part, :GROUP], w_ref[...]) + dot_t(low[part, GROUP:], wv_ref[...])
            out[part, :] = grad.astype(BF16)

        step = 256

        @pl.loop(0, width // step)
        def _(i):
            part = pl.ds(pl.multiple_of(i * step, step), step)
            made = dot(x_ref[:, part].T, low[...])
            wide[part, :GROUP] = made[:, :GROUP].astype(BF16)
            lanes = lax.broadcasted_iota(jnp.int32, (step, 128), 1)
            beside = jnp.concatenate([r_ref[part, :], r_ref[part, :]], axis=1)
            wide[part, GROUP:] = jnp.where(
                lanes < HEAD_SIZE, made[:, GROUP:], beside.astype(F32)
            ).astype(BF16)
        tall[...] = dot(m_ref[...].T, b_ref[...])[:used].astype(BF16)

    return pl.pallas_call(
        kernel,
        out_shape=[
            jax.ShapeDtypeStruct((length, width), BF16),
            jax.ShapeDtypeStruct((width, GROUP + 128), BF16),
            jax.ShapeDtypeStruct((used, width), BF16),
        ],
        in_specs=[SMEM_SPEC] + [VMEM_SPEC] * 11,
        out_specs=[VMEM_SPEC] * 3,
        scratch_shapes=[
            pltpu.VMEM((length, GROUP), BF16),
            pltpu.VMEM((length, GROUP), BF16),
            pltpu.VMEM((length, GROUP), BF16),
            pltpu.VMEM((length, GROUP), F32),
            pltpu.VMEM((length, GROUP), F32),
            pltpu.VMEM((length, GROUP + 128), BF16),
        ],
        compiler_params=pltpu.CompilerParams(vmem_limit_bytes=50 << 20),
        cost_estimate=busy(20),
        name="attend_backward",
    )(starts, normed, *slab, out_rows, cosine, sine, heads, values, mixed, branch, rest)


def norm_factor(stream):
    return lax.rsqrt(jnp.mean(stream * stream, axis=-1, keepdims=True) + EPSILON)


def norm_back(stream, factor, gain_row, upstream):
    scaled = gain_row * upstream
    inner_mean = jnp.mean(stream * scaled, axis=-1, keepdims=True)
    return factor * scaled - stream * (factor * factor * factor) * inner_mean


def per_device(
    layer_in,
    cotangent,
    doc_starts,
    routes,
    attn_gain,
    ffn_gain,
    query_weight,
    key_matrix,
    value_matrix,
    out_weight,
    router_weight,
    gate_weight,
    up_weight,
    down_weight,
):
    planes, groups = lax.axis_size("za"), lax.axis_size("grp")
    seq_count = 2 * planes
    place = lax.axis_index("za") * 2 + lax.axis_index("yb")
    count, width = layer_in.shape[1:]
    length = count * seq_count
    layers = attn_gain.shape[0]
    experts_all = router_weight.shape[2]
    local = gate_weight.shape[1]
    top = routes.shape[2]
    slots = -(-(count * top * 4 // (3 * experts_all) + 1) // 16) * 16
    columns = query_weight.shape[2] // 8
    kv = key_matrix.shape[2] // 8
    bands = query_weight.shape[1]

    swap = [(a * 4 + f, f * 4 + a) for a in range(planes) for f in range(4)]

    def exchange(array):
        return lax.ppermute(array, ("za", "xh", "co"), swap)


    small = jnp.stack([attn_gain, ffn_gain], axis=-1)
    used = columns + 2 * kv + experts_all + 2
    padded = -(-used // 128) * 128

    def whole_rows(array):
        if groups == 1:
            return array
        return jnp.moveaxis(lax.all_gather(array, "grp"), 0, 1).reshape(
            layers, groups * bands, array.shape[-1]
        )

    packed = jnp.concatenate(
        [
            jnp.moveaxis(query_weight.reshape(layers, bands, 8, columns), 2, 0),
            jnp.moveaxis(key_matrix.reshape(layers, bands, 8, kv), 2, 0),
            jnp.moveaxis(value_matrix.reshape(layers, bands, 8, kv), 2, 0),
            jnp.broadcast_to(
                jnp.concatenate(
                    [router_weight, small, jnp.zeros((layers, bands, padded - used), BF16)], axis=-1
                )[None],
                (8, layers, bands, padded - columns - 2 * kv),
            ),
        ],
        axis=-1,
    )
    pieces = packed
    if groups > 1:
        pieces = jnp.transpose(lax.all_gather(packed, "grp"), (1, 2, 0, 3, 4)).reshape(
            8, layers, groups * bands, padded
        )
    band_rows = groups * bands

    def in_order(array):
        if groups > 1:
            array = array.reshape(planes, 2, 4, groups, bands, -1)
            array = jnp.swapaxes(array, 2, 3)
        return array.reshape(width, -1)

    all_out = whole_rows(out_weight)
    def carry(array, layer):
        return (array, layer) if groups == 1 and layer < layers else None

    firsts, late_heads, late_others, swapped, carried = enter(
        layer_in[0],
        pieces[..., : padded - 128],
        pieces[..., padded - 128 :],
        all_out[0],
        (cotangent[0], routes[0], doc_starts),
        used - 2 - (padded - 128),
        planes,
        carry(gate_weight, 0),
    )
    normed_first, stream, tall_rows, heads_slab, other_slab = firsts
    stream = stream.astype(F32)
    slabs = [(in_order(heads_slab), in_order(other_slab))]
    upstream_low, chosen, starts = swapped

    def sum_share(term):
        return lax.psum_scatter(term, ("xh", "co"), scatter_dimension=0)

    def sum_experts(gate_term, up_term, down_term):
        axes = ("grp", "xh", "co")
        return (
            lax.psum_scatter(gate_term, axes, scatter_dimension=0),
            lax.psum_scatter(up_term, axes, scatter_dimension=0),
            lax.psum_scatter(down_term, axes, scatter_dimension=0),
        )

    named = jnp.sum(
        (chosen[:, :, None] == jnp.arange(experts_all, dtype=jnp.int32)).astype(F32), axis=1
    )
    ids = jnp.arange(count, dtype=jnp.int32)
    before = (ids[None, :] < ids[:, None]).astype(BF16)
    rank = jnp.dot(before, named.astype(BF16), preferred_element_type=F32)
    codes = jnp.where(named > 0, rank, -1.0)
    codes = jnp.pad(codes, ((0, 0), (0, 128 - experts_all)), constant_values=-1.0).astype(BF16)

    angles = np.arange(length)[:, None] * 10000.0 ** (
        -2.0 * np.arange(HEAD_SIZE // 2)[None, :] / HEAD_SIZE
    )
    cosine = jnp.asarray(np.tile(np.cos(angles), (1, 8)), F32)
    sine = jnp.asarray(np.tile(np.sin(angles), (1, 8)), F32)

    def fetch_experts(layer):
        axes = ("grp", "xh", "co")
        return [
            lax.all_gather(gate_weight[layer], axes, axis=1, tiled=True)[None],
            lax.all_gather(up_weight[layer], axes, axis=1, tiled=True)[None],
            lax.all_gather(down_weight[layer], axes, axis=2, tiled=True)[None],
        ]

    states, arrived = [], []
    out_rows = []
    for layer in range(layers):
        if groups > 1:
            carried = fetch_experts(layer)
        slab = slabs[layer]
        small_part = slab[1][:, columns + 2 * kv - GROUP :]
        attn_row = small_part[:, experts_all].astype(F32)
        ffn_row = small_part[:, experts_all + 1].astype(F32)
        router_w = small_part[:, :experts_all]
        factor_one = norm_factor(stream)
        if layer == 0:
            normed_one = normed_first
        else:
            own_one = (stream * factor_one * attn_row).astype(BF16)
            normed_one, tall_rows = gather_plane(own_one, tall_rows)
        tall_rows = jnp.swapaxes(tall_rows.reshape(4, groups, bands, width), 0, 1)
        out_rows.append(tall_rows.reshape(columns, width))
        normed_one = normed_one.reshape(length, width)
        tall = out_rows[layer]
        branch, heads_low, values, mixed = attention_forward(
            normed_one, slab, tall, starts, cosine, sine
        )
        branch = branch.reshape(8, count, width)
        if layer + 1 < layers:
            share = carry(up_weight, 0) if layer == 0 else None
            branch, *later = scatter_plane_first(
                branch, (late_heads[layer], late_others[layer]), all_out[layer + 1], planes, share
            )
            if share is not None:
                carried, later = [carried[0], later[0]], later[1:]
            tall_rows, *later = later
            slabs.append([in_order(array) for array in later])
        else:
            branch = scatter_plane(branch)
        middle = stream + branch
        factor_two = norm_factor(middle)
        own_two = (middle * factor_two * ffn_row).astype(BF16)
        if layer == 0:
            results = gather_group(own_two, planes, 8, carry(down_weight, 0), codes)
            normed_two, codes = results[0], results[-1]
            if groups == 1:
                carried = [*carried, results[1]]
        else:
            share = carry(down_weight, layer)
            normed_two = gather_group(own_two, planes, 12, share)
            if share is not None:
                normed_two, last = normed_two
                carried = [*carried, last]
        share = count // layers
        gate_w, up_w, down_w = carried
        share = count // layers
        total, gate_part, up_part, gate_probs, probs_t, gathered, *carried = experts_forward(
            normed_two, codes, slab[1], gate_w, up_w, down_w,
            upstream_low[layer * share : (layer + 1) * share], slots, planes,
            11 if layer == 0 else 13, carry(gate_weight, layer + 1),
        )
        arrived.append(gathered)
        own_probs = lax.dynamic_index_in_dim(gate_probs, place, 0, keepdims=False)[:, :experts_all]
        states.append(
            (
                stream, factor_one, normed_one, heads_low, values, mixed, tall, middle,
                factor_two, own_two, normed_two, own_probs, probs_t, gate_part, up_part, total,
                gate_w, up_w, down_w, attn_row, ffn_row, slab, router_w,
            )
        )
        if layer + 1 < layers:
            share = carry(up_weight, layer + 1)
            added = scatter_group(total, planes, 14, () if share is None else (share,))
            if share is not None:
                added, last = added
                carried = [*carried, last]
            stream = middle + added

    result, pending = None, None
    upstream = upstream_low.astype(F32)
    expert_out = [None] * layers
    wide_terms, tall_terms = [None] * layers, [None] * layers
    for layer in reversed(range(layers)):
        (
            stream, factor_one, normed_one, heads_low, values, mixed, tall, middle,
            factor_two, own_two, normed_two, own_probs, probs_t, gate_part, up_part, total,
            gate_w, up_w, down_w, attn_row, ffn_row, slab, router_w,
        ) = states[layer]
        if layer + 1 < layers:
            sending = upstream.astype(BF16)
            arrived = gather_group(sending, planes, 0, pending)
            if pending is not None:
                arrived, up_sum = arrived
                expert_out[layer + 1] = (expert_out[layer + 1][0], up_sum, expert_out[layer + 1][2])
            arrived = [arrived]
        row_sums, gate_term, up_term, down_term, *added = experts_backward(
            normed_two, arrived, codes, probs_t, gate_w, up_w, down_w, gate_part, up_part,
            slots, 4 * groups, total if layer + 1 == layers else None, planes,
        )
        if added:
            result = exchange((middle + added[0]).astype(BF16))
        if groups > 1:
            summed = scatter_group(row_sums, planes, 2)
            expert_out[layer] = sum_experts(gate_term, up_term, down_term)
        else:
            second = gate_term if layer > 0 else up_term
            summed, down_sum, second = scatter_group(
                row_sums, planes, 2, ((down_term, None), (second, None))
            )
            pending = (up_term, None) if layer > 0 else (gate_term, None)
            expert_out[layer] = (second, None, down_sum) if layer > 0 else (None, second, down_sum)
        weighted = summed[:, width : width + experts_all]
        weighted = weighted + summed[:, width + 64 : width + 64 + experts_all]
        logit_grad = weighted - own_probs * jnp.sum(weighted, axis=-1, keepdims=True)
        router_term = jnp.einsum("td,te->de", own_two.astype(F32), logit_grad, precision=HIGHEST)
        normed_two_grad = summed[:, :width] + jnp.einsum(
            "te,de->td", logit_grad, router_w.astype(F32), precision=HIGHEST
        )
        ffn_gain_term = jnp.sum(normed_two_grad * middle * factor_two, axis=0)
        middle_grad = upstream + norm_back(middle, factor_two, ffn_row, normed_two_grad)
        branch_low = gather_plane(middle_grad.astype(BF16)).reshape(length, width)
        rest = jnp.concatenate([router_term, ffn_gain_term[:, None]], axis=1)
        rest = jnp.pad(rest, ((0, 0), (0, 32 - experts_all - 1)))
        high = rest.astype(BF16)
        low_part = (rest - high.astype(F32)).astype(BF16)
        partial, qkv_term, out_term = attention_backward(
            normed_one, slab, tall, starts, cosine, sine, heads_low, values, mixed, branch_low,
            jnp.concatenate([high, low_part], axis=1),
        )
        partial = partial.reshape(8, count, width)
        normed_one_grad = scatter_plane(partial)
        upstream = middle_grad + norm_back(stream, factor_one, attn_row, normed_one_grad)
        if groups > 1:
            qkv_term = jnp.swapaxes(
                qkv_term.reshape(planes, 2, groups, 4, bands, padded), 2, 3
            )
            out_term = jnp.swapaxes(out_term.reshape(groups, 4, bands, width), 0, 1)
        wide_terms[layer] = qkv_term.reshape(planes, 8, band_rows, padded)
        tall_terms[layer] = out_term.reshape(4, band_rows, width)

    if groups > 1:
        sums = collect(wide_terms, tall_terms, planes)
        input_grad = exchange(upstream.astype(BF16))
    else:
        query_out, key_out, value_out, tall_out, rest, input_grad, gate_sum = collect(
            wide_terms, tall_terms, planes, (pending,),
            (query_weight, key_matrix, value_matrix), upstream.astype(BF16),
        )
        expert_out[0] = (gate_sum, *expert_out[0][1:])
        products = rest[..., 32]
    if groups > 1:
        sums = [
            lax.psum_scatter(array, "grp", scatter_dimension=array.ndim - 2, tiled=True)
            for array in sums
        ]
        wide_sums = jnp.stack(sums[:layers]).astype(F32)

        def by_heads(start, stop):
            return jnp.swapaxes(wide_sums[..., start:stop], 1, 2).reshape(layers, bands, -1)

        query_out = by_heads(0, columns)
        key_out = by_heads(columns, columns + kv)
        value_out = by_heads(columns + kv, columns + 2 * kv)
        tall_out = jnp.stack(sums[layers:]).astype(F32)
        rest = jnp.sum(wide_sums[..., columns + 2 * kv :], axis=1)
        rest = rest[..., :32] + rest[..., 32:64]
        products = (
            jnp.sum(query_weight.astype(F32) * query_out, axis=-1)
            + jnp.sum(key_matrix.astype(F32) * key_out, axis=-1)
            + jnp.sum(value_matrix.astype(F32) * value_out, axis=-1)
        )
    attn_out = products / attn_gain.astype(F32)

    def stacked(lists, i):
        return jnp.stack([lists[layer][i] for layer in range(layers)]).astype(F32)

    return (
        result[None],
        input_grad.astype(F32)[None],
        attn_out,
        rest[..., experts_all],
        query_out,
        key_out,
        value_out,
        tall_out,
        rest[..., :experts_all],
        stacked(expert_out, 0),
        stacked(expert_out, 1),
        stacked(expert_out, 2),
    )


def solution(mesh):
    seq, fsdp = mesh.shape["seq"], mesh.shape["fsdp"]
    split = Mesh(mesh.devices.reshape(seq // 2, 2, fsdp // 4, 2, 2), AX)
    s, f = ("za", "yb"), ("grp", "xh", "co")
    token = P(f, s, None)
    dense = P(None, s + f, None)
    gain = P(None, s + f)
    wide, tall = P(None, s, f, None), P(None, s, None, f)
    return jax.shard_map(
        per_device,
        mesh=split,
        in_specs=(token, token, P(f, None), token, gain, gain, dense, dense, dense, dense, dense, wide, wide, tall),
        out_specs=(token, token, gain, gain, dense, dense, dense, dense, dense, wide, wide, tall),
        check_vma=False,
    )
```

```python
import math

import numpy as np
import jax, jax.numpy as jnp
from jax import lax
from jax.experimental import pallas as pl
from jax.experimental.pallas import tpu as pltpu
from jax.sharding import Mesh, PartitionSpec as P
MESH = pl.DeviceIdType.MESH
AX=("za","yb","grp","xh","co")

class Ring8:
    def __init__(self, na):
        self.n=2*na; self.na=na
        za=lax.axis_index("za"); yb=lax.axis_index("yb")
        self.rho = za + yb*(2*na-1-2*za)
    def pos(self, r):
        r = lax.rem(r+2*self.n, self.n)
        yb = r//self.na
        za = r + yb*(2*self.na-1-2*r)
        return za, yb
    def dev(self, r):
        za,yb=self.pos(r); return {"za":za,"yb":yb}
    def slot(self, r):
        za,yb=self.pos(r); return za*2+yb

class Ring4:
    def __init__(self):
        self.n=4
        x=lax.axis_index("xh"); b=lax.axis_index("yb"); self.c=lax.axis_index("co")
        self.rho = 2*x + (x+b-2*x*b)
    def pos(self, r):
        r = lax.rem(r+2*self.n, self.n)
        x = r//2; m=lax.rem(r,2)
        return x, m+x-2*x*m
    def dev(self, r):
        x,b=self.pos(r); return {"xh":x,"yb":b}
    def slot(self, r, sib=False):
        x,b=self.pos(r); c = (1-self.c) if sib else self.c
        return (x*2+c)*2+b
    def sib_dev(self):
        return {"co":1-self.c}

def barrier(devs):
    sem = pltpu.get_barrier_semaphore()
    for d in devs:
        pl.semaphore_signal(sem, inc=1, device_id=d, device_id_type=MESH)
    pl.semaphore_wait(sem, len(devs))

def rcopy(src, dst, ss, rs, dev):
    return pltpu.make_async_remote_copy(src_ref=src, dst_ref=dst, send_sem=ss, recv_sem=rs, device_id=dev, device_id_type=MESH)

def ag_ring(ring, K, own, out, send, recv, sib=None, beside=None):
    n=ring.n; S=n//2; T=own.shape[0]; rows=T//K; rho=ring.rho
    def chunks(d,s): return range(K) if s<S else (range(K//2) if d==0 else range(K//2,K))
    def mk(d,s,c):
        sg=1-2*d
        slot=ring.slot(rho-(s-1)*sg)
        sl=pl.ds(c*rows,rows)
        src = own.at[sl] if s==1 else out.at[slot,sl]
        return rcopy(src, out.at[slot,sl], send.at[d,s-1,c], recv.at[d,s-1,c], ring.dev(rho+sg))
    def rd(d,s,c):
        sg=1-2*d
        slot=ring.slot(rho-s*sg); sl=pl.ds(c*rows,rows)
        return rcopy(out.at[slot,sl], out.at[slot,sl], send.at[d,s-1,c], recv.at[d,s-1,c], ring.dev(rho-sg))
    started=[]
    def sibcopy(slot, slot_src, c, idx, src):
        ss,rs=sib
        cp=rcopy(src, out.at[slot,pl.ds(c*rows,rows)], ss.at[idx,c], rs.at[idx,c], ring.sib_dev())
        cp.start(); started.append(cp)
    def arrived(d,s,c):
        rd(d,s,c).wait_recv()
        if sib is not None:
            sg=1-2*d
            slot=ring.slot(rho-s*sg)
            idx = s*sg % n
            sibcopy(slot, None, c, idx, out.at[slot,pl.ds(c*rows,rows)])
    sends=[]
    for s in range(1,S+1):
        for c in range(K):
            for d in (0,1):
                if c in chunks(d,s):
                    if s>1: arrived(d,s-1,c)
                    cp=mk(d,s,c); cp.start(); sends.append(cp)
        if beside is not None: beside(s)
        if s==1 and sib is not None:
            for c in range(K): sibcopy(ring.slot(rho), None, c, 0, own.at[pl.ds(c*rows,rows)])
    for s in (S-1,S):
        for c in range(K):
            for d in (0,1):
                if s==S and c in chunks(d,S): arrived(d,S,c)
                if s==S-1 and S>1 and c not in chunks(d,S): arrived(d,S-1,c)
    if sib is not None:
        ss,rs=sib
        for idx in range(n):
            for c in range(K):
                slot=ring.slot(rho-idx, True); sl=pl.ds(c*rows,rows)
                rcopy(out.at[slot,sl],out.at[slot,sl],ss.at[idx,c],rs.at[idx,c],ring.sib_dev()).wait_recv()
    for cp in sends+started: cp.wait_send()

class RingGather:
    def __init__(self, ring, chunks, own, out, send, recv):
        self.ring, self.k, self.own, self.out, self.send, self.recv = ring, chunks, own, out, send, recv
        self.last = ring.n // 2
        self.rows = own.shape[0] // chunks

    def chunks(self, d, s):
        if s < self.last:
            return range(self.k)
        return range(self.k // 2) if d == 0 else range(self.k // 2, self.k)

    def copy(self, d, s, c):
        sign = 1 - 2 * d
        slot = self.ring.slot(self.ring.rho - (s - 1) * sign)
        part = pl.ds(c * self.rows, self.rows)
        source = self.own.at[part] if s == 1 else self.out.at[slot, part]
        return rcopy(
            source, self.out.at[slot, part], self.send.at[d, s - 1, c], self.recv.at[d, s - 1, c],
            self.ring.dev(self.ring.rho + sign),
        )

    def arrive(self, d, s, c):
        sign = 1 - 2 * d
        ref = self.out.at[self.ring.slot(self.ring.rho - s * sign), pl.ds(c * self.rows, self.rows)]
        rcopy(
            ref, ref, self.send.at[d, s - 1, c], self.recv.at[d, s - 1, c],
            self.ring.dev(self.ring.rho - sign),
        ).wait_recv()

    def step(self, s):
        for c in range(self.k):
            for d in (0, 1):
                if c in self.chunks(d, s):
                    if s > 1:
                        self.arrive(d, s - 1, c)
                    self.copy(d, s, c).start()

    def finish(self):
        for s in (self.last - 1, self.last):
            for c in range(self.k):
                for d in (0, 1):
                    if c in self.chunks(d, s) and (s == self.last or c not in self.chunks(d, s + 1)):
                        self.arrive(d, s, c)
        for s in range(1, self.last + 1):
            for c in range(self.k):
                for d in (0, 1):
                    if c in self.chunks(d, s):
                        self.copy(d, s, c).wait_send()


class RingScatter:
    def __init__(self, ring, chunks, part, buf, stage, send, recv, load):
        self.ring, self.k, self.part, self.buf, self.stage = ring, chunks, part, buf, stage
        self.send, self.recv, self.load = send, recv, load
        self.last = ring.n // 2
        self.rows = stage.shape[1] // chunks

    def chunks(self, d, s):
        if s > 1:
            return range(self.k)
        return range(self.k // 2) if d == 0 else range(self.k // 2, self.k)

    def slot(self, d, s):
        return self.ring.slot(self.ring.rho + (1 - 2 * d) * (self.last + 1 - s))

    def loading(self, d, s):
        return pltpu.make_async_copy(
            self.part.at[self.slot(d, s)], self.stage.at[d], self.load.at[d]
        )

    def copy(self, d, s, c):
        rows = pl.ds(c * self.rows, self.rows)
        if s > 1 and c in self.chunks(d, s - 1):
            source = self.buf.at[d, s - 2, rows]
        else:
            source = self.part.at[self.slot(d, s), rows]
        return rcopy(
            source, self.buf.at[d, s - 1, rows], self.send.at[d, s - 1, c],
            self.recv.at[d, s - 1, c], self.ring.dev(self.ring.rho + 1 - 2 * d),
        )

    def arrive(self, d, s, c):
        ref = self.buf.at[d, s - 1, pl.ds(c * self.rows, self.rows)]
        rcopy(
            ref, ref, self.send.at[d, s - 1, c], self.recv.at[d, s - 1, c],
            self.ring.dev(self.ring.rho - (1 - 2 * d)),
        ).wait_recv()

    def step(self, s):
        if s > 1:
            for d in (0, 1):
                self.loading(d, s).wait()
        for c in range(self.k):
            for d in (0, 1):
                if c not in self.chunks(d, s):
                    continue
                if s > 1 and c in self.chunks(d, s - 1):
                    self.arrive(d, s - 1, c)
                    rows = pl.ds(c * self.rows, self.rows)
                    self.buf[d, s - 2, rows, :] = (
                        self.buf[d, s - 2, rows, :].astype(F32)
                        + self.stage[d, rows, :].astype(F32)
                    ).astype(BF16)
                self.copy(d, s, c).start()
        for d in (0, 1):
            if s < self.last or d == 0:
                self.loading(d, s + 1).start()

    def finish(self):
        self.loading(0, self.last + 1).wait()
        for d in (0, 1):
            for c in range(self.k):
                self.arrive(d, self.last, c)
        for s in range(1, self.last + 1):
            for d in (0, 1):
                for c in self.chunks(d, s):
                    self.copy(d, s, c).wait_send()
        return (
            self.buf[0, self.last - 1].astype(F32) + self.buf[1, self.last - 1].astype(F32)
        ) + self.stage[0].astype(F32)


def rs_ring(ring, K, part, buf, send, recv, slotf, beside=None):
    n=ring.n; S=n//2; T=buf.shape[2]; rows=T//K; rho=ring.rho
    def chunks(d,s): return range(K) if s>1 else (range(K//2) if d==0 else range(K//2,K))
    sends=[]
    def rd(d,s,c):
        sl=pl.ds(c*rows,rows)
        return rcopy(buf.at[d,s-1,sl],buf.at[d,s-1,sl],send.at[d,s-1,c],recv.at[d,s-1,c],ring.dev(rho-(1-2*d)))
    for s in range(1,S+1):
        order=list(range(K))
        if s==2:
            pass
        for c in order:
            for d in (0,1):
                if c not in chunks(d,s): continue
                sg=1-2*d
                dest=rho+sg*(S+1-s)
                sl=pl.ds(c*rows,rows)
                if s>1 and c in chunks(d,s-1):
                    rd(d,s-1,c).wait_recv()
                    buf[d,s-2,sl,:] = (buf[d,s-2,sl,:].astype(jnp.float32)+part[slotf(dest),sl,:].astype(jnp.float32)).astype(buf.dtype)
                    src=buf.at[d,s-2,sl]
                else:
                    src=part.at[slotf(dest),sl]
                cp=rcopy(src,buf.at[d,s-1,sl],send.at[d,s-1,c],recv.at[d,s-1,c],ring.dev(rho+sg))
                cp.start(); sends.append(cp)
        if beside is not None: beside(s+1)
    for c in range(K):
        for d in (0,1):
            rd(d,S,c).wait_recv()
    for cp in sends: cp.wait_send()

HEAD_SIZE = 64
EPSILON = 1e-05
HIGHEST = lax.Precision.HIGHEST
F32 = jnp.float32
BF16 = jnp.bfloat16
ANY_SPEC = pl.BlockSpec(memory_space=pltpu.HBM)
GATHERED_SPEC = pl.BlockSpec(memory_space=pl.ANY)
VMEM_SPEC = pl.BlockSpec(memory_space=pltpu.VMEM)
CHUNKS = 4
DMA = pltpu.SemaphoreType.DMA


class ShareGather:
    def __init__(self, source, out, sems):
        self.source, self.out = source, out
        self.x_send, self.x_recv, self.s_send, self.s_recv, self.own, self.room = sems
        x, c = lax.axis_index("xh"), lax.axis_index("co")
        self.mine, self.across = x * 2 + c, (1 - x) * 2 + c
        self.beside, self.beside_across = x * 2 + 1 - c, (1 - x) * 2 + 1 - c
        self.chip, self.core = {"xh": 1 - x}, {"co": 1 - c}
        self.parts = source.shape[0]

    def to_chip(self, e):
        return rcopy(
            self.source.at[e], self.out.at[self.mine, e], self.x_send.at[e], self.x_recv.at[e],
            self.chip,
        )

    def to_core(self, e):
        if e == self.parts:
            source, target = self.source, self.out.at[self.mine]
        else:
            source = target = self.out.at[self.across, e]
        return rcopy(source, target, self.s_send.at[e], self.s_recv.at[e], self.core)

    def keep(self, half):
        ends = (self.source, self.room) if half == 0 else (self.room, self.out.at[self.mine])
        return pltpu.make_async_copy(*ends, self.own.at[half])

    def start(self):
        for e in range(self.parts):
            self.to_chip(e).start()
        self.to_core(self.parts).start()
        self.keep(0).start()

    def middle(self):
        self.keep(0).wait()
        self.keep(1).start()

    def end(self):
        self.forward()
        self.finish()

    def forward(self):
        for e in range(self.parts):
            ref = self.out.at[self.across, e]
            rcopy(ref, ref, self.x_send.at[e], self.x_recv.at[e], self.chip).wait_recv()
            self.to_core(e).start()

    def finish(self):
        for e in range(self.parts + 1):
            ref = self.out.at[self.beside_across, e] if e < self.parts else self.out.at[self.beside]
            rcopy(ref, ref, self.s_send.at[e], self.s_recv.at[e], self.core).wait_recv()
        for e in range(self.parts):
            self.to_chip(e).wait_send()
        for e in range(self.parts + 1):
            self.to_core(e).wait_send()
        self.keep(1).wait()


class ShareScatter:
    def __init__(self, source, out, rest):
        self.source, self.out = source, out
        (
            self.own, self.came, self.far, self.load, self.s_send, self.s_recv, self.x_send,
            self.x_recv, self.put,
        ) = rest
        x, c = lax.axis_index("xh"), lax.axis_index("co")
        self.mine = ((1 - x) * 2 + c, x * 2 + c)
        self.theirs = ((1 - x) * 2 + 1 - c, x * 2 + 1 - c)
        self.chip, self.core = {"xh": 1 - x}, {"co": 1 - c}
        self.parts = source.shape[1]

    def loading(self, k):
        return pltpu.make_async_copy(self.source.at[self.mine[k]], self.own.at[k], self.load.at[k])

    def to_core(self, k, e):
        return rcopy(
            self.source.at[self.theirs[k], e], self.came.at[k, e], self.s_send.at[k, e],
            self.s_recv.at[k, e], self.core,
        )

    def to_chip(self, e):
        return rcopy(
            self.own.at[0, e], self.far.at[e], self.x_send.at[e], self.x_recv.at[e], self.chip
        )

    def start(self):
        for k in (0, 1):
            self.loading(k).start()
            for e in range(self.parts):
                self.to_core(k, e).start()

    def middle(self):
        self.loading(0).wait()
        for e in range(self.parts):
            self.to_core(0, e).wait_recv()
            self.own[0, e] = (
                self.own[0, e].astype(F32) + self.came[0, e].astype(F32)
            ).astype(BF16)
            self.to_chip(e).start()

    def end(self):
        self.loading(1).wait()
        for e in range(self.parts):
            self.to_core(1, e).wait_recv()
            self.to_chip(e).wait_recv()
            self.own[1, e] = (
                self.own[1, e].astype(F32) + self.came[1, e].astype(F32) + self.far[e].astype(F32)
            ).astype(BF16)
        store = pltpu.make_async_copy(self.own.at[1], self.out, self.put)
        store.start()
        for e in range(self.parts):
            self.to_chip(e).wait_send()
            for k in (0, 1):
                self.to_core(k, e).wait_send()
        store.wait()


def carrier(share, source, out, rest):
    if share[1] is None:
        return ShareScatter(source, out, rest)
    return ShareGather(source.at[share[1]], out, rest)


def share_devices():
    return [{"xh": 1 - lax.axis_index("xh")}, {"co": 1 - lax.axis_index("co")}]


def share_shapes(share):
    if share is None:
        return [], [], []
    array = share[0]
    parts = array.shape[1]
    if share[1] is None:
        return (
            [array],
            [jax.ShapeDtypeStruct(array.shape[1:], BF16)],
            [
                pltpu.VMEM((2,) + array.shape[1:], BF16),
                pltpu.VMEM((2,) + array.shape[1:], BF16),
                pltpu.VMEM(array.shape[1:], BF16),
                DMA((2,)),
                DMA((2, parts)),
                DMA((2, parts)),
                DMA((parts,)),
                DMA((parts,)),
                DMA,
            ],
        )
    return (
        [array],
        [jax.ShapeDtypeStruct((4,) + array.shape[1:], BF16)],
        [
            DMA((parts,)),
            DMA((parts,)),
            DMA((parts + 1,)),
            DMA((parts + 1,)),
            DMA((2,)),
            pltpu.VMEM(array.shape[1:], BF16),
        ],
    )


def comm_params(number, megabytes=40):
    return pltpu.CompilerParams(
        collective_id=number, has_side_effects=True, vmem_limit_bytes=megabytes << 20
    )


def busy(microseconds):
    return pl.CostEstimate(flops=0, bytes_accessed=microseconds * 3_690_000, transcendentals=0)


def gather_group(rows, planes, number, share=None, beside=None):
    count, width = rows.shape
    more, outs, sems = share_shapes(share)
    extra = [] if beside is None else [beside]

    def kernel(x_ref, *refs):
        if more:
            w_ref, refs = refs[0], refs[1:]
        if extra:
            y_ref, refs = refs[0], refs[1:]
        o_ref, refs = refs[0], refs[1:]
        if more:
            b_ref, refs = refs[0], refs[1:]
        if extra:
            yo_ref, refs = refs[0], refs[1:]
        send, recv, own, *rest = refs
        if extra:
            y_send, y_recv, y_own, *rest = rest
        ring = Ring8(planes)
        devices = [ring.dev(ring.rho + 1), ring.dev(ring.rho - 1)]
        barrier(devices + share_devices() * len(more))
        local = pltpu.make_async_copy(x_ref, o_ref.at[ring.slot(ring.rho)], own)
        local.start()
        if more:
            carried = carrier(share, w_ref, b_ref, rest)
            carried.start()


        if extra:
            y_local = pltpu.make_async_copy(y_ref, yo_ref.at[ring.slot(ring.rho)], y_own)
            y_local.start()
            small = RingGather(ring, 2, y_ref, yo_ref, y_send, y_recv)

        def turn_of(turn):
            if extra:
                small.step(turn)
            if turn == 1 and more:
                carried.middle()

        ag_ring(ring, CHUNKS, x_ref, o_ref, send, recv, None, turn_of)
        if extra:
            small.finish()
            y_local.wait()
        if more:
            carried.end()
        local.wait()

    results = pl.pallas_call(
        kernel,
        out_shape=[jax.ShapeDtypeStruct((2 * planes, count, width), BF16)]
        + outs
        + [jax.ShapeDtypeStruct((2 * planes,) + array.shape, BF16) for array in extra],
        in_specs=[VMEM_SPEC] + [ANY_SPEC] * len(more) + [VMEM_SPEC] * len(extra),
        out_specs=[GATHERED_SPEC] + [ANY_SPEC] * len(more) + [VMEM_SPEC] * len(extra),
        scratch_shapes=[DMA((2, planes, CHUNKS)), DMA((2, planes, CHUNKS)), DMA]
        + [DMA((2, planes, 2)), DMA((2, planes, 2)), DMA] * len(extra)
        + sems,
        compiler_params=comm_params(number),
        cost_estimate=busy(33),
        name="gather_group",
    )(rows, *more, *extra)
    return results if more or extra else results[0]


def scatter_group(parts, planes, number, shares=()):
    _, count, width = parts.shape
    held = [share_shapes(share) for share in shares]
    more = [array for arrays, _, _ in held for array in arrays]

    def kernel(p_ref, *refs):
        w_refs, o_ref, refs = refs[: len(more)], refs[len(more)], refs[len(more) + 1 :]
        b_refs, refs = refs[: len(more)], refs[len(more) :]
        buf, send, recv, *rest = refs
        ring = Ring8(planes)
        devices = [ring.dev(ring.rho + 1), ring.dev(ring.rho - 1)]
        barrier(devices + share_devices() * (len(more) > 0))
        carried = []
        for i, share in enumerate(shares):
            some, rest = rest[: len(held[i][2])], rest[len(held[i][2]) :]
            carried.append(carrier(share, w_refs[i], b_refs[i], some))
            carried[-1].start()

        def beside(turn):
            if turn - 2 < len(carried):
                carried[turn - 2].middle()

        rs_ring(ring, CHUNKS, p_ref, buf, send, recv, ring.slot, beside)
        last = planes - 1
        o_ref[...] = (
            buf[0, last].astype(F32) + buf[1, last].astype(F32)
        ) + p_ref[ring.slot(ring.rho)].astype(F32)
        for one in carried:
            one.end()

    results = pl.pallas_call(
        kernel,
        out_shape=[jax.ShapeDtypeStruct((count, width), F32)]
        + [shape for _, shapes, _ in held for shape in shapes],
        in_specs=[VMEM_SPEC] + [ANY_SPEC] * len(more),
        out_specs=[VMEM_SPEC] + [ANY_SPEC] * len(more),
        scratch_shapes=[
            pltpu.VMEM((2, planes, count, width), BF16),
            DMA((2, planes, CHUNKS)),
            DMA((2, planes, CHUNKS)),
        ]
        + [one for _, _, scratch in held for one in scratch],
        compiler_params=comm_params(number),
        cost_estimate=busy(32),
        name="scatter_group",
    )(parts, *more)
    return results if more else results[0]


def gather_plane(rows, tall=None, swap=None, planes=None):
    count, width = rows.shape
    more, trades = tall is not None, swap is not None

    def kernel(x_ref, *refs):
        if more:
            w_ref, o_ref, t_ref, *refs = refs
            *refs, f_send, f_recv, f_own = refs
        elif trades:
            y_ref, o_ref, yo_ref, *refs = refs
            *refs, y_send, y_recv = refs
        else:
            o_ref, *refs = refs
        send, recv, sib_send, sib_recv, own = refs
        ring = Ring4()
        if more:
            barrier([peer[0] for peer in plane_peers()])
        elif trades:
            line_barrier(planes, [peer[0] for peer in plane_peers()], True)
            trade(y_ref, yo_ref, y_send, y_recv, lambda copy: copy.start())
        else:
            barrier([ring.dev(ring.rho + 1), ring.dev(ring.rho - 1), ring.sib_dev()])
        local = pltpu.make_async_copy(x_ref, o_ref.at[ring.slot(ring.rho)], own)
        local.start()
        ends = []

        def beside(turn):
            if turn == 1 and more:
                ends.append(hand_over(w_ref, t_ref, f_send, f_recv, f_own))

        ag_ring(ring, CHUNKS, x_ref, o_ref, send, recv, (sib_send, sib_recv), beside)
        local.wait()
        for end in ends:
            end()
        if trades:
            trade(y_ref, yo_ref, y_send, y_recv, lambda copy: copy.wait())

    shapes = [jax.ShapeDtypeStruct((8, count, width), BF16)]
    if more:
        shapes.append(jax.ShapeDtypeStruct(tall.shape, BF16))
    if trades:
        shapes.append(jax.ShapeDtypeStruct(swap.shape, BF16))
    results = pl.pallas_call(
        kernel,
        out_shape=shapes,
        in_specs=[VMEM_SPEC] * len(shapes),
        out_specs=[ANY_SPEC] + [VMEM_SPEC] * (len(shapes) - 1),
        scratch_shapes=[
            DMA((2, 2, CHUNKS)),
            DMA((2, 2, CHUNKS)),
            DMA((4, CHUNKS)),
            DMA((4, CHUNKS)),
            DMA,
        ]
        + [DMA((3,)), DMA((3,)), DMA] * more
        + [DMA, DMA] * trades,
        compiler_params=comm_params(10 if more else 16 if trades else 3),
        cost_estimate=busy(20),
        name="gather_plane",
    )(rows, *([tall] if more else []), *([swap] if trades else []))
    return results if more or trades else results[0]


def scatter_plane(parts, share=None):
    results = scatter_plane_call(parts, [], 1, 4 if share is None else 17, share)
    return results[0] if share is None else results


def scatter_plane_first(parts, slabs, out_weight, planes, share):
    return scatter_plane_call(parts, [out_weight, *slabs], planes, 9, share)


def scatter_plane_call(parts, beside, planes, number, share):
    _, count, width = parts.shape
    extra = len(beside)
    more, outs, sems = share_shapes(share)

    def kernel(p_ref, *refs):
        if more:
            w_ref, refs = refs[0], refs[1:]
        b_refs, o_ref, refs = refs[:extra], refs[extra], refs[extra + 1 :]
        if more:
            blocks, refs = refs[0], refs[1:]
        if extra:
            stores, refs = refs[:extra], refs[extra:]
        pair, buf, send, recv, sib_send, sib_recv, refs = *refs[:6], refs[6:]
        ring = Ring4()
        if extra:
            put, z_send, z_recv, *refs = refs
            line_barrier(planes, [peer[0] for peer in plane_peers()])
            if more:
                carried = carrier(share, w_ref, blocks, refs)
                carried.start()
            za = lax.axis_index("za")
            puts = [
                pltpu.make_async_copy(b_refs[i], stores[i].at[za], put.at[i]) for i in range(extra)
            ]
            for copy in puts:
                copy.start()
            line = LineGather(planes, stores, z_send, z_recv)
        else:
            barrier([ring.dev(ring.rho + 1), ring.dev(ring.rho - 1), ring.sib_dev()])

        def chip(r):
            x, b = ring.pos(r)
            return x * 2 + b

        copies = []
        for i in (2, 1, 3, 0):
            copy = rcopy(
                p_ref.at[ring.slot(ring.rho + i, True)],
                pair.at[chip(ring.rho + i)],
                sib_send.at[i],
                sib_recv.at[i],
                ring.sib_dev(),
            )
            copy.start()
            copies.append(copy)
        if more and not extra:
            carried = carrier(share, w_ref, blocks, refs)
            carried.start()
        if extra:
            for copy in puts:
                copy.wait()
            line.step(1)
        for i, copy in zip((2, 1, 3, 0), copies):
            place = chip(ring.rho + i)
            copy.wait_recv()
            pair[place] = (
                pair[place].astype(F32) + p_ref[ring.slot(ring.rho + i)].astype(F32)
            ).astype(BF16)
        if more and extra:
            carried.middle()

        def beside(turn):
            if extra:
                line.step(turn)
            elif more and turn == 2:
                carried.middle()

        rs_ring(ring, CHUNKS, pair, buf, send, recv, chip, beside)
        o_ref[...] = (
            buf[0, 1].astype(F32) + buf[1, 1].astype(F32)
        ) + pair[chip(ring.rho)].astype(F32)
        for copy in copies:
            copy.wait_send()
        if extra:
            for turn in range(4, planes):
                line.step(turn)
            line.finish()
        if more:
            carried.end()

    shapes, scratch = [], []
    if extra:
        shapes = [
            jax.ShapeDtypeStruct((planes,) + array.shape, BF16) for array in beside
        ]
        scratch = [
            DMA((extra,)),
            DMA((extra, 2, planes - 1)),
            DMA((extra, 2, planes - 1)),
        ]
    return pl.pallas_call(
        kernel,
        out_shape=[jax.ShapeDtypeStruct((count, width), F32)] + outs + shapes,
        in_specs=[VMEM_SPEC] + [ANY_SPEC] * len(more) + [VMEM_SPEC] * extra,
        out_specs=[VMEM_SPEC] + [ANY_SPEC] * len(more) + [VMEM_SPEC] * len(shapes),
        scratch_shapes=[
            pltpu.VMEM((4, count, width), BF16),
            pltpu.VMEM((2, 2, count, width), BF16),
            DMA((2, 2, CHUNKS)),
            DMA((2, 2, CHUNKS)),
            DMA((4,)),
            DMA((4,)),
        ]
        + scratch
        + sems,
        compiler_params=comm_params(number),
        cost_estimate=busy(20),
        name="scatter_plane_first" if extra else "scatter_plane",
    )(parts, *more, *beside)


def plane_peers():
    x, c, b = lax.axis_index("xh"), lax.axis_index("co"), lax.axis_index("yb")
    peers = []
    for k in range(1, 8):
        px = x + (k // 4) * (1 - 2 * x)
        pc = c + (k // 2 % 2) * (1 - 2 * c)
        pb = b + (k % 2) * (1 - 2 * b)
        peers.append(
            ({"xh": px, "co": pc, "yb": pb}, (px * 2 + pc) * 2 + pb, pb * 4 + px * 2 + pc)
        )
    return peers


def own_places():
    x, c, b = lax.axis_index("xh"), lax.axis_index("co"), lax.axis_index("yb")
    return (x * 2 + c) * 2 + b, b * 4 + x * 2 + c


def trade(source, target, send, recv, act):
    za = lax.axis_index("za")
    f = lax.axis_index("xh") * 2 + lax.axis_index("co")

    @pl.when(za != f)
    def _():
        act(rcopy(source, target, send, recv, swap_partner()))

    @pl.when(za == f)
    def _():
        act(pltpu.make_async_copy(source, target, send))


def swap_partner():
    za = lax.axis_index("za")
    f = lax.axis_index("xh") * 2 + lax.axis_index("co")
    return {"za": f, "xh": za // 2, "co": lax.rem(za, 2)}


def line_barrier(planes, devices, swaps=False, line=True):
    za = lax.axis_index("za")
    f = lax.axis_index("xh") * 2 + lax.axis_index("co")
    sem = pltpu.get_barrier_semaphore()
    for device in devices:
        pl.semaphore_signal(sem, inc=1, device_id=device, device_id_type=MESH)

    below, above = 0, 0
    if line:

        @pl.when(za > 0)
        def _():
            pl.semaphore_signal(sem, inc=1, device_id={"za": za - 1}, device_id_type=MESH)

        @pl.when(za < planes - 1)
        def _():
            pl.semaphore_signal(sem, inc=1, device_id={"za": za + 1}, device_id_type=MESH)

        below, above = (za + planes - 1) // planes, (2 * planes - 2 - za) // planes
    apart = 0
    if swaps:

        @pl.when(za != f)
        def _():
            pl.semaphore_signal(sem, inc=1, device_id=swap_partner(), device_id_type=MESH)

        apart = ((za - f) * (za - f) + 8) // 9
    pl.semaphore_wait(sem, len(devices) + below + above + apart)


class LineGather:
    def __init__(self, planes, stores, send, recv):
        self.planes, self.stores, self.send, self.recv = planes, stores, send, recv
        self.za = lax.axis_index("za")

    def copy(self, i, d, s):
        sign = 1 - 2 * d
        block = self.za - (s - 1) * sign
        return rcopy(
            self.stores[i].at[block],
            self.stores[i].at[block],
            self.send.at[i, d, s - 1],
            self.recv.at[i, d, s - 1],
            {"za": self.za + sign},
        )

    def sends(self, d, s):
        za, last = self.za, self.planes - 1
        if d == 0:
            return (za < last) & (za >= s - 1)
        return (za > 0) & (za <= last - (s - 1))

    def step(self, s):
        for i in range(len(self.stores)):
            for d in (0, 1):
                if s > 1:
                    self.wait_arrival(i, d, s - 1)

                @pl.when(self.sends(d, s))
                def _():
                    self.copy(i, d, s).start()

    def wait_arrival(self, i, d, s):
        za, last, sign = self.za, self.planes - 1, 1 - 2 * d
        has = (za >= s) if d == 0 else (za <= last - s)

        @pl.when(has)
        def _():
            block = za - s * sign
            ref = self.stores[i].at[block]
            rcopy(
                ref, ref, self.send.at[i, d, s - 1], self.recv.at[i, d, s - 1],
                {"za": za - sign},
            ).wait_recv()

    def finish(self):
        for i in range(len(self.stores)):
            for d in (0, 1):
                self.wait_arrival(i, d, self.planes - 1)
        self.finish_sends()

    def finish_sends(self):
        for i in range(len(self.stores)):
            for d in (0, 1):
                for s in range(1, self.planes):

                    @pl.when(self.sends(d, s))
                    def _():
                        self.copy(i, d, s).wait_send()


def flat_peers():
    x, c = lax.axis_index("xh"), lax.axis_index("co")
    peers = []
    for k in (1, 2, 3):
        px = x + (k // 2) * (1 - 2 * x)
        pc = c + (k % 2) * (1 - 2 * c)
        peers.append(({"xh": px, "co": pc}, px * 2 + pc))
    return peers, x * 2 + c


def hand_over(stage, target, send, recv, own):
    peers, mine = flat_peers()
    copies = []
    for k, (device, f) in enumerate(peers):
        copies.append(rcopy(stage.at[f], target.at[mine], send.at[k], recv.at[k], device))
        copies[-1].start()
    keep = pltpu.make_async_copy(stage.at[mine], target.at[mine], own)
    keep.start()
    return lambda: hand_over_end(peers, target, send, recv, keep, copies)


def hand_over_end(peers, target, send, recv, keep, copies):
    keep.wait()
    for k, (device, f) in enumerate(peers):
        ref = target.at[f]
        rcopy(ref, ref, send.at[k], recv.at[k], device).wait_recv()
    for copy in copies:
        copy.wait_send()


def enter(tokens, heads_part, other_part, out_weight, others, gain_lane, planes, share):
    count, width = tokens.shape
    more, outs, sems = share_shapes(share)
    also = len(others)
    layers, rows = heads_part.shape[1:3]
    extra = layers - 1

    def kernel(x_ref, a_ref, b_ref, w_ref, *refs):
        y_refs, refs = refs[:also], refs[also:]
        if more:
            s_ref, refs = refs[0], refs[1:]
        o_ref, stream_ref, t_ref, a_out, b_out, refs = *refs[:5], refs[5:]
        a_late, b_late, refs = refs[:extra], refs[extra : 2 * extra], refs[2 * extra :]
        y_outs, refs = refs[:also], refs[also:]
        if more:
            blocks, refs = refs[0], refs[1:]
        (
            stage, normed, swap_send, swap_recv, send, recv, own, ring_send, ring_recv, sib_send,
            sib_recv, put, za_send, za_recv, f_send, f_recv, *rest
        ) = refs
        za = lax.axis_index("za")
        x, c = lax.axis_index("xh"), lax.axis_index("co")
        f = x * 2 + c
        partner = swap_partner()
        ring = Ring4()
        peers = plane_peers()
        group, place = own_places()
        line_barrier(planes, [peer[0] for peer in peers], True)

        trades = [(x_ref, stream_ref), *zip(y_refs, y_outs)]

        def trade(i, act):
            source, target = trades[i]

            @pl.when(za != f)
            def _():
                act(rcopy(source, target, swap_send.at[i], swap_recv.at[i], partner))

            @pl.when(za == f)
            def _():
                act(pltpu.make_async_copy(source, target, swap_send.at[i]))

        trade(0, lambda copy: copy.start())

        copies = []

        def target(kind, layer, at):
            if layer == 0:
                return (a_out, b_out)[kind].at[za, at]
            return (a_late, b_late)[kind][layer - 1].at[at]

        def scatter(kind, layer):
            source = (a_ref, b_ref)[kind]
            for k, (device, their_group, _) in enumerate(peers):
                copy = rcopy(
                    source.at[their_group, layer], target(kind, layer, place),
                    send.at[kind, layer, k], recv.at[kind, layer, k], device,
                )
                copy.start()
                copies.append(copy)
            local = pltpu.make_async_copy(
                source.at[group, layer], target(kind, layer, place), own.at[kind * layers + layer]
            )
            local.start()
            return local

        def arrivals(kind, layer, local):
            for k, (device, _, their_place) in enumerate(peers):
                ref = target(kind, layer, their_place)
                rcopy(
                    ref, ref, send.at[kind, layer, k], recv.at[kind, layer, k], device
                ).wait_recv()
            local.wait()

        w_put = pltpu.make_async_copy(w_ref, stage.at[za], put)
        w_put.start()
        b_local = scatter(1, 0)
        a_local = scatter(0, 0)
        if more:
            carried = carrier(share, s_ref, blocks, rest)
            carried.start()
        tall = LineGather(planes, [stage], za_send.at[pl.ds(2, 1)], za_recv.at[pl.ds(2, 1)])
        small = LineGather(planes, [b_out], za_send.at[pl.ds(0, 1)], za_recv.at[pl.ds(0, 1)])
        line = LineGather(planes, [a_out], za_send.at[pl.ds(1, 1)], za_recv.at[pl.ds(1, 1)])
        arrivals(1, 0, b_local)
        for turn in range(1, planes):
            small.step(turn)
        w_put.wait()
        tall.step(1)
        arrivals(0, 0, a_local)
        line.step(1)
        for d in (0, 1):
            small.wait_arrival(0, d, planes - 1)
        if more:
            carried.middle()
        columns = b_out[...].reshape(width, 128).astype(F32)
        gain = columns.T[gain_lane : gain_lane + 1, :]

        trade(0, lambda copy: copy.wait())
        for i in range(1, 1 + also):
            trade(i, lambda copy: copy.start())
        stream = stream_ref[...].astype(F32)
        factor = lax.rsqrt(jnp.mean(stream * stream, axis=1, keepdims=True) + EPSILON)
        normed[...] = (stream * factor * gain).astype(BF16)
        local = pltpu.make_async_copy(normed, o_ref.at[ring.slot(ring.rho)], own.at[2 * layers])
        local.start()
        ends = []

        def beside(turn):
            if turn <= 2:
                tall.step(turn + 1)
                line.step(turn + 1)
            if turn == 2:
                for layer in range(1, layers):
                    for kind in (1, 0):
                        ends.append((kind, layer, scatter(kind, layer)))

        ag_ring(ring, CHUNKS, normed, o_ref, ring_send, ring_recv, (sib_send, sib_recv), beside)
        for turn in range(4, planes):
            tall.step(turn)
            line.step(turn)
        tall.finish()
        handed = hand_over(stage, t_ref, f_send, f_recv, own.at[2 * layers + 1])
        local.wait()
        line.finish()
        small.finish_sends()
        for kind, layer, local in ends:
            arrivals(kind, layer, local)
        for copy in copies:
            copy.wait_send()
        handed()
        for i in range(1, 1 + also):
            trade(i, lambda copy: copy.wait())
        if more:
            carried.end()

    late = [
        jax.ShapeDtypeStruct((8, rows, part.shape[-1]), BF16)
        for part in (heads_part, other_part)
        for _ in range(extra)
    ]
    results = pl.pallas_call(
        kernel,
        out_shape=[
            jax.ShapeDtypeStruct((8, count, width), BF16),
            jax.ShapeDtypeStruct((count, width), BF16),
            jax.ShapeDtypeStruct((4,) + out_weight.shape, BF16),
            jax.ShapeDtypeStruct((planes, 8, rows, heads_part.shape[-1]), BF16),
            jax.ShapeDtypeStruct((planes, 8, rows, other_part.shape[-1]), BF16),
        ]
        + late
        + [jax.ShapeDtypeStruct(array.shape, array.dtype) for array in others]
        + outs,
        in_specs=[VMEM_SPEC] * (4 + also) + [ANY_SPEC] * len(more),
        out_specs=[GATHERED_SPEC] + [VMEM_SPEC] * (4 + len(late) + also) + [ANY_SPEC] * len(more),
        scratch_shapes=[
            pltpu.VMEM((planes,) + out_weight.shape, BF16),
            pltpu.VMEM((count, width), BF16),
            DMA((1 + also,)),
            DMA((1 + also,)),
            DMA((2, layers, 7)),
            DMA((2, layers, 7)),
            DMA((2 * layers + 2,)),
            DMA((2, 2, CHUNKS)),
            DMA((2, 2, CHUNKS)),
            DMA((4, CHUNKS)),
            DMA((4, CHUNKS)),
            DMA,
            DMA((3, 2, planes - 1)),
            DMA((3, 2, planes - 1)),
            DMA((3,)),
            DMA((3,)),
        ]
        + sems,
        compiler_params=comm_params(5),
        cost_estimate=busy(40),
        name="enter",
    )(tokens, heads_part, other_part, out_weight, *others, *more)
    first, rest = results[:5], results[5:]
    late_heads, late_others, rest = rest[:extra], rest[extra : 2 * extra], rest[2 * extra :]
    return first, late_heads, late_others, rest[:also], rest[also:]


def collect(wide, tall, planes, shares=(), weights=None, tokens=None):
    layers = len(wide)
    count, width = wide[0].shape[2:]
    depth = tall[0].shape[2]
    held = [share_shapes(share) for share in shares]
    more = [array for arrays, _, _ in held for array in arrays]
    more_outs = [shape for _, shapes, _ in held for shape in shapes]
    last_stage = weights is not None
    sizes = [array.shape[2] for array in weights] if last_stage else []

    def kernel(*refs):
        w_in, refs = refs[:layers], refs[layers:]
        t_in, refs = refs[:layers], refs[layers:]
        own_refs, refs = refs[: len(sizes)], refs[len(sizes) :]
        if last_stage:
            x_ref, refs = refs[0], refs[1:]
        g_in, refs = refs[: len(more)], refs[len(more) :]
        f_out, refs = refs[: 2 + len(sizes)], refs[(2 + len(sizes)) * last_stage :]
        if last_stage:
            y_ref, refs = refs[0], refs[1:]
            g_out, refs = refs[: len(more)], refs[len(more) :]
        w_out, refs = refs[:layers], refs[layers:]
        t_out, refs = refs[:layers], refs[layers:]
        if not last_stage:
            g_out, refs = refs[: len(more)], refs[len(more) :]
        w_up, t_own, t_up, summed, own, f_send, f_recv, z_send, z_recv, p_send, p_recv, *rest = refs
        za = lax.axis_index("za")
        x, c = lax.axis_index("xh"), lax.axis_index("co")
        mine = x * 2 + c
        peers = plane_peers()
        f = x * 2 + c
        line_barrier(planes, [peer[0] for peer in peers], last_stage)
        group, place = own_places()
        if last_stage:
            swap_send, swap_recv, *rest = rest

        def trade(act):
            @pl.when(za != f)
            def _():
                act(rcopy(x_ref, y_ref, swap_send, swap_recv, swap_partner()))

            @pl.when(za == f)
            def _():
                act(pltpu.make_async_copy(x_ref, y_ref, swap_send))

        if last_stage:
            trade(lambda copy: copy.start())
        carried = []
        for i, share in enumerate(shares):
            some, rest = rest[: len(held[i][2])], rest[len(held[i][2]) :]
            carried.append(carrier(share, g_in[i], g_out[i], some))
            carried[-1].start()
        firsts, keeps = [], []
        for l in range(layers):
            for k in (1, 2, 3):
                px = x + (k // 2) * (1 - 2 * x)
                pc = c + (k % 2) * (1 - 2 * c)
                copy = rcopy(
                    t_in[l].at[px * 2 + pc], t_own.at[l, mine], f_send.at[l, k - 1],
                    f_recv.at[l, k - 1], {"xh": px, "co": pc},
                )
                copy.start()
                firsts.append(copy)
            keep = pltpu.make_async_copy(t_in[l].at[mine], t_own.at[l, mine], own.at[l])
            keep.start()
            keeps.append(keep)

        def arrive(l):
            for k in (1, 2, 3):
                px = x + (k // 2) * (1 - 2 * x)
                pc = c + (k % 2) * (1 - 2 * c)
                ref = t_own.at[l, px * 2 + pc]
                rcopy(
                    ref, ref, f_send.at[l, k - 1], f_recv.at[l, k - 1], {"xh": px, "co": pc}
                ).wait_recv()
            keeps[l].wait()

        def parts(l, kind):
            if kind == 0:
                return w_in[l], w_up.at[l]
            return t_own.at[l], t_up.at[l]

        def along(l, kind, d, dest):
            _, came = parts(l, kind)
            ref = came.at[d, dest]
            return ref, rcopy(
                ref, ref, z_send.at[l, kind, d, dest], z_recv.at[l, kind, d, dest],
                {"za": za + (1 - 2 * d)},
            )

        last = planes - 1
        def pass_on(l, kind, d, dest):
            held, came = parts(l, kind)
            sends = (za < dest) if d == 0 else (za > dest)
            inner = (za > 0) if d == 0 else (za < last)
            ref, copy = along(l, kind, d, dest)

            @pl.when(sends & inner)
            def _():
                copy.wait_recv()
                came[d, dest] = (
                    came[d, dest].astype(F32) + held[dest].astype(F32)
                ).astype(BF16)
                copy.start()

            @pl.when(sends & jnp.logical_not(inner))
            def _():
                rcopy(
                    held.at[dest], ref, z_send.at[l, kind, d, dest],
                    z_recv.at[l, kind, d, dest], {"za": za + (1 - 2 * d)},
                ).start()

        for far in range(last):
            for kind in (0, 1):
                if kind == 1 and far == 0:
                    for l in range(layers):
                        arrive(l)
                for l in reversed(range(layers)):
                    for d in (0, 1):
                        pass_on(l, kind, d, last - far if d == 0 else far)
            if far < len(carried):
                carried[far].middle()

        def total(l, kind, result):
            _, came = parts(l, kind)
            for d in (0, 1):

                @pl.when((za > 0) if d == 0 else (za < last))
                def _():
                    ref = came.at[d, za]
                    rcopy(
                        ref, ref, z_send.at[l, kind, d, za], z_recv.at[l, kind, d, za],
                        {"za": za - (1 - 2 * d)},
                    ).wait_recv()
                    result[...] = (result[...].astype(F32) + came[d, za].astype(F32)).astype(BF16)

        def finish_layer(l):
            heads = [w_out[l][h].astype(F32) for h in range(8)]
            start, product = 0, jnp.zeros((count, 1), F32)
            for i, size in enumerate(sizes):
                stop = start + size // 8
                made = jnp.concatenate([head[:, start:stop] for head in heads], axis=1)
                f_out[i][l] = made
                product = product + jnp.sum(own_refs[i][l].astype(F32) * made, axis=1, keepdims=True)
                start = stop
            f_out[len(sizes)][l] = t_out[l][...].astype(F32)
            rest = sum(heads[1:], heads[0])[:, width - 128 :]
            rest = pltpu.roll(rest, 64, 1) + pltpu.roll(rest, 32, 1)
            lanes = lax.broadcasted_iota(jnp.int32, rest.shape, 1)
            f_out[len(sizes) + 1][l] = jnp.where(lanes == 32, product, rest)

        outs = []
        for l in reversed(range(layers)):
            summed[l] = w_in[l][za]
            total(l, 0, summed.at[l])
            for k, (device, _, their_place) in enumerate(peers):
                copy = rcopy(
                    summed.at[l, their_place], w_out[l].at[group], p_send.at[l, k],
                    p_recv.at[l, k], device,
                )
                copy.start()
                outs.append(copy)
            w_out[l][group] = summed[l, place]
        for l in reversed(range(layers)):
            t_out[l][...] = t_own[l, za]
            total(l, 1, t_out[l])
        for l in reversed(range(layers)):
            for k, (device, their_group, _) in enumerate(peers):
                ref = w_out[l].at[their_group]
                rcopy(ref, ref, p_send.at[l, k], p_recv.at[l, k], device).wait_recv()
        for copy in firsts + outs:
            copy.wait_send()
        for kind in (0, 1):
            for l in range(layers):
                for d in (0, 1):
                    for far in range(last):
                        dest = last - far if d == 0 else far

                        @pl.when((za < dest) if d == 0 else (za > dest))
                        def _():
                            along(l, kind, d, dest)[1].wait_send()

        if last_stage:
            trade(lambda copy: copy.wait())
            for l in range(layers):
                finish_layer(l)
        for one in carried:
            one.end()

    final_outs, plain_outs, plain_scratch = [], [], []
    sums = [((8, count, width), BF16)] * layers + [((count, depth), BF16)] * layers
    if last_stage:
        final_outs = [
            jax.ShapeDtypeStruct((layers, count, size), F32) for size in [*sizes, depth, 128]
        ] + [jax.ShapeDtypeStruct(tokens.shape, BF16)]
        plain_scratch = [pltpu.VMEM(*one) for one in sums]
    else:
        plain_outs = [jax.ShapeDtypeStruct(*one) for one in sums]
    return pl.pallas_call(
        kernel,
        out_shape=final_outs + plain_outs + more_outs,
        in_specs=[VMEM_SPEC] * (2 * layers + len(sizes) + last_stage) + [ANY_SPEC] * len(more),
        out_specs=[VMEM_SPEC] * len(final_outs + plain_outs) + [ANY_SPEC] * len(more),
        scratch_shapes=plain_scratch
        + [
            pltpu.VMEM((layers, 2, planes, 8, count, width), BF16),
            pltpu.VMEM((layers, 4, count, depth), BF16),
            pltpu.VMEM((layers, 2, planes, count, depth), BF16),
            pltpu.VMEM((layers, 8, count, width), BF16),
            DMA((layers,)),
            DMA((layers, 3)),
            DMA((layers, 3)),
            DMA((layers, 2, 2, planes)),
            DMA((layers, 2, 2, planes)),
            DMA((layers, 7)),
            DMA((layers, 7)),
        ]
        + [DMA, DMA] * last_stage
        + [one for _, _, scratch in held for one in scratch],
        compiler_params=comm_params(7, 58),
        cost_estimate=busy(40),
        name="collect",
    )(*wide, *tall, *(weights or []), *([tokens] if last_stage else []), *more)


def row_codes(code_rows, first, local, slots, weights=None):
    blocks = []
    for e in range(local):
        code = code_rows(first + e)
        ids = lax.broadcasted_iota(jnp.int32, (slots, code.shape[1]), 0).astype(F32)
        value = 1.0 if weights is None else weights(first + e)
        blocks.append(jnp.where(ids == code, value, 0.0))
    return jnp.concatenate(blocks, axis=0).astype(BF16)


def column_codes(code, first, local, slots, weights=None):
    lanes = lax.broadcasted_iota(jnp.int32, code.shape, 1)
    blocks = []
    for e in range(local):
        chosen = lanes == first + e
        column = jnp.sum(jnp.where(chosen, code, 0.0), axis=1, keepdims=True)
        ids = lax.broadcasted_iota(jnp.int32, (code.shape[0], slots), 1).astype(F32)
        value = 1.0
        if weights is not None:
            value = jnp.sum(jnp.where(chosen, weights, 0.0), axis=1, keepdims=True)
        blocks.append(jnp.where(ids == column, value, 0.0))
    return jnp.concatenate(blocks, axis=1).astype(BF16)


def dot(a, b):
    return jnp.dot(a, b, preferred_element_type=F32)


def dot_t(a, b):
    return lax.dot_general(a, b, (((1,), (1,)), ((), ())), preferred_element_type=F32)


def plain_params(megabytes, number=None):
    return pltpu.CompilerParams(
        vmem_limit_bytes=megabytes << 20,
        dimension_semantics=("arbitrary",),
        collective_id=number,
        has_side_effects=number is not None,
    )


def once(shape):
    return pl.BlockSpec(shape, lambda e: (0,) * len(shape), pipeline_mode=pl.Buffered(1))


def per_expert(shape):
    return pl.BlockSpec((1,) + shape, lambda e: (e,) + (0,) * len(shape))


def shares_of_expert(shape):
    return pl.BlockSpec((shape[0], 1) + shape[2:], lambda e: (0, e, 0, 0))


def side_by_side(ref):
    return jnp.concatenate([ref[i, 0] for i in range(ref.shape[0])], axis=1)


def experts_forward(normed, codes, router, gate_w, up_w, down_w, beside, slots, planes, number, share=None):
    blocks, count, width = normed.shape
    _, local, _, hidden_size = gate_w.shape
    more, extra_outs, sems = share_shapes(share)
    lines = local * slots
    halves = 2
    span = blocks // halves

    def kernel(
        n_ref, c_ref, r_ref, gw_ref, uw_ref, dw_ref, x_ref, *refs
    ):
        if more:
            s_ref, refs = refs[0], refs[1:]
        out, g_out, u_out, p_out, pt_out, b_out, *refs = refs
        if more:
            carried = carrier(share, s_ref, refs[0], refs[7:])
            refs = refs[1:]
        rows, back, codes_t, send, recv, own = refs[:6]
        e = pl.program_id(0)
        ring = Ring8(planes)
        gather = RingGather(ring, 2, x_ref, b_out, send, recv)
        keep = pltpu.make_async_copy(x_ref, b_out.at[ring.slot(ring.rho)], own)
        first = (lax.axis_index("za") * 2 + lax.axis_index("yb")) * local

        @pl.when(e == 0)
        def _():
            devices = [ring.dev(ring.rho + 1), ring.dev(ring.rho - 1)]
            barrier(devices + share_devices() * len(more))
            keep.start()
            gather.step(1)
            if more:
                carried.start()

            @pl.loop(0, blocks)
            def _(b):
                tokens = n_ref[b]
                logits = pltpu.roll(dot(tokens, r_ref[...]), 128 - HEAD_SIZE, 1)
                code = c_ref[b].astype(F32)
                codes_t[...] = code.T
                routed = code >= 0.0
                highest = jnp.max(jnp.where(routed, logits, -1e30), axis=1, keepdims=True)
                raised = jnp.where(routed, jnp.exp(logits - highest), 0.0)
                probs = raised / jnp.sum(raised, axis=1, keepdims=True)
                p_out[b] = probs
                pt_out[b] = probs.T[: pt_out.shape[1]]
                back[b] = column_codes(code, first, local, slots, probs)
                ones = row_codes(lambda i: codes_t[pl.ds(i, 1), :], first, local, slots)
                rows[b] = dot(ones, tokens).astype(BF16)

            gather.step(2)
            if more:
                carried.middle()

        mine = pl.ds(pl.multiple_of(e * slots, slots), slots)
        for h in range(halves):
            part = pl.ds(h * span, span)
            held = rows[part, mine, :].reshape(span * slots, width)
            gate = dot(held, gw_ref[:, 0].reshape(width, hidden_size))
            up = dot(held, uw_ref[:, 0].reshape(width, hidden_size))
            at = pl.ds(h * span * slots, span * slots)
            g_out[0, at, :] = gate
            u_out[0, at, :] = up
            hidden = (gate * jax.nn.sigmoid(gate) * up).astype(BF16)
            made = dot(hidden, side_by_side(dw_ref)).astype(BF16)
            rows[part, mine, :] = made.reshape(span, slots, width)

        for turn in range(3, planes + 1):

            @pl.when(e == min(turn - 3, local - 1))
            def _():
                gather.step(turn)

        @pl.when(e == local - 1)
        def _():
            @pl.loop(0, blocks)
            def _(b):
                out[b] = dot(back[b], rows[b]).astype(BF16)

            gather.finish()
            keep.wait()
            if more:
                carried.end()

    wide = (local, blocks * slots, hidden_size)
    return pl.pallas_call(
        kernel,
        grid=(local,),
        out_shape=[
            jax.ShapeDtypeStruct(normed.shape, BF16),
            jax.ShapeDtypeStruct(wide, F32),
            jax.ShapeDtypeStruct(wide, F32),
            jax.ShapeDtypeStruct(codes.shape, F32),
            jax.ShapeDtypeStruct((blocks, 32, count), F32),
            jax.ShapeDtypeStruct((blocks,) + beside.shape, BF16),
        ]
        + extra_outs,
        in_specs=[
            once(normed.shape),
            once(codes.shape),
            once(router.shape),
            shares_of_expert(gate_w.shape),
            shares_of_expert(up_w.shape),
            shares_of_expert(down_w.shape),
            ANY_SPEC,
        ]
        + [ANY_SPEC] * len(more),
        out_specs=[
            once(normed.shape),
            per_expert(wide[1:]),
            per_expert(wide[1:]),
            once(codes.shape),
            once((blocks, 32, count)),
            ANY_SPEC,
        ]
        + [ANY_SPEC] * len(more),
        scratch_shapes=[
            pltpu.VMEM((blocks, lines, width), BF16),
            pltpu.VMEM((blocks, count, lines), BF16),
            pltpu.VMEM((codes.shape[2], count), F32),
            DMA((2, planes, 2)),
            DMA((2, planes, 2)),
            DMA,
        ]
        + sems,
        compiler_params=plain_params(56, number),
        cost_estimate=busy(16),
        name="experts_forward",
    )(normed, codes, router, gate_w, up_w, down_w, beside, *more)


def experts_backward(
    normed, arrived, codes, probs_t, gate_w, up_w, down_w, gate_part, up_part, slots, shares,
    late=None, planes=None, share=None, swap=None,
):
    blocks, count, width = normed.shape
    pieces = len(arrived)
    more = [] if late is None else [late]
    shared, shared_outs, shared_scratch = share_shapes(share)
    swaps = [] if swap is None else [swap]
    _, local, _, hidden_size = gate_w.shape
    lines = local * slots
    total = blocks * slots
    band = width // shares
    split = band % 128 == 0

    def kernel(
        n_ref, c_ref, pt_ref, gw_ref, uw_ref, dw_ref, g_ref, u_ref, *refs
    ):
        a_refs, refs = refs[:pieces], refs[pieces:]
        if more:
            l_ref, refs = refs[0], refs[1:]
        w_ref, refs = refs[: len(shared)], refs[len(shared) :]
        y_ref, refs = refs[: len(swaps)], refs[len(swaps) :]
        out, dg_out, du_out, dd_out, *refs = refs
        if more:
            l_out, refs = refs[0], refs[1:]
        b_ref, refs = refs[: len(shared)], refs[len(shared) :]
        yo_ref, refs = refs[: len(swaps)], refs[len(swaps) :]
        rows, outs, back, marks, codes_t, *refs = refs
        if more:
            ring = Ring8(planes)
            scatter = RingScatter(ring, 2, l_ref, *refs)
        if swaps:
            swap_send, swap_recv, *refs = refs
        if shared:
            carried = carrier(share, w_ref[0], b_ref[0], refs)
        e = pl.program_id(0)
        first = (lax.axis_index("za") * 2 + lax.axis_index("yb")) * local

        @pl.when(e == 0)
        def _():
            if more:
                barrier([ring.dev(ring.rho + 1), ring.dev(ring.rho - 1)])
                scatter.step(1)
            if swaps or shared:
                line_barrier(planes, share_devices(), len(swaps) > 0, False)
            if shared:
                carried.start()
            if swaps:
                trade(y_ref[0], yo_ref[0], swap_send, swap_recv, lambda copy: copy.start())

            @pl.loop(0, blocks)
            def _(b):
                codes_t[...] = c_ref[b].astype(F32).T

                def code(i):
                    return codes_t[pl.ds(i, 1), :]

                def prob(i):
                    return pt_ref[b, pl.ds(i, 1), :]

                back[b] = column_codes(c_ref[b].astype(F32), first, local, slots)
                rows[b] = dot(row_codes(code, first, local, slots), n_ref[b]).astype(BF16)
                upstream = jnp.concatenate([ref[b] for ref in a_refs], axis=0)
                outs[b] = dot(row_codes(code, first, local, slots, prob), upstream).astype(BF16)

            if more:
                scatter.step(2)
            if shared:
                carried.middle()

        mine = pl.ds(pl.multiple_of(e * slots, slots), slots)
        upstream = outs[:, mine, :].reshape(total, width)
        hidden_grad = dot_t(upstream, side_by_side(dw_ref))
        gate, up = g_ref[0], u_ref[0]
        logistic = jax.nn.sigmoid(gate)
        hidden = (gate * logistic * up).astype(BF16)
        gate_low = (hidden_grad * up * logistic * (1.0 + gate * (1.0 - logistic))).astype(BF16)
        up_low = (hidden_grad * gate * logistic).astype(BF16)
        weighted = jnp.sum(hidden.astype(F32) * hidden_grad, axis=1, keepdims=True)
        high = weighted.astype(BF16).astype(F32)
        lanes = lax.broadcasted_iota(jnp.int32, (total, 128), 1)
        mark = jnp.where(lanes == first + e, high, 0.0)
        mark = mark + jnp.where(lanes == first + e + 64, weighted - high, 0.0)
        marks[:, mine, :] = mark.astype(BF16).reshape(blocks, slots, 128)
        turned = rows[:, mine, :].reshape(total, width).T
        for f in range(shares):
            cut = turned[f * band : (f + 1) * band]
            dg_out[f, 0] = dot(cut, gate_low).astype(BF16)
            du_out[f, 0] = dot(cut, up_low).astype(BF16)
        down = dot(hidden.T, upstream).astype(BF16)
        if split:
            for f in range(shares):
                dd_out[f, 0] = down[:, f * band : (f + 1) * band]
        else:
            dd_out[0] = down
        back_rows = dot_t(gate_low, gw_ref[:, 0].reshape(width, hidden_size))
        back_rows = back_rows + dot_t(up_low, uw_ref[:, 0].reshape(width, hidden_size))
        rows[:, mine, :] = back_rows.astype(BF16).reshape(blocks, slots, width)

        if more:
            for turn in range(3, planes + 1):

                @pl.when(e == min(turn - 3, local - 1))
                def _():
                    scatter.step(turn)

        @pl.when(e == local - 1)
        def _():
            if more:
                l_out[...] = scatter.finish()
            if shared:
                carried.end()
            if swaps:
                trade(y_ref[0], yo_ref[0], swap_send, swap_recv, lambda copy: copy.wait())

            @pl.loop(0, blocks)
            def _(b):
                out[b, :, :width] = dot(back[b], rows[b]).astype(BF16)
                out[b, :, width:] = dot(back[b], marks[b]).astype(BF16)

    cut_shape = (shares, local, band, hidden_size)
    cut_spec = pl.BlockSpec((shares, 1, band, hidden_size), lambda e: (0, e, 0, 0))
    if split:
        down_shape = (shares, local, hidden_size, band)
        down_spec = pl.BlockSpec((shares, 1, hidden_size, band), lambda e: (0, e, 0, 0))
    else:
        down_shape = (local, hidden_size, width)
        down_spec = per_expert(down_shape[1:])
    late_scratch = []
    if more:
        late_scratch = [
            pltpu.VMEM((2, planes, count, width), BF16),
            pltpu.VMEM((2, count, width), BF16),
            DMA((2, planes, 2)),
            DMA((2, planes, 2)),
            DMA((2,)),
        ]
    results = pl.pallas_call(
        kernel,
        grid=(local,),
        out_shape=[
            jax.ShapeDtypeStruct((blocks, count, width + 128), BF16),
            jax.ShapeDtypeStruct(cut_shape, BF16),
            jax.ShapeDtypeStruct(cut_shape, BF16),
            jax.ShapeDtypeStruct(down_shape, BF16),
        ]
        + [jax.ShapeDtypeStruct((count, width), F32)] * len(more)
        + shared_outs
        + [jax.ShapeDtypeStruct(array.shape, BF16) for array in swaps],
        in_specs=[
            once(normed.shape),
            once(codes.shape),
            once(probs_t.shape),
            shares_of_expert(gate_w.shape),
            shares_of_expert(up_w.shape),
            shares_of_expert(down_w.shape),
            per_expert(gate_part.shape[1:]),
            per_expert(up_part.shape[1:]),
        ]
        + [once(array.shape) for array in arrived]
        + [ANY_SPEC] * (len(more) + len(shared) + len(swaps)),
        out_specs=[once((blocks, count, width + 128)), cut_spec, cut_spec, down_spec]
        + [once((count, width))] * len(more)
        + [ANY_SPEC] * (len(shared) + len(swaps)),
        scratch_shapes=[
            pltpu.VMEM((blocks, lines, width), BF16),
            pltpu.VMEM((blocks, lines, width), BF16),
            pltpu.VMEM((blocks, count, lines), BF16),
            pltpu.VMEM((blocks, lines, 128), BF16),
            pltpu.VMEM((codes.shape[2], count), F32),
        ]
        + late_scratch
        + [DMA, DMA] * len(swaps)
        + shared_scratch,
        compiler_params=plain_params(62, 15 if more else 19 if shared or swaps else None),
        cost_estimate=busy(30),
        name="experts_backward",
    )(normed, codes, probs_t, gate_w, up_w, down_w, gate_part, up_part, *arrived, *more, *shared, *swaps)
    row_sums, gate_term, up_term, down_term, *added = results
    if not split:
        down_term = jnp.moveaxis(
            down_term.reshape(local, hidden_size, shares, band), 2, 0
        )
    return row_sums, gate_term, up_term, down_term, *added


GROUP = 4 * HEAD_SIZE


def turn_heads(values, cosine, sine, sign):
    half = HEAD_SIZE // 2
    lanes = lax.broadcasted_iota(jnp.int32, values.shape, 1)
    first = lax.rem(lanes, HEAD_SIZE) < half
    other = jnp.where(
        first, -pltpu.roll(values, GROUP - half, 1), pltpu.roll(values, half, 1)
    )
    return values * cosine + sign * other * sine


def spread_head(values, place):
    lanes = lax.broadcasted_iota(jnp.int32, values.shape, 1) // HEAD_SIZE
    alone = jnp.where(lanes == place, values, jnp.zeros_like(values))
    return (
        alone
        + pltpu.roll(alone, HEAD_SIZE, 1)
        + pltpu.roll(alone, 2 * HEAD_SIZE, 1)
        + pltpu.roll(alone, 3 * HEAD_SIZE, 1)
    )


def only_head(values, h):
    lanes = lax.broadcasted_iota(jnp.int32, values.shape, 1) // HEAD_SIZE
    return jnp.where(lanes == h, values, jnp.zeros_like(values))


def may_attend(starts_ref, first, rows, stop):
    here = first + lax.broadcasted_iota(jnp.int32, (rows, 1), 0)
    there = lax.broadcasted_iota(jnp.int32, (1, stop), 1)
    mine, theirs = jnp.zeros_like(here), jnp.zeros_like(there)
    for i in range(starts_ref.shape[1]):
        start = starts_ref[0, i]
        mine = mine + jnp.where(here >= start, 1, 0)
        theirs = theirs + jnp.where(there >= start, 1, 0)
    return (mine == theirs) & (there <= here)


def probabilities(query_rows, keys, allowed):
    scores = jnp.where(allowed, dot_t(query_rows, keys) * (1.0 / math.sqrt(HEAD_SIZE)), -1e30)
    weights = jnp.exp(scores - jnp.max(scores, axis=1, keepdims=True))
    return weights / jnp.sum(weights, axis=1, keepdims=True)


SMEM_SPEC = pl.BlockSpec(memory_space=pltpu.SMEM)
ROWS = 256


def attention_forward(normed, slab, out_rows, starts, cosine, sine):
    length, width = normed.shape
    rows = min(ROWS, length)

    def kernel(starts_ref, x_ref, w_ref, wv_ref, o_ref, c_ref, s_ref, out, heads, values, mixed, keys, spread):
        @pl.loop(0, length // rows)
        def _(i):
            part = pl.ds(pl.multiple_of(i * rows, rows), rows)
            turned = turn_heads(dot(x_ref[part, :], w_ref[...]), c_ref[part, :], s_ref[part, :], 1.0).astype(BF16)
            heads[part, :] = turned
            tail = dot(x_ref[part, :], wv_ref[...])
            lanes = lax.broadcasted_iota(jnp.int32, tail.shape, 1)
            value = jnp.where(lanes < HEAD_SIZE, tail, 0.0)
            values[part, :] = value.astype(BF16)
            keys[part, :] = spread_head(turned.astype(F32), 3).astype(BF16)
            both = jnp.concatenate([value, jnp.zeros_like(value)], axis=1)
            spread[part, :] = spread_head(both, 0).astype(BF16)

        for i in range(length // rows):
            first, stop = i * rows, (i + 1) * rows
            allowed = may_attend(starts_ref, first, rows, stop)
            queries = heads[first:stop, :]
            total = jnp.zeros((rows, GROUP), F32)
            for h in range(3):
                probs = probabilities(only_head(queries, h), keys[:stop, :], allowed).astype(BF16)
                total = total + dot(probs, only_head(spread[:stop, :], h))
            low = total.astype(BF16)
            mixed[first:stop, :] = low
            out[first:stop, :] = dot(low[:, : 3 * HEAD_SIZE], o_ref[...]).astype(BF16)

    return pl.pallas_call(
        kernel,
        out_shape=[
            jax.ShapeDtypeStruct((length, width), BF16),
            jax.ShapeDtypeStruct((length, GROUP), BF16),
            jax.ShapeDtypeStruct((length, 128), BF16),
            jax.ShapeDtypeStruct((length, GROUP), BF16),
        ],
        in_specs=[SMEM_SPEC] + [VMEM_SPEC] * 6,
        out_specs=[VMEM_SPEC] * 4,
        scratch_shapes=[pltpu.VMEM((length, GROUP), BF16), pltpu.VMEM((length, GROUP), BF16)],
        compiler_params=pltpu.CompilerParams(vmem_limit_bytes=40 << 20),
        cost_estimate=busy(10),
        name="attend_forward",
    )(starts, normed, *slab, out_rows, cosine, sine)


def attention_backward(normed, slab, out_rows, starts, cosine, sine, heads, values, mixed, branch, rest, share=None):
    length, width = normed.shape
    rows = min(ROWS, length)
    scale = 1.0 / math.sqrt(HEAD_SIZE)
    used = 3 * HEAD_SIZE
    more, more_outs, more_scratch = share_shapes(share)

    def kernel(starts_ref, x_ref, w_ref, wv_ref, o_ref, c_ref, s_ref, h_ref, v_ref, m_ref, b_ref, r_ref, *refs):
        in_ref, refs = refs[: len(more)], refs[len(more) :]
        out, wide, tall, *refs = refs
        sum_ref, refs = refs[: len(more)], refs[len(more) :]
        keys, spread, grads, key_sum, value_sum, low, *refs = refs
        if more:
            barrier(share_devices())
            carried = carrier(share, in_ref[0], sum_ref[0], refs)
            carried.start()

        @pl.loop(0, length // rows)
        def _(i):
            part = pl.ds(pl.multiple_of(i * rows, rows), rows)
            keys[part, :] = spread_head(h_ref[part, :].astype(F32), 3).astype(BF16)
            value = v_ref[part, :].astype(F32)
            both = jnp.concatenate([value, jnp.zeros_like(value)], axis=1)
            spread[part, :] = spread_head(both, 0).astype(BF16)
            grad = dot_t(b_ref[part, :], o_ref[...])
            grads[part, :] = jnp.concatenate(
                [grad, jnp.zeros((rows, HEAD_SIZE), F32)], axis=1
            ).astype(BF16)
            key_sum[part, :] = jnp.zeros((rows, GROUP), F32)
            value_sum[part, :] = jnp.zeros((rows, GROUP), F32)

        if more:
            carried.middle()

        for i in range(length // rows):
            first, stop = i * rows, (i + 1) * rows
            allowed = may_attend(starts_ref, first, rows, stop)
            queries, upstream = h_ref[first:stop, :], grads[first:stop, :]
            query_grad = jnp.zeros((rows, GROUP), F32)
            for h in range(3):
                query_rows, grad_rows = only_head(queries, h), only_head(upstream, h)
                probs = probabilities(query_rows, keys[:stop, :], allowed)
                prob_grad = dot_t(grad_rows, spread[:stop, :])
                centre = jnp.sum(probs * prob_grad, axis=1, keepdims=True)
                score_grad = (probs * (prob_grad - centre)).astype(BF16)
                query_grad = query_grad + dot(score_grad, only_head(keys[:stop, :], h))
                key_sum[:stop, :] += dot(score_grad.T, query_rows)
                value_sum[:stop, :] += dot(probs.astype(BF16).T, grad_rows)
            low[first:stop, :GROUP] = (query_grad * scale).astype(BF16)

        @pl.loop(0, length // rows)
        def _(i):
            part = pl.ds(pl.multiple_of(i * rows, rows), rows)
            keyed = key_sum[part, :]
            keyed = (
                pltpu.roll(keyed, HEAD_SIZE, 1)
                + pltpu.roll(keyed, 2 * HEAD_SIZE, 1)
                + pltpu.roll(keyed, 3 * HEAD_SIZE, 1)
            ) * scale
            lanes = lax.broadcasted_iota(jnp.int32, keyed.shape, 1)
            raw = jnp.where(lanes < used, low[part, :GROUP].astype(F32), keyed)
            raw = raw.astype(BF16).astype(F32)
            low[part, :GROUP] = turn_heads(raw, c_ref[part, :], s_ref[part, :], -1.0).astype(BF16)
            valued = value_sum[part, :]
            valued = (
                valued
                + pltpu.roll(valued, GROUP - HEAD_SIZE, 1)
                + pltpu.roll(valued, GROUP - 2 * HEAD_SIZE, 1)
            )[:, :128]
            lanes = lax.broadcasted_iota(jnp.int32, valued.shape, 1)
            low[part, GROUP:] = jnp.where(lanes < HEAD_SIZE, valued, 0.0).astype(BF16)
            grad = dot_t(low[part, :GROUP], w_ref[...]) + dot_t(low[part, GROUP:], wv_ref[...])
            out[part, :] = grad.astype(BF16)

        step = 256

        @pl.loop(0, width // step)
        def _(i):
            part = pl.ds(pl.multiple_of(i * step, step), step)
            made = dot(x_ref[:, part].T, low[...])
            wide[part, :GROUP] = made[:, :GROUP].astype(BF16)
            lanes = lax.broadcasted_iota(jnp.int32, (step, 128), 1)
            beside = jnp.concatenate([r_ref[part, :], r_ref[part, :]], axis=1)
            wide[part, GROUP:] = jnp.where(
                lanes < HEAD_SIZE, made[:, GROUP:], beside.astype(F32)
            ).astype(BF16)
        tall[...] = dot(m_ref[...].T, b_ref[...])[:used].astype(BF16)
        if more:
            carried.end()

    return pl.pallas_call(
        kernel,
        out_shape=[
            jax.ShapeDtypeStruct((length, width), BF16),
            jax.ShapeDtypeStruct((width, GROUP + 128), BF16),
            jax.ShapeDtypeStruct((used, width), BF16),
        ]
        + more_outs,
        in_specs=[SMEM_SPEC] + [VMEM_SPEC] * 11 + [ANY_SPEC] * len(more),
        out_specs=[VMEM_SPEC] * 3 + [ANY_SPEC] * len(more),
        scratch_shapes=[
            pltpu.VMEM((length, GROUP), BF16),
            pltpu.VMEM((length, GROUP), BF16),
            pltpu.VMEM((length, GROUP), BF16),
            pltpu.VMEM((length, GROUP), F32),
            pltpu.VMEM((length, GROUP), F32),
            pltpu.VMEM((length, GROUP + 128), BF16),
        ]
        + more_scratch,
        compiler_params=comm_params(1, 50)
        if more
        else pltpu.CompilerParams(vmem_limit_bytes=50 << 20),
        cost_estimate=busy(20),
        name="attend_backward",
    )(starts, normed, *slab, out_rows, cosine, sine, heads, values, mixed, branch, rest, *more)


def norm_factor(stream):
    return lax.rsqrt(jnp.mean(stream * stream, axis=-1, keepdims=True) + EPSILON)


def norm_back(stream, factor, gain_row, upstream):
    scaled = gain_row * upstream
    inner_mean = jnp.mean(stream * scaled, axis=-1, keepdims=True)
    return factor * scaled - stream * (factor * factor * factor) * inner_mean


def per_device(
    layer_in,
    cotangent,
    doc_starts,
    routes,
    attn_gain,
    ffn_gain,
    query_weight,
    key_matrix,
    value_matrix,
    out_weight,
    router_weight,
    gate_weight,
    up_weight,
    down_weight,
):
    planes, groups = lax.axis_size("za"), lax.axis_size("grp")
    seq_count = 2 * planes
    place = lax.axis_index("za") * 2 + lax.axis_index("yb")
    count, width = layer_in.shape[1:]
    length = count * seq_count
    layers = attn_gain.shape[0]
    experts_all = router_weight.shape[2]
    local = gate_weight.shape[1]
    top = routes.shape[2]
    slots = -(-(count * top * 4 // (3 * experts_all) + 1) // 16) * 16
    columns = query_weight.shape[2] // 8
    kv = key_matrix.shape[2] // 8
    bands = query_weight.shape[1]

    swap = [(a * 4 + f, f * 4 + a) for a in range(planes) for f in range(4)]

    def exchange(array):
        return lax.ppermute(array, ("za", "xh", "co"), swap)


    small = jnp.stack([attn_gain, ffn_gain], axis=-1)
    used = columns + 2 * kv + experts_all + 2
    padded = -(-used // 128) * 128

    def whole_rows(array):
        if groups == 1:
            return array
        return jnp.moveaxis(lax.all_gather(array, "grp"), 0, 1).reshape(
            layers, groups * bands, array.shape[-1]
        )

    packed = jnp.concatenate(
        [
            jnp.moveaxis(query_weight.reshape(layers, bands, 8, columns), 2, 0),
            jnp.moveaxis(key_matrix.reshape(layers, bands, 8, kv), 2, 0),
            jnp.moveaxis(value_matrix.reshape(layers, bands, 8, kv), 2, 0),
            jnp.broadcast_to(
                jnp.concatenate(
                    [router_weight, small, jnp.zeros((layers, bands, padded - used), BF16)], axis=-1
                )[None],
                (8, layers, bands, padded - columns - 2 * kv),
            ),
        ],
        axis=-1,
    )
    pieces = packed
    if groups > 1:
        pieces = jnp.transpose(lax.all_gather(packed, "grp"), (1, 2, 0, 3, 4)).reshape(
            8, layers, groups * bands, padded
        )
    band_rows = groups * bands

    def in_order(array):
        if groups > 1:
            array = array.reshape(planes, 2, 4, groups, bands, -1)
            array = jnp.swapaxes(array, 2, 3)
        return array.reshape(width, -1)

    all_out = whole_rows(out_weight)
    def carry(array, layer):
        return (array, layer) if groups == 1 and layer < layers else None

    firsts, late_heads, late_others, swapped, carried = enter(
        layer_in[0],
        pieces[..., : padded - 128],
        pieces[..., padded - 128 :],
        all_out[0],
        (cotangent[0], routes[0], doc_starts),
        used - 2 - (padded - 128),
        planes,
        carry(gate_weight, 0),
    )
    normed_first, stream, tall_rows, heads_slab, other_slab = firsts
    stream = stream.astype(F32)
    slabs = [(in_order(heads_slab), in_order(other_slab))]
    upstream_low, chosen, starts = swapped

    def sum_share(term):
        return lax.psum_scatter(term, ("xh", "co"), scatter_dimension=0)

    def sum_experts(gate_term, up_term, down_term):
        axes = ("grp", "xh", "co")
        return (
            lax.psum_scatter(gate_term, axes, scatter_dimension=0),
            lax.psum_scatter(up_term, axes, scatter_dimension=0),
            lax.psum_scatter(down_term, axes, scatter_dimension=0),
        )

    named = jnp.sum(
        (chosen[:, :, None] == jnp.arange(experts_all, dtype=jnp.int32)).astype(F32), axis=1
    )
    ids = jnp.arange(count, dtype=jnp.int32)
    before = (ids[None, :] < ids[:, None]).astype(BF16)
    rank = jnp.dot(before, named.astype(BF16), preferred_element_type=F32)
    codes = jnp.where(named > 0, rank, -1.0)
    codes = jnp.pad(codes, ((0, 0), (0, 128 - experts_all)), constant_values=-1.0).astype(BF16)

    angles = np.arange(length)[:, None] * 10000.0 ** (
        -2.0 * np.arange(HEAD_SIZE // 2)[None, :] / HEAD_SIZE
    )
    cosine = jnp.asarray(np.tile(np.cos(angles), (1, 8)), F32)
    sine = jnp.asarray(np.tile(np.sin(angles), (1, 8)), F32)

    def fetch_experts(layer):
        axes = ("grp", "xh", "co")
        return [
            lax.all_gather(gate_weight[layer], axes, axis=1, tiled=True)[None],
            lax.all_gather(up_weight[layer], axes, axis=1, tiled=True)[None],
            lax.all_gather(down_weight[layer], axes, axis=2, tiled=True)[None],
        ]

    states, arrived = [], []
    out_rows = []
    for layer in range(layers):
        if groups > 1:
            carried = fetch_experts(layer)
        slab = slabs[layer]
        small_part = slab[1][:, columns + 2 * kv - GROUP :]
        attn_row = small_part[:, experts_all].astype(F32)
        ffn_row = small_part[:, experts_all + 1].astype(F32)
        router_w = small_part[:, :experts_all]
        factor_one = norm_factor(stream)
        if layer == 0:
            normed_one = normed_first
        else:
            own_one = (stream * factor_one * attn_row).astype(BF16)
            normed_one, tall_rows = gather_plane(own_one, tall_rows)
        tall_rows = jnp.swapaxes(tall_rows.reshape(4, groups, bands, width), 0, 1)
        out_rows.append(tall_rows.reshape(columns, width))
        normed_one = normed_one.reshape(length, width)
        tall = out_rows[layer]
        branch, heads_low, values, mixed = attention_forward(
            normed_one, slab, tall, starts, cosine, sine
        )
        branch = branch.reshape(8, count, width)
        if layer + 1 < layers:
            share = carry(up_weight, 0) if layer == 0 else None
            branch, *later = scatter_plane_first(
                branch, (late_heads[layer], late_others[layer]), all_out[layer + 1], planes, share
            )
            if share is not None:
                carried, later = [carried[0], later[0]], later[1:]
            tall_rows, *later = later
            slabs.append([in_order(array) for array in later])
        else:
            branch = scatter_plane(branch)
        middle = stream + branch
        factor_two = norm_factor(middle)
        own_two = (middle * factor_two * ffn_row).astype(BF16)
        if layer == 0:
            results = gather_group(own_two, planes, 8, carry(down_weight, 0), codes)
            normed_two, codes = results[0], results[-1]
            if groups == 1:
                carried = [*carried, results[1]]
        else:
            share = carry(down_weight, layer)
            normed_two = gather_group(own_two, planes, 12, share)
            if share is not None:
                normed_two, last = normed_two
                carried = [*carried, last]
        share = count // layers
        gate_w, up_w, down_w = carried
        share = count // layers
        total, gate_part, up_part, gate_probs, probs_t, gathered, *carried = experts_forward(
            normed_two, codes, slab[1], gate_w, up_w, down_w,
            upstream_low[layer * share : (layer + 1) * share], slots, planes,
            11 if layer == 0 else 13, carry(gate_weight, layer + 1),
        )
        arrived.append(gathered)
        own_probs = lax.dynamic_index_in_dim(gate_probs, place, 0, keepdims=False)[:, :experts_all]
        states.append(
            (
                stream, factor_one, normed_one, heads_low, values, mixed, tall, middle,
                factor_two, own_two, normed_two, own_probs, probs_t, gate_part, up_part, total,
                gate_w, up_w, down_w, attn_row, ffn_row, slab, router_w,
            )
        )
        if layer + 1 < layers:
            share = carry(up_weight, layer + 1)
            added = scatter_group(total, planes, 14, () if share is None else (share,))
            if share is not None:
                added, last = added
                carried = [*carried, last]
            stream = middle + added

    result, pending = None, None
    upstream = upstream_low.astype(F32)
    expert_out = [None] * layers
    wide_terms, tall_terms = [None] * layers, [None] * layers
    for layer in reversed(range(layers)):
        (
            stream, factor_one, normed_one, heads_low, values, mixed, tall, middle,
            factor_two, own_two, normed_two, own_probs, probs_t, gate_part, up_part, total,
            gate_w, up_w, down_w, attn_row, ffn_row, slab, router_w,
        ) = states[layer]
        if layer + 1 < layers:
            sending = upstream.astype(BF16)
            arrived = gather_group(sending, planes, 0, pending)
            if pending is not None:
                arrived, up_sum = arrived
                expert_out[layer + 1] = (expert_out[layer + 1][0], up_sum, expert_out[layer + 1][2])
            arrived = [arrived]
        outermost = layer + 1 == layers
        row_sums, gate_term, up_term, down_term, *added = experts_backward(
            normed_two, arrived, codes, probs_t, gate_w, up_w, down_w, gate_part, up_part,
            slots, 4 * groups, total if outermost else None, planes, None, result,
        )
        result = (middle + added[0]).astype(BF16) if outermost else added[0]
        if groups > 1:
            summed = scatter_group(row_sums, planes, 2)
            expert_out[layer] = sum_experts(gate_term, up_term, down_term)
            beside = None
        else:
            summed, down_sum = scatter_group(row_sums, planes, 2, ((down_term, None),))
            pending, beside = (up_term, None), (gate_term, None)
        weighted = summed[:, width : width + experts_all]
        weighted = weighted + summed[:, width + 64 : width + 64 + experts_all]
        logit_grad = weighted - own_probs * jnp.sum(weighted, axis=-1, keepdims=True)
        router_term = jnp.einsum("td,te->de", own_two.astype(F32), logit_grad, precision=HIGHEST)
        normed_two_grad = summed[:, :width] + jnp.einsum(
            "te,de->td", logit_grad, router_w.astype(F32), precision=HIGHEST
        )
        ffn_gain_term = jnp.sum(normed_two_grad * middle * factor_two, axis=0)
        middle_grad = upstream + norm_back(middle, factor_two, ffn_row, normed_two_grad)
        branch_low = gather_plane(middle_grad.astype(BF16)).reshape(length, width)
        rest = jnp.concatenate([router_term, ffn_gain_term[:, None]], axis=1)
        rest = jnp.pad(rest, ((0, 0), (0, 32 - experts_all - 1)))
        high = rest.astype(BF16)
        low_part = (rest - high.astype(F32)).astype(BF16)
        partial, qkv_term, out_term, *sums = attention_backward(
            normed_one, slab, tall, starts, cosine, sine, heads_low, values, mixed, branch_low,
            jnp.concatenate([high, low_part], axis=1), beside,
        )
        if beside is not None:
            expert_out[layer] = (sums[0], None, down_sum)
        partial = partial.reshape(8, count, width)
        normed_one_grad = scatter_plane(partial)
        upstream = middle_grad + norm_back(stream, factor_one, attn_row, normed_one_grad)
        if groups > 1:
            qkv_term = jnp.swapaxes(
                qkv_term.reshape(planes, 2, groups, 4, bands, padded), 2, 3
            )
            out_term = jnp.swapaxes(out_term.reshape(groups, 4, bands, width), 0, 1)
        wide_terms[layer] = qkv_term.reshape(planes, 8, band_rows, padded)
        tall_terms[layer] = out_term.reshape(4, band_rows, width)

    if groups > 1:
        sums = collect(wide_terms, tall_terms, planes)
        input_grad = exchange(upstream.astype(BF16))
    else:
        query_out, key_out, value_out, tall_out, rest, input_grad, up_sum = collect(
            wide_terms, tall_terms, planes, (pending,),
            (query_weight, key_matrix, value_matrix), upstream.astype(BF16),
        )
        expert_out[0] = (expert_out[0][0], up_sum, expert_out[0][2])
        products = rest[..., 32]
    if groups > 1:
        sums = [
            lax.psum_scatter(array, "grp", scatter_dimension=array.ndim - 2, tiled=True)
            for array in sums
        ]
        wide_sums = jnp.stack(sums[:layers]).astype(F32)

        def by_heads(start, stop):
            return jnp.swapaxes(wide_sums[..., start:stop], 1, 2).reshape(layers, bands, -1)

        query_out = by_heads(0, columns)
        key_out = by_heads(columns, columns + kv)
        value_out = by_heads(columns + kv, columns + 2 * kv)
        tall_out = jnp.stack(sums[layers:]).astype(F32)
        rest = jnp.sum(wide_sums[..., columns + 2 * kv :], axis=1)
        rest = rest[..., :32] + rest[..., 32:64]
        products = (
            jnp.sum(query_weight.astype(F32) * query_out, axis=-1)
            + jnp.sum(key_matrix.astype(F32) * key_out, axis=-1)
            + jnp.sum(value_matrix.astype(F32) * value_out, axis=-1)
        )
    attn_out = products / attn_gain.astype(F32)

    def stacked(lists, i):
        return jnp.stack([lists[layer][i] for layer in range(layers)]).astype(F32)

    return (
        result[None],
        input_grad.astype(F32)[None],
        attn_out,
        rest[..., experts_all],
        query_out,
        key_out,
        value_out,
        tall_out,
        rest[..., :experts_all],
        stacked(expert_out, 0),
        stacked(expert_out, 1),
        stacked(expert_out, 2),
    )


def solution(mesh):
    seq, fsdp = mesh.shape["seq"], mesh.shape["fsdp"]
    split = Mesh(mesh.devices.reshape(seq // 2, 2, fsdp // 4, 2, 2), AX)
    s, f = ("za", "yb"), ("grp", "xh", "co")
    token = P(f, s, None)
    dense = P(None, s + f, None)
    gain = P(None, s + f)
    wide, tall = P(None, s, f, None), P(None, s, None, f)
    return jax.shard_map(
        per_device,
        mesh=split,
        in_specs=(token, token, P(f, None), token, gain, gain, dense, dense, dense, dense, dense, wide, wide, tall),
        out_specs=(token, token, gain, gain, dense, dense, dense, dense, dense, wide, wide, tall),
        check_vma=False,
    )
```
